32 devices in a mesh: chol: 16 (over z, y, x), walker: 1, orb: 2 (over core).
Axes of the slice: x: 2, y: 2, z: 4, core: 2. Of those that a mesh axis runs over, the one named last changes fastest.
Arguments:
- chol_vals: bfloat16 [4096, 4, 64, 128], P('chol', 'orb'), may hold values from -0.05 to 0.05, as said below
- chol_cols: int32 [4096, 4, 2], P('chol', 'orb'), may hold values from 0 to 4, as said below
- greens: bfloat16 [32, 256, 256], P('walker', 'orb'), may hold values from -0.75 to 0.75
- walkers: bfloat16 [32, 256, 128], P('walker', 'orb'), may hold values from -6 to 6
- fields: float32 [4096, 32], P('chol', 'walker'), may hold values from -6 to 6
Outputs:
- new_walkers: bfloat16 [32, 256, 128], P('walker', 'orb')
- energy: float32 [32], P('walker')
The draws below stay inside these ranges and needn't reach their ends.
Inputs may be any that keep to these rules, and one draw needn't show every extreme that they name: `chol_cols`: for every vector g and block row r, slot 0 holds r; the other slots hold distinct block columns different from r, or 4 for an empty slot. `chol_vals`: values of the stored blocks; entries in empty slots are not used.
All inputs are finite; a program needn't handle non-finite values.
Results may differ from the reference program's by a relative error of at most 0.0055.
Values may be sent and summed in bfloat16 or wider, within the bound.
No kernel may reach another device: no remote copies, remote signals or barrier semaphores. Data moves between devices by JAX's collectives and lax.ppermute only.
A program may use at most 128 MiB of HBM per device.

```python
import jax
import jax.numpy as jnp
from jax import lax

NORB = 256
NOCC = 128
BLOCK = 64
SLOTS = 2
TAYLOR = 4
VEC_DEV = 256
ROWBLK = 4
NVEC = 4096
WALKERS = 32


def draw_chol_vals(key, part):
    array_shape = (NVEC, ROWBLK, BLOCK, SLOTS * BLOCK)
    vector_index = jnp.arange(NVEC, dtype=jnp.float32)
    decay_scale = 0.0075 * jnp.exp(-1.4 * vector_index / NVEC)
    base_draw = jnp.clip(jax.random.normal(key, array_shape, jnp.float32), -6.0, 6.0)
    return (base_draw * decay_scale[:, None, None, None]).astype(jnp.bfloat16)


def draw_chol_cols(key, part):
    first_key = jax.random.fold_in(key, 11)
    second_key = jax.random.fold_in(key, 23)
    scores = jax.random.randint(first_key, (NVEC, ROWBLK, ROWBLK), 0, 1 << 20) * ROWBLK
    scores = scores + jnp.arange(ROWBLK, dtype=jnp.int32)
    diagonal_mask = jnp.arange(ROWBLK)[:, None] == jnp.arange(ROWBLK)[None, :]
    scores = jnp.where(diagonal_mask[None], -1, scores)
    ranked = jnp.argsort(scores, axis=-1)[..., :SLOTS].astype(jnp.int32)
    empty_slot = jax.random.randint(second_key, (NVEC, ROWBLK, SLOTS), 0, 3) == 0
    slot_zero = jnp.arange(SLOTS)[None, None, :] == 0
    return jnp.where(empty_slot & jnp.logical_not(slot_zero), ROWBLK, ranked).astype(jnp.int32)


def block_scale(key, dims, cuts, smallest, top_value):
    factor_of, own = 1.0, jax.random.fold_in(key, 6)
    for axis_at, parts in cuts:
        draws = jnp.exp(jax.random.uniform(jax.random.fold_in(own, axis_at), (parts,), jnp.float32, smallest / len(cuts), top_value / len(cuts)))
        factor_of = factor_of * jnp.repeat(draws, dims[axis_at] // parts).reshape([-1 if axis == axis_at else 1 for axis in range(len(dims))])
    return factor_of


def noise(rng, dims, deviation, limit, split=(), kind=jnp.bfloat16):
    array = deviation * jax.random.normal(rng, dims, jnp.float32)
    if split:
        array = array * block_scale(rng, dims, split, -0.22, 0.18)
    return jnp.clip(array, -limit, limit).astype(kind)


def setup_inputs(seed: int = 0) -> dict:
    streams_of = jax.random.split(jax.random.key(seed), 6)
    chol_vals = draw_chol_vals(jax.random.fold_in(streams_of[5], 71), 0)
    chol_cols = draw_chol_cols(jax.random.fold_in(streams_of[5], 71), 0)
    greens = noise(streams_of[2], (WALKERS, NORB, NORB), 0.125, 0.75, ((1, 2),))
    walkers = noise(streams_of[3], (WALKERS, NORB, NOCC), 1.0, 6.0, ((1, 2),))
    fields = noise(streams_of[4], (NVEC, WALKERS), 1.0, 6.0, ((0, 16),), jnp.float32)
    return dict(chol_vals=chol_vals, chol_cols=chol_cols, greens=greens, walkers=walkers, fields=fields)


def dense_rows(values, columns):
    vectors = values.shape[0]
    pieces = values.astype(jnp.float32).reshape(vectors, ROWBLK, BLOCK, SLOTS, BLOCK)
    onehot = (columns[..., None] == jnp.arange(ROWBLK, dtype=jnp.int32)).astype(jnp.float32)
    placed = jnp.einsum('grsc,grisj->gricj', onehot, pieces, precision=lax.Precision.HIGHEST)
    return placed.reshape(vectors, NORB * NORB)


def reference(chol_vals, chol_cols, greens, walkers, fields):
    groups = NVEC // VEC_DEV
    value_groups = chol_vals.reshape(groups, VEC_DEV, ROWBLK, BLOCK, SLOTS * BLOCK)
    column_groups = chol_cols.reshape(groups, VEC_DEV, ROWBLK, SLOTS)
    green_flat = greens.astype(jnp.float32).reshape(WALKERS, NORB * NORB)

    def bias_group(pair):
        matrix = dense_rows(pair[0], pair[1])
        return jnp.dot(matrix, green_flat.T, precision=lax.Precision.HIGHEST)

    force_bias = lax.map(bias_group, (value_groups, column_groups)).reshape(NVEC, WALKERS)
    energy = 0.5 * jnp.sum(force_bias * force_bias, axis=0)
    shifted = lax.optimization_barrier((fields - force_bias).astype(jnp.bfloat16))
    shift_groups = shifted.astype(jnp.float32).reshape(groups, VEC_DEV, WALKERS)

    def add_group(total, triple):
        matrix = dense_rows(triple[0], triple[1])
        return total + jnp.dot(triple[2].T, matrix, precision=lax.Precision.HIGHEST), None

    total, unused = lax.scan(add_group, jnp.zeros((WALKERS, NORB * NORB), jnp.float32),
                             (value_groups, column_groups, shift_groups))
    step_factor = 72.0 / float(NVEC * BLOCK) ** 0.5
    potential = lax.optimization_barrier((step_factor * total).reshape(WALKERS, NORB, NORB).astype(jnp.bfloat16))
    potential = potential.astype(jnp.float32)
    series_term = walkers
    series_sum = jnp.zeros((WALKERS, NORB, NOCC), jnp.float32)
    for degree in range(1, TAYLOR + 1):
        product = jnp.einsum('wij,wja->wia', potential, series_term.astype(jnp.float32),
                             precision=lax.Precision.HIGHEST)
        series_term = lax.optimization_barrier((product / degree).astype(jnp.bfloat16))
        series_sum = series_sum + series_term.astype(jnp.float32)
    new_walkers = (walkers.astype(jnp.float32) + series_sum).astype(jnp.bfloat16)
    return new_walkers, energy
```

```python
import functools

import jax
import jax.numpy as jnp
from jax import lax
from jax.experimental import pallas as pl
from jax.experimental.pallas import tpu as pltpu
from jax.sharding import PartitionSpec as P

BLOCK = 64
TAYLOR = 4
ROWBLK = 4
LANES = 2 * BLOCK
CHUNK = 16
VMEM_LIMIT = 56 * 1024 * 1024


def params():
    return pltpu.CompilerParams(vmem_limit_bytes=VMEM_LIMIT)


def column_order(row):
    other = 2 - 2 * (row // 2)
    return row, row + 1 - 2 * (row % 2), other, other + 1


def slot_masks(cols, row):
    return [cols == column for column in column_order(row)[1:]]


def bias_kernel(steps, vals_ref, greens_ref, cols_ref, turned_ref, bias_ref, v32, gx, gy, gyr, gs, acc):
    t = pl.program_id(0)
    local = t // steps
    row = lax.axis_index("orb") * cols_ref.shape[0] + local
    vectors = vals_ref.shape[0]
    walk = greens_ref.shape[0]

    v32[...] = vals_ref[:, 0].astype(jnp.float32).reshape(vectors * CHUNK, LANES)
    for i in range(CHUNK):
        turned_ref[:, i * LANES:(i + 1) * LANES] = v32[pl.ds(i, vectors, stride=CHUNK), :].astype(jnp.bfloat16)

    green = greens_ref[...].astype(jnp.float32)
    left = green[:, :, :LANES].reshape(walk * CHUNK, LANES)
    right = green[:, :, LANES:].reshape(walk * CHUNK, LANES)
    upper = row // 2 == 1
    pair = jnp.where(upper, right, left)
    rest = jnp.where(upper, left, right)
    gx[...] = jnp.where(row % 2 == 1, pltpu.roll(pair, BLOCK, 1), pair)
    gy[...] = rest
    gyr[...] = pltpu.roll(rest, BLOCK, 1)
    first = lax.broadcasted_iota(jnp.int32, (walk, LANES), 1) < BLOCK
    for i in range(CHUNK):
        cut = slice(i * LANES, (i + 1) * LANES)
        rows = pl.ds(i, walk, stride=CHUNK)
        x = gx[rows, :]
        gs[0:walk, cut] = jnp.where(first, x, 0.0).astype(jnp.bfloat16)
        gs[walk:2 * walk, cut] = jnp.where(first, 0.0, x).astype(jnp.bfloat16)
        gs[2 * walk:3 * walk, cut] = jnp.where(first, 0.0, gyr[rows, :]).astype(jnp.bfloat16)
        gs[3 * walk:4 * walk, cut] = jnp.where(first, 0.0, gy[rows, :]).astype(jnp.bfloat16)

    part = lax.dot_general(
        gs[...], turned_ref[...], (((1,), (1,)), ((), ())), preferred_element_type=jnp.float32
    )

    @pl.when(t % steps == 0)
    def _():
        acc[...] = part

    @pl.when(t % steps != 0)
    def _():
        acc[...] += part

    @pl.when(t == 0)
    def _():
        bias_ref[...] = jnp.zeros_like(bias_ref)

    @pl.when(t % steps == steps - 1)
    def _():
        total = acc[0:walk]
        cols = cols_ref[pl.ds(local, 1), 1, :]
        for k, mask in enumerate(slot_masks(cols, row)):
            total = total + jnp.where(mask, acc[(k + 1) * walk:(k + 2) * walk], 0.0)
        bias_ref[...] += total


def bias_call(vals, greens, cols):
    vectors, rowblocks = vals.shape[:2]
    walk, half_rows, norb = greens.shape
    steps = BLOCK // CHUNK
    wide = CHUNK * LANES
    grid = (rowblocks * steps,)
    return pl.pallas_call(
        functools.partial(bias_kernel, steps),
        grid=grid,
        in_specs=[
            pl.BlockSpec((vectors, 1, CHUNK, LANES), lambda t: (0, t // steps, t % steps, 0)),
            pl.BlockSpec((walk, CHUNK, norb), lambda t: (0, t, 0)),
            pl.BlockSpec(cols.shape, lambda t: (0, 0, 0)),
        ],
        out_specs=[
            pl.BlockSpec((vectors, wide), lambda t: (0, t)),
            pl.BlockSpec((walk, vectors), lambda t: (0, 0)),
        ],
        out_shape=[
            jax.ShapeDtypeStruct((vectors, rowblocks * BLOCK * LANES), jnp.bfloat16),
            jax.ShapeDtypeStruct((walk, vectors), jnp.float32),
        ],
        scratch_shapes=[
            pltpu.VMEM((vectors * CHUNK, LANES), jnp.float32),
            pltpu.VMEM((walk * CHUNK, LANES), jnp.float32),
            pltpu.VMEM((walk * CHUNK, LANES), jnp.float32),
            pltpu.VMEM((walk * CHUNK, LANES), jnp.float32),
            pltpu.VMEM((4 * walk, wide), jnp.bfloat16),
            pltpu.VMEM((4 * walk, vectors), jnp.float32),
        ],
        compiler_params=params(),
        name="force_bias",
    )(vals, greens, cols)


def potential_kernel(start, steps, layout, by_plane, fields_ref, own_ref, *refs):
    nz, plane, own = layout
    others = refs[:lax.axis_size("orb") - 1]
    cols_ref, turned_ref = refs[len(others):len(others) + 2]
    groups = plane if by_plane else nz
    outs = refs[len(others) + 2:len(others) + 2 + groups]
    energy_ref, s_ref, scratch = refs[len(others) + 2 + groups:]
    t = pl.program_id(0)
    walk, vectors = fields_ref.shape
    rowblocks = cols_ref.shape[0]

    @pl.when(t == 0)
    def _():
        me = lax.axis_index("chol")
        bias = own_ref[...]
        for other in others:
            bias = bias + other[...]
        energy = 0.5 * jnp.sum(bias * bias, axis=1, keepdims=True)
        energy_ref[...] = jnp.broadcast_to(energy, energy_ref.shape)
        shifted = (fields_ref[...] - bias).astype(jnp.bfloat16)
        at = lax.broadcasted_iota(jnp.int32, (walk, walk), 0)
        source = lax.broadcasted_iota(jnp.int32, (walk, walk), 1)
        chip = at // own
        z = (me // plane + chip // plane) % nz
        p = (me % plane) ^ (chip % plane)
        wanted = (z * plane + p) * own + at % own
        pick = (wanted == source).astype(jnp.float32).astype(jnp.bfloat16)
        ordered = jnp.dot(pick, shifted, preferred_element_type=jnp.float32)
        for local in range(rowblocks):
            row = lax.axis_index("orb") * rowblocks + local
            s_ref[local, 0:walk] = ordered.astype(jnp.bfloat16)
            for k, mask in enumerate(slot_masks(cols_ref[local, 1:2, :], row)):
                s_ref[local, (k + 1) * walk:(k + 2) * walk] = jnp.where(mask, ordered, 0.0).astype(jnp.bfloat16)

    left = s_ref[(start + t) // (BLOCK // CHUNK)]
    first = lax.broadcasted_iota(jnp.int32, (walk, LANES), 1) < BLOCK
    for i in range(0, CHUNK, 2):
        both = jnp.dot(left, turned_ref[:, i * LANES:(i + 2) * LANES], preferred_element_type=jnp.float32)
        for side in range(2):
            out = both[:, side * LANES:(side + 1) * LANES]
            near = jnp.where(first, out[0:walk], out[walk:2 * walk])
            far = jnp.where(first, pltpu.roll(out[2 * walk:3 * walk], BLOCK, 1), out[3 * walk:])
            scratch[(i + side) * walk:(i + side + 1) * walk, :] = near
            scratch[(CHUNK + i + side) * walk:(CHUNK + i + side + 1) * walk, :] = far
    for w in range(walk):
        chip, j = w // own, w % own
        group, inner = (chip % plane, chip // plane) if by_plane else (chip // plane, chip % plane)
        for half in range(2):
            tile = scratch[pl.ds(half * CHUNK * walk + w, CHUNK, stride=walk), :]
            outs[group][inner, j, half * CHUNK:(half + 1) * CHUNK, :] = tile.astype(jnp.bfloat16)


def potential_call(start, steps, layout, by_plane, fields, bias, others, cols, turned):
    nz, plane, own = layout
    walk, vectors = fields.shape
    groups, inner = (plane, nz) if by_plane else (nz, plane)
    whole = lambda a: pl.BlockSpec(a.shape, lambda t: (0,) * a.ndim)
    small = [fields, bias, *others, cols]
    rows = 2 * CHUNK
    energy = jax.ShapeDtypeStruct((walk, LANES), jnp.float32)
    *parts, energy = pl.pallas_call(
        functools.partial(potential_kernel, start, steps, layout, by_plane),
        grid=(steps,),
        in_specs=[
            *map(whole, small),
            pl.BlockSpec((vectors, CHUNK * LANES), lambda t: (0, start + t)),
        ],
        out_specs=[
            *[pl.BlockSpec((inner, own, rows, LANES), lambda t: (0, 0, t, 0))] * groups,
            whole(energy),
        ],
        out_shape=[
            *[jax.ShapeDtypeStruct((inner, own, steps * rows, LANES), jnp.bfloat16)] * groups,
            energy,
        ],
        scratch_shapes=[
            pltpu.VMEM((cols.shape[0], 4 * walk, vectors), jnp.bfloat16),
            pltpu.VMEM((2 * CHUNK * walk, LANES), jnp.float32),
        ],
        compiler_params=params(),
        name="potential",
    )(*small, turned)
    return parts, energy


def sum_kernel(count, *refs):
    ins, outs = refs[:count], refs[count:]
    for k, out in enumerate(outs):
        total = ins[0][k].astype(jnp.float32)
        for ref in ins[1:]:
            total = total + ref[k].astype(jnp.float32)
        out[...] = total.astype(out.dtype)


def sum_call(arrays):
    pieces = arrays[0].shape[0]
    shape = jax.ShapeDtypeStruct(arrays[0].shape[1:], jnp.bfloat16)
    return pl.pallas_call(
        functools.partial(sum_kernel, len(arrays)),
        out_shape=[shape] * pieces,
        compiler_params=params(),
        name="sum_parts",
    )(*arrays)


def series_kernel(sizes, *refs):
    n_orb, late_steps, early_steps = sizes
    late, early, start = refs[:n_orb], refs[n_orb:2 * n_orb], refs[2 * n_orb:3 * n_orb]
    plane_ref, z_ref, pot, term, total = refs[3 * n_orb:]
    me = lax.axis_index("orb")
    own, half_rows = start[0].shape[:2]
    rowblocks = half_rows // BLOCK
    per = BLOCK // CHUNK
    for d in range(n_orb):
        at = lax.rem(me + d, n_orb)
        term[pl.ds(at, 1)] = start[d][...][None]
        for t in range(rowblocks * per):
            ref, k = (early[d], t) if t < early_steps else (late[d], t - early_steps)
            for half in range(2):
                rows = slice((2 * k + half) * CHUNK, (2 * k + half + 1) * CHUNK)
                pot[pl.ds(at * rowblocks + t // per, 1), :, (t % per) * CHUNK:(t % per + 1) * CHUNK,
                    half * LANES:(half + 1) * LANES] = ref[:, rows, :][None]
    for j in range(own):
        blocks = [term[r // rowblocks, j, (r % rowblocks) * BLOCK:(r % rowblocks + 1) * BLOCK] for r in range(ROWBLK)]
        sums = [jnp.zeros(blocks[0].shape, jnp.float32)] * ROWBLK
        begin = blocks
        for degree in range(1, TAYLOR + 1):
            after = []
            for r in range(ROWBLK):
                right = jnp.concatenate([blocks[c] for c in column_order(r)], axis=0)
                product = jnp.dot(pot[r, j], right, preferred_element_type=jnp.float32)
                after.append((product / degree).astype(jnp.bfloat16))
            blocks = after
            sums = [s + b.astype(jnp.float32) for s, b in zip(sums, blocks)]
        for r in range(ROWBLK):
            moved = begin[r].astype(jnp.float32) + sums[r]
            total[r // rowblocks, j, (r % rowblocks) * BLOCK:(r % rowblocks + 1) * BLOCK] = moved.astype(jnp.bfloat16)
    mine = total[pl.ds(me, 1)][0]
    cut = z_ref.shape[1]
    z_ref[...] = mine[:, :cut]
    plane_ref[...] = mine[:, cut:]


def series_call(sizes, cut, late, early, start):
    n_orb = sizes[0]
    own, half_rows, nocc = start[0].shape
    return pl.pallas_call(
        functools.partial(series_kernel, sizes),
        out_shape=[
            jax.ShapeDtypeStruct((own, half_rows - cut, nocc), jnp.bfloat16),
            jax.ShapeDtypeStruct((own, cut, nocc), jnp.bfloat16),
        ],
        scratch_shapes=[
            pltpu.VMEM((ROWBLK, own, BLOCK, 2 * LANES), jnp.bfloat16),
            pltpu.VMEM((n_orb, own, half_rows, nocc), jnp.bfloat16),
            pltpu.VMEM((n_orb, own, half_rows, nocc), jnp.bfloat16),
        ],
        compiler_params=params(),
        name="series",
    )(*late, *early, *start)


def place_kernel(layout, *refs):
    nz, plane, own = layout
    z_first, plane_first = refs[:plane], refs[plane:plane + nz]
    out, sems = refs[plane + nz:]
    me = lax.axis_index("chol")
    cut = z_first[0].shape[2]
    copies = []
    for dp in range(plane):
        for dz in range(nz):
            chip = lax.rem(me // plane + nz - dz, nz) * plane + (lax.rem(me, plane) ^ dp)
            to = pl.ds(chip * own, own)
            n = 2 * (dp * nz + dz)
            copies.append(pltpu.make_async_copy(z_first[dp].at[dz], out.at[to, :cut], sems.at[n]))
            copies.append(pltpu.make_async_copy(plane_first[dz].at[dp], out.at[to, cut:], sems.at[n + 1]))
    for copy in copies:
        copy.start()
    for copy in copies:
        copy.wait()


def place_call(layout, z_first, plane_first):
    nz, plane, own = layout
    cut, rest, nocc = z_first[0].shape[2], plane_first[0].shape[2], z_first[0].shape[3]
    return pl.pallas_call(
        functools.partial(place_kernel, layout),
        in_specs=[pl.BlockSpec(memory_space=pl.ANY)] * (nz + plane),
        out_specs=pl.BlockSpec(memory_space=pl.ANY),
        out_shape=jax.ShapeDtypeStruct((nz * plane * own, cut + rest, nocc), jnp.bfloat16),
        scratch_shapes=[pltpu.SemaphoreType.DMA((2 * nz * plane,))],
        compiler_params=params(),
        name="place_walkers",
    )(*z_first, *plane_first)


def per_device(chol_vals, chol_cols, greens, walkers, fields):
    vectors, rowblocks = chol_vals.shape[:2]
    walk, half_rows = greens.shape[:2]
    chips = lax.axis_size("chol")
    n_orb = lax.axis_size("orb")
    plane = 4 if chips % 4 == 0 else 1
    nz = chips // plane
    own = walk // chips
    layout = (nz, plane, own)
    step_factor = 72.0 / float(vectors * chips * BLOCK) ** 0.5
    me = lax.axis_index("chol")

    def to_plane(a, dp):
        return lax.ppermute(a, "chol", [(c, (c // plane) * plane + ((c % plane) ^ dp)) for c in range(chips)])

    def to_z(a, dz):
        return lax.ppermute(a, "chol", [(c, ((c // plane + dz) % nz) * plane + c % plane) for c in range(chips)])

    def around_orb(a):
        return [a] + [lax.ppermute(a, "orb", [((c + d) % n_orb, c) for c in range(n_orb)]) for d in range(1, n_orb)]

    cols = jnp.transpose(chol_cols, (1, 2, 0))
    mine = lax.dynamic_slice_in_dim(walkers, me * own, own, 0)
    start = around_orb(mine)

    turned, partial_bias = bias_call(chol_vals, greens, cols)
    bias, *others = around_orb(partial_bias)

    total_steps = rowblocks * BLOCK // CHUNK
    early_steps = total_steps * 3 // 8
    late_steps = total_steps - early_steps
    fields_t = fields.T
    early, energy = potential_call(0, early_steps, layout, False, fields_t, bias, others, cols, turned)
    early_in = [early[0]] + [to_z(early[dz], dz) for dz in range(1, nz)]
    late, _ = potential_call(early_steps, late_steps, layout, True, fields_t, bias, others, cols, turned)
    late_in = [late[0]] + [to_plane(late[dp], dp) for dp in range(1, plane)]
    early_sums = sum_call(early_in)
    early_in = [early_sums[0]] + [to_plane(early_sums[dp], dp) for dp in range(1, plane)]
    late_sums = sum_call(late_in)
    late_in = [late_sums[0]] + [to_z(late_sums[dz], dz) for dz in range(1, nz)]

    energy = energy[:, 0]
    energy = energy + sum(to_plane(energy, dp) for dp in range(1, plane))
    energy = energy + sum(to_z(energy, dz) for dz in range(1, nz))

    def finish(arrays):
        total = arrays[0].astype(jnp.float32)
        for a in arrays[1:]:
            total = total + a.astype(jnp.float32)
        return around_orb((step_factor * total).astype(jnp.bfloat16))

    cut = half_rows // CHUNK * 5 // 8 * CHUNK
    b_part, a_part = series_call((n_orb, late_steps, early_steps), cut, finish(late_in), finish(early_in), start)

    a_all = jnp.stack([a_part] + [to_z(a_part, dz) for dz in range(1, nz)])
    b_all = jnp.stack([b_part] + [to_plane(b_part, dp) for dp in range(1, plane)])
    z_first = [a_all] + [to_plane(a_all, dp) for dp in range(1, plane)]
    plane_first = [b_all] + [to_z(b_all, dz) for dz in range(1, nz)]
    return place_call(layout, z_first, plane_first), energy


def solution(mesh):
    in_specs = (
        P("chol", "orb", None, None),
        P("chol", "orb", None),
        P("walker", "orb", None),
        P("walker", "orb", None),
        P("chol", "walker"),
    )
    out_specs = (P("walker", "orb", None), P("walker"))
    return jax.shard_map(
        per_device, mesh=mesh, in_specs=in_specs, out_specs=out_specs, check_vma=False
    )
```

```python
import functools

import jax
import jax.numpy as jnp
from jax import lax
from jax.experimental import pallas as pl
from jax.experimental.pallas import tpu as pltpu
from jax.sharding import PartitionSpec as P

BLOCK = 64
TAYLOR = 4
ROWBLK = 4
LANES = 2 * BLOCK
CHUNK = 16
MIB = 1024 * 1024


def params(mib):
    return pltpu.CompilerParams(vmem_limit_bytes=mib * MIB)


def in_vmem(*arrays):
    return [pltpu.with_memory_space_constraint(a, pltpu.VMEM) for a in arrays]


def swap_matrix():
    to = lax.broadcasted_iota(jnp.int32, (CHUNK * CHUNK, CHUNK * CHUNK), 0)
    at = lax.broadcasted_iota(jnp.int32, (CHUNK * CHUNK, CHUNK * CHUNK), 1)
    same = (to // CHUNK == at % CHUNK) & (to % CHUNK == at // CHUNK)
    return same.astype(jnp.float32).astype(jnp.bfloat16)


def column_order(row):
    other = 2 - 2 * (row // 2)
    return row, row + 1 - 2 * (row % 2), other, other + 1


def slot_masks(cols, row):
    return [cols == column for column in column_order(row)[1:]]


def bias_kernel(vals_hbm, greens_hbm, cols_ref, turned_ref, bias_ref, vals, greens, swap, gs, acc, vsem, gsem):
    total_steps, vectors = turned_ref.shape[:2]
    walk = bias_ref.shape[0]
    steps = BLOCK // CHUNK

    def copies(t):
        rows = pl.ds(lax.rem(t, steps) * CHUNK, CHUNK)
        return (
            pltpu.make_async_copy(vals_hbm.at[:, lax.div(t, steps), rows, :], vals.at[t], vsem.at[t]),
            pltpu.make_async_copy(greens_hbm.at[:, pl.ds(t * CHUNK, CHUNK), :], greens.at[t], gsem.at[t]),
        )

    def begin(t, carry):
        for copy in copies(t):
            copy.start()
        return carry

    lax.fori_loop(0, total_steps, begin, 0)
    swap[...] = swap_matrix()
    bias_ref[...] = jnp.zeros_like(bias_ref)
    first = lax.broadcasted_iota(jnp.int32, (CHUNK * CHUNK, LANES), 1) < BLOCK

    def step(t, carry):
        for copy in copies(t):
            copy.wait()
        local = lax.div(t, steps)
        row = lax.axis_index("orb") * cols_ref.shape[0] + local
        upper = row // 2 == 1
        odd = row % 2 == 1
        for w in range(0, walk, CHUNK):
            mixed = greens[t, w:w + CHUNK].reshape(CHUNK * CHUNK, 2 * LANES)
            mixed = jnp.dot(swap[...], mixed, preferred_element_type=jnp.float32)
            pair = jnp.where(upper, mixed[:, LANES:], mixed[:, :LANES])
            rest = jnp.where(upper, mixed[:, :LANES], mixed[:, LANES:])
            pair = jnp.where(odd, pltpu.roll(pair, BLOCK, 1), pair)
            pieces = (
                jnp.where(first, pair, 0.0),
                jnp.where(first, 0.0, pair),
                jnp.where(first, 0.0, pltpu.roll(rest, BLOCK, 1)),
                jnp.where(first, 0.0, rest),
            )
            for k, piece in enumerate(pieces):
                piece = piece.astype(jnp.bfloat16)
                for i in range(CHUNK):
                    gs[k * walk + w:k * walk + w + CHUNK, i * LANES:(i + 1) * LANES] = piece[i * CHUNK:(i + 1) * CHUNK]
        for g in range(0, vectors, 2 * CHUNK):
            both = [vals[t, g + side * CHUNK:g + (side + 1) * CHUNK].reshape(CHUNK * CHUNK, LANES) for side in range(2)]
            both = jnp.dot(swap[...], jnp.concatenate(both, axis=1), preferred_element_type=jnp.float32)
            both = both.astype(jnp.bfloat16)
            for i in range(CHUNK):
                for side in range(2):
                    turned_ref[t, g + side * CHUNK:g + (side + 1) * CHUNK, i * LANES:(i + 1) * LANES] = (
                        both[i * CHUNK:(i + 1) * CHUNK, side * LANES:(side + 1) * LANES]
                    )
        part = lax.dot_general(
            turned_ref[t], gs[...], (((1,), (1,)), ((), ())), preferred_element_type=jnp.float32
        )
        begins = lax.rem(t, steps) == 0
        acc[...] = jnp.where(begins, 0.0, acc[...]) + part

        @pl.when(lax.rem(t, steps) == steps - 1)
        def _():
            flat = acc[...].T
            total = flat[0:walk]
            cols = cols_ref[local, 1:2, :]
            for k, mask in enumerate(slot_masks(cols, row)):
                total = total + jnp.where(mask, flat[(k + 1) * walk:(k + 2) * walk], 0.0)
            bias_ref[...] += total

        return carry

    acc[...] = jnp.zeros_like(acc)
    lax.fori_loop(0, total_steps, step, 0)


def bias_call(vals, greens, cols):
    vectors, rowblocks = vals.shape[:2]
    walk, half_rows, norb = greens.shape
    steps = half_rows // CHUNK
    wide = CHUNK * LANES
    return pl.pallas_call(
        bias_kernel,
        in_specs=[
            pl.BlockSpec(memory_space=pl.ANY),
            pl.BlockSpec(memory_space=pl.ANY),
            pl.BlockSpec(memory_space=pltpu.VMEM),
        ],
        out_specs=[pl.BlockSpec(memory_space=pltpu.VMEM)] * 2,
        out_shape=[
            pltpu.VMEM((steps, vectors, wide), jnp.bfloat16),
            pltpu.VMEM((walk, vectors), jnp.float32),
        ],
        scratch_shapes=[
            pltpu.VMEM((steps, vectors, CHUNK, LANES), jnp.bfloat16),
            pltpu.VMEM((steps, walk, CHUNK, norb), jnp.bfloat16),
            pltpu.VMEM((CHUNK * CHUNK, CHUNK * CHUNK), jnp.bfloat16),
            pltpu.VMEM((4 * walk, wide), jnp.bfloat16),
            pltpu.VMEM((vectors, 4 * walk), jnp.float32),
            pltpu.SemaphoreType.DMA((steps,)),
            pltpu.SemaphoreType.DMA((steps,)),
        ],
        compiler_params=params(24),
        name="force_bias",
    )(vals, greens, cols)


def potential_kernel(start, steps, layout, by_plane, fields_ref, own_ref, *refs):
    nz, plane, own = layout
    others = refs[:lax.axis_size("orb") - 1]
    cols_ref, turned_ref = refs[len(others):len(others) + 2]
    groups = plane if by_plane else nz
    outs = refs[len(others) + 2:len(others) + 2 + groups]
    energy_ref, s_ref, swap = refs[len(others) + 2 + groups:]
    walk, vectors = fields_ref.shape
    rowblocks = cols_ref.shape[0]

    me = lax.axis_index("chol")
    bias = own_ref[...]
    for other in others:
        bias = bias + other[...]
    energy = 0.5 * jnp.sum(bias * bias, axis=1, keepdims=True)
    energy_ref[...] = jnp.broadcast_to(energy, energy_ref.shape)
    shifted = (fields_ref[...] - bias).astype(jnp.bfloat16)
    at = lax.broadcasted_iota(jnp.int32, (walk, walk), 0)
    source = lax.broadcasted_iota(jnp.int32, (walk, walk), 1)
    chip = at // own
    z = (me // plane + chip // plane) % nz
    p = (me % plane) ^ (chip % plane)
    wanted = (z * plane + p) * own + at % own
    pick = (wanted == source).astype(jnp.float32).astype(jnp.bfloat16)
    ordered = jnp.dot(pick, shifted, preferred_element_type=jnp.float32)
    for local in range(rowblocks):
        row = lax.axis_index("orb") * rowblocks + local
        s_ref[local, 0:walk] = ordered.astype(jnp.bfloat16)
        for k, mask in enumerate(slot_masks(cols_ref[local, 1:2, :], row)):
            s_ref[local, (k + 1) * walk:(k + 2) * walk] = jnp.where(mask, ordered, 0.0).astype(jnp.bfloat16)
    swap[...] = swap_matrix()
    first = lax.broadcasted_iota(jnp.int32, (walk, LANES), 1) < BLOCK

    def step(t, carry):
        left = s_ref[lax.div(start + t, BLOCK // CHUNK)]
        tiles = []
        for i in range(0, CHUNK, 2):
            both = jnp.dot(
                left, turned_ref[start + t, :, i * LANES:(i + 2) * LANES], preferred_element_type=jnp.float32
            )
            for side in range(2):
                out = both[:, side * LANES:(side + 1) * LANES]
                near = jnp.where(first, out[0:walk], out[walk:2 * walk])
                far = jnp.where(first, pltpu.roll(out[2 * walk:3 * walk], BLOCK, 1), out[3 * walk:])
                tiles.append(jnp.concatenate([near, far], axis=1).astype(jnp.bfloat16))
        for w0 in range(0, walk, CHUNK):
            mixed = jnp.concatenate([tile[w0:w0 + CHUNK] for tile in tiles], axis=0)
            mixed = jnp.dot(swap[...], mixed, preferred_element_type=jnp.float32).astype(jnp.bfloat16)
            for w in range(CHUNK):
                chip, j = (w0 + w) // own, (w0 + w) % own
                group, inner = (chip % plane, chip // plane) if by_plane else (chip // plane, chip % plane)
                for half in range(2):
                    rows = pl.ds(pl.multiple_of((2 * t + half) * CHUNK, CHUNK), CHUNK)
                    outs[group][inner, j, rows, :] = (
                        mixed[w * CHUNK:(w + 1) * CHUNK, half * LANES:(half + 1) * LANES]
                    )
        return carry

    lax.fori_loop(0, steps, step, 0)


def potential_call(start, steps, layout, by_plane, fields, bias, others, cols, turned):
    nz, plane, own = layout
    walk, vectors = fields.shape
    groups, inner = (plane, nz) if by_plane else (nz, plane)
    rows = 2 * CHUNK
    *parts, energy = pl.pallas_call(
        functools.partial(potential_kernel, start, steps, layout, by_plane),
        out_shape=[
            *[pltpu.VMEM((inner, own, steps * rows, LANES), jnp.bfloat16)] * groups,
            pltpu.VMEM((walk, LANES), jnp.float32),
        ],
        scratch_shapes=[
            pltpu.VMEM((cols.shape[0], 4 * walk, vectors), jnp.bfloat16),
            pltpu.VMEM((CHUNK * CHUNK, CHUNK * CHUNK), jnp.bfloat16),
        ],
        compiler_params=params(16),
        name="potential",
    )(fields, *in_vmem(bias, *others), cols, *in_vmem(turned))
    return parts, energy


def sum_kernel(count, *refs):
    ins, outs = refs[:count], refs[count:]
    for k, out in enumerate(outs):
        total = ins[0][k].astype(jnp.float32)
        for ref in ins[1:]:
            total = total + ref[k].astype(jnp.float32)
        out[...] = total.astype(out.dtype)


def sum_call(arrays):
    pieces = arrays[0].shape[0]
    shape = pltpu.VMEM(arrays[0].shape[1:], jnp.bfloat16)
    return pl.pallas_call(
        functools.partial(sum_kernel, len(arrays)),
        out_shape=[shape] * pieces,
        compiler_params=params(16),
        name="sum_parts",
    )(*in_vmem(*arrays))


def series_kernel(sizes, *refs):
    n_orb, late_steps, early_steps = sizes
    late, early, start = refs[:n_orb], refs[n_orb:2 * n_orb], refs[2 * n_orb:3 * n_orb]
    plane_ref, z_ref, pot, term, total = refs[3 * n_orb:]
    me = lax.axis_index("orb")
    own, half_rows = start[0].shape[:2]
    rowblocks = half_rows // BLOCK
    per = BLOCK // CHUNK
    for d in range(n_orb):
        at = lax.rem(me + d, n_orb)
        term[pl.ds(at, 1)] = start[d][...][None]
        for t in range(rowblocks * per):
            ref, k = (early[d], t) if t < early_steps else (late[d], t - early_steps)
            for half in range(2):
                rows = slice((2 * k + half) * CHUNK, (2 * k + half + 1) * CHUNK)
                pot[pl.ds(at * rowblocks + t // per, 1), :, (t % per) * CHUNK:(t % per + 1) * CHUNK,
                    half * LANES:(half + 1) * LANES] = ref[:, rows, :][None]
    for j in range(own):
        blocks = [term[r // rowblocks, j, (r % rowblocks) * BLOCK:(r % rowblocks + 1) * BLOCK] for r in range(ROWBLK)]
        sums = [jnp.zeros(blocks[0].shape, jnp.float32)] * ROWBLK
        begin = blocks
        for degree in range(1, TAYLOR + 1):
            after = []
            for r in range(ROWBLK):
                right = jnp.concatenate([blocks[c] for c in column_order(r)], axis=0)
                product = jnp.dot(pot[r, j], right, preferred_element_type=jnp.float32)
                after.append((product / degree).astype(jnp.bfloat16))
            blocks = after
            sums = [s + b.astype(jnp.float32) for s, b in zip(sums, blocks)]
        for r in range(ROWBLK):
            moved = begin[r].astype(jnp.float32) + sums[r]
            total[r // rowblocks, j, (r % rowblocks) * BLOCK:(r % rowblocks + 1) * BLOCK] = moved.astype(jnp.bfloat16)
    mine = total[pl.ds(me, 1)][0]
    cut = z_ref.shape[1]
    z_ref[...] = mine[:, :cut]
    plane_ref[...] = mine[:, cut:]


def series_call(sizes, cut, late, early, start):
    n_orb = sizes[0]
    own, half_rows, nocc = start[0].shape
    return pl.pallas_call(
        functools.partial(series_kernel, sizes),
        out_shape=[
            pltpu.VMEM((own, half_rows - cut, nocc), jnp.bfloat16),
            pltpu.VMEM((own, cut, nocc), jnp.bfloat16),
        ],
        scratch_shapes=[
            pltpu.VMEM((ROWBLK, own, BLOCK, 2 * LANES), jnp.bfloat16),
            pltpu.VMEM((n_orb, own, half_rows, nocc), jnp.bfloat16),
            pltpu.VMEM((n_orb, own, half_rows, nocc), jnp.bfloat16),
        ],
        compiler_params=params(16),
        name="series",
    )(*in_vmem(*late, *early, *start))


def place_kernel(layout, *refs):
    nz, plane, own = layout
    z_first, plane_first = refs[:plane], refs[plane:plane + nz]
    out = refs[plane + nz]
    me = lax.axis_index("chol")
    cut = z_first[0].shape[2]
    for dp in range(plane):
        for dz in range(nz):
            chip = lax.rem(me // plane + nz - dz, nz) * plane + (lax.rem(me, plane) ^ dp)
            to = pl.ds(chip * own, own)
            out[to, :cut, :] = z_first[dp][dz]
            out[to, cut:, :] = plane_first[dz][dp]


def place_call(layout, z_first, plane_first):
    nz, plane, own = layout
    cut, rest, nocc = z_first[0].shape[2], plane_first[0].shape[2], z_first[0].shape[3]
    return pl.pallas_call(
        functools.partial(place_kernel, layout),
        out_shape=jax.ShapeDtypeStruct((nz * plane * own, cut + rest, nocc), jnp.bfloat16),
        compiler_params=params(16),
        name="place_walkers",
    )(*in_vmem(*z_first, *plane_first))


def per_device(chol_vals, chol_cols, greens, walkers, fields):
    vectors, rowblocks = chol_vals.shape[:2]
    walk, half_rows = greens.shape[:2]
    chips = lax.axis_size("chol")
    n_orb = lax.axis_size("orb")
    plane = 4 if chips % 4 == 0 else 1
    nz = chips // plane
    own = walk // chips
    layout = (nz, plane, own)
    step_factor = 72.0 / float(vectors * chips * BLOCK) ** 0.5
    me = lax.axis_index("chol")

    def to_plane(a, dp):
        return lax.ppermute(a, "chol", [(c, (c // plane) * plane + ((c % plane) ^ dp)) for c in range(chips)])

    def to_z(a, dz):
        return lax.ppermute(a, "chol", [(c, ((c // plane + dz) % nz) * plane + c % plane) for c in range(chips)])

    def around_orb(a):
        return [a] + [lax.ppermute(a, "orb", [((c + d) % n_orb, c) for c in range(n_orb)]) for d in range(1, n_orb)]

    cols = jnp.transpose(chol_cols, (1, 2, 0))
    mine = lax.dynamic_slice_in_dim(walkers, me * own, own, 0)
    start = around_orb(mine)

    turned, partial_bias = bias_call(chol_vals, greens, cols)
    bias, *others = around_orb(partial_bias)

    total_steps = rowblocks * BLOCK // CHUNK
    early_steps = total_steps * 3 // 8
    late_steps = total_steps - early_steps
    fields_t = fields.T
    early, energy = potential_call(0, early_steps, layout, False, fields_t, bias, others, cols, turned)
    early_in = [early[0]] + [to_z(early[dz], dz) for dz in range(1, nz)]
    late, _ = potential_call(early_steps, late_steps, layout, True, fields_t, bias, others, cols, turned)
    late_in = [late[0]] + [to_plane(late[dp], dp) for dp in range(1, plane)]
    energy = energy[:, 0]
    energy_in = [to_plane(energy, dp) for dp in range(1, plane)]
    start, energy_in, early_in = lax.optimization_barrier((start, energy_in, early_in))
    energy = energy + sum(energy_in)
    early_sums = sum_call(early_in)
    early_in = [early_sums[0]] + [to_plane(early_sums[dp], dp) for dp in range(1, plane)]
    late_sums = sum_call(late_in)
    late_in = [late_sums[0]] + [to_z(late_sums[dz], dz) for dz in range(1, nz)]

    energy_in = [to_z(energy, dz) for dz in range(1, nz)]
    energy_in, late_in = lax.optimization_barrier((energy_in, late_in))
    energy = energy + sum(energy_in)

    def finish(arrays):
        total = arrays[0].astype(jnp.float32)
        for a in arrays[1:]:
            total = total + a.astype(jnp.float32)
        return around_orb((step_factor * total).astype(jnp.bfloat16))

    cut = half_rows // CHUNK * 5 // 8 * CHUNK
    b_part, a_part = series_call((n_orb, late_steps, early_steps), cut, finish(late_in), finish(early_in), start)

    a_all = jnp.stack([a_part] + [to_z(a_part, dz) for dz in range(1, nz)])
    b_all = jnp.stack([b_part] + [to_plane(b_part, dp) for dp in range(1, plane)])
    z_first = [a_all] + [to_plane(a_all, dp) for dp in range(1, plane)]
    plane_first = [b_all] + [to_z(b_all, dz) for dz in range(1, nz)]
    return place_call(layout, z_first, plane_first), energy


def solution(mesh):
    in_specs = (
        P("chol", "orb", None, None),
        P("chol", "orb", None),
        P("walker", "orb", None),
        P("walker", "orb", None),
        P("chol", "walker"),
    )
    out_specs = (P("walker", "orb", None), P("walker"))
    return jax.shard_map(
        per_device, mesh=mesh, in_specs=in_specs, out_specs=out_specs, check_vma=False
    )
```

```python
import functools

import jax
import jax.numpy as jnp
from jax import lax
from jax.experimental import pallas as pl
from jax.experimental.pallas import tpu as pltpu
from jax.sharding import PartitionSpec as P

BLOCK = 64
TAYLOR = 4
ROWBLK = 4
LANES = 2 * BLOCK
CHUNK = 16
MIB = 1024 * 1024


def params(mib):
    return pltpu.CompilerParams(vmem_limit_bytes=mib * MIB)


def in_vmem(*arrays):
    return [pltpu.with_memory_space_constraint(a, pltpu.VMEM) for a in arrays]


def in_hbm(*arrays):
    return [pltpu.with_memory_space_constraint(a, pltpu.HBM) for a in arrays]


def swap_matrix():
    to = lax.broadcasted_iota(jnp.int32, (CHUNK * CHUNK, CHUNK * CHUNK), 0)
    at = lax.broadcasted_iota(jnp.int32, (CHUNK * CHUNK, CHUNK * CHUNK), 1)
    same = (to // CHUNK == at % CHUNK) & (to % CHUNK == at // CHUNK)
    return same.astype(jnp.float32).astype(jnp.bfloat16)


def column_order(row):
    other = 2 - 2 * (row // 2)
    return row, row + 1 - 2 * (row % 2), other, other + 1


def slot_masks(cols, row):
    return [cols == column for column in column_order(row)[1:]]


def bias_kernel(vals_hbm, greens_hbm, walkers_hbm, cols_ref, turned_ref, bias_ref, mine_ref, vals, greens, swap, gs, acc, vsem,
                gsem, wsem):
    total_steps, vectors = turned_ref.shape[:2]
    walk = bias_ref.shape[0]
    steps = BLOCK // CHUNK

    def copies(t):
        rows = pl.ds(lax.rem(t, steps) * CHUNK, CHUNK)
        return (
            pltpu.make_async_copy(vals_hbm.at[:, lax.div(t, steps), rows, :], vals.at[t], vsem.at[t]),
            pltpu.make_async_copy(greens_hbm.at[:, pl.ds(t * CHUNK, CHUNK), :], greens.at[t], gsem.at[t]),
        )

    def begin(t, carry):
        for copy in copies(t):
            copy.start()
        return carry

    own = mine_ref.shape[0]
    lax.fori_loop(0, total_steps, begin, 0)
    take = pltpu.make_async_copy(walkers_hbm.at[pl.ds(lax.axis_index("chol") * own, own)], mine_ref, wsem)
    take.start()
    swap[...] = swap_matrix()
    bias_ref[...] = jnp.zeros_like(bias_ref)
    first = lax.broadcasted_iota(jnp.int32, (CHUNK * CHUNK, LANES), 1) < BLOCK

    def step(t, carry):
        for copy in copies(t):
            copy.wait()
        local = lax.div(t, steps)
        row = lax.axis_index("orb") * cols_ref.shape[0] + local
        upper = row // 2 == 1
        odd = row % 2 == 1
        for w in range(0, walk, CHUNK):
            mixed = greens[t, w:w + CHUNK].reshape(CHUNK * CHUNK, 2 * LANES)
            mixed = jnp.dot(swap[...], mixed, preferred_element_type=jnp.float32)
            pair = jnp.where(upper, mixed[:, LANES:], mixed[:, :LANES])
            rest = jnp.where(upper, mixed[:, :LANES], mixed[:, LANES:])
            pair = jnp.where(odd, pltpu.roll(pair, BLOCK, 1), pair)
            pieces = (
                jnp.where(first, pair, 0.0),
                jnp.where(first, 0.0, pair),
                jnp.where(first, 0.0, pltpu.roll(rest, BLOCK, 1)),
                jnp.where(first, 0.0, rest),
            )
            for k, piece in enumerate(pieces):
                piece = piece.astype(jnp.bfloat16)
                for i in range(CHUNK):
                    gs[k * walk + w:k * walk + w + CHUNK, i * LANES:(i + 1) * LANES] = piece[i * CHUNK:(i + 1) * CHUNK]
        for g in range(0, vectors, 2 * CHUNK):
            both = [vals[t, g + side * CHUNK:g + (side + 1) * CHUNK].reshape(CHUNK * CHUNK, LANES) for side in range(2)]
            both = jnp.dot(swap[...], jnp.concatenate(both, axis=1), preferred_element_type=jnp.float32)
            both = both.astype(jnp.bfloat16)
            for i in range(CHUNK):
                for side in range(2):
                    turned_ref[t, g + side * CHUNK:g + (side + 1) * CHUNK, i * LANES:(i + 1) * LANES] = (
                        both[i * CHUNK:(i + 1) * CHUNK, side * LANES:(side + 1) * LANES]
                    )
        part = lax.dot_general(
            turned_ref[t], gs[...], (((1,), (1,)), ((), ())), preferred_element_type=jnp.float32
        )
        begins = lax.rem(t, steps) == 0
        acc[...] = jnp.where(begins, 0.0, acc[...]) + part

        @pl.when(lax.rem(t, steps) == steps - 1)
        def _():
            flat = acc[...].T
            total = flat[0:walk]
            cols = cols_ref[local, 1:2, :]
            for k, mask in enumerate(slot_masks(cols, row)):
                total = total + jnp.where(mask, flat[(k + 1) * walk:(k + 2) * walk], 0.0)
            bias_ref[...] += total

        return carry

    acc[...] = jnp.zeros_like(acc)
    lax.fori_loop(0, total_steps, step, 0)
    take.wait()


def bias_call(vals, greens, walkers, cols, own):
    vectors, rowblocks = vals.shape[:2]
    walk, half_rows, norb = greens.shape
    steps = half_rows // CHUNK
    wide = CHUNK * LANES
    return pl.pallas_call(
        bias_kernel,
        in_specs=[
            *[pl.BlockSpec(memory_space=pl.ANY)] * 3,
            pl.BlockSpec(memory_space=pltpu.VMEM),
        ],
        out_specs=[pl.BlockSpec(memory_space=pltpu.VMEM)] * 3,
        out_shape=[
            pltpu.VMEM((steps, vectors, wide), jnp.bfloat16),
            pltpu.VMEM((walk, vectors), jnp.float32),
            pltpu.VMEM((own, *walkers.shape[1:]), jnp.bfloat16),
        ],
        scratch_shapes=[
            pltpu.VMEM((steps, vectors, CHUNK, LANES), jnp.bfloat16),
            pltpu.VMEM((steps, walk, CHUNK, norb), jnp.bfloat16),
            pltpu.VMEM((CHUNK * CHUNK, CHUNK * CHUNK), jnp.bfloat16),
            pltpu.VMEM((4 * walk, wide), jnp.bfloat16),
            pltpu.VMEM((vectors, 4 * walk), jnp.float32),
            pltpu.SemaphoreType.DMA((steps,)),
            pltpu.SemaphoreType.DMA((steps,)),
            pltpu.SemaphoreType.DMA,
        ],
        compiler_params=params(24),
        name="force_bias",
    )(*in_hbm(vals, greens, walkers), cols)


def potential_kernel(start, steps, layout, by_plane, fields_ref, own_ref, *refs):
    nz, plane, own = layout
    others = refs[:lax.axis_size("orb") - 1]
    cols_ref, turned_ref = refs[len(others):len(others) + 2]
    groups = plane if by_plane else nz
    outs = refs[len(others) + 2:len(others) + 2 + groups]
    energy_ref, s_ref, swap = refs[len(others) + 2 + groups:]
    walk, vectors = fields_ref.shape
    rowblocks = cols_ref.shape[0]

    me = lax.axis_index("chol")
    bias = own_ref[...]
    for other in others:
        bias = bias + other[...]
    energy = 0.5 * jnp.sum(bias * bias, axis=1, keepdims=True)
    energy_ref[...] = jnp.broadcast_to(energy, energy_ref.shape)
    shifted = (fields_ref[...] - bias).astype(jnp.bfloat16)
    at = lax.broadcasted_iota(jnp.int32, (walk, walk), 0)
    source = lax.broadcasted_iota(jnp.int32, (walk, walk), 1)
    chip = at // own
    z = (me // plane + chip // plane) % nz
    p = (me % plane) ^ (chip % plane)
    wanted = (z * plane + p) * own + at % own
    pick = (wanted == source).astype(jnp.float32).astype(jnp.bfloat16)
    ordered = jnp.dot(pick, shifted, preferred_element_type=jnp.float32)
    for local in range(rowblocks):
        row = lax.axis_index("orb") * rowblocks + local
        s_ref[local, 0:walk] = ordered.astype(jnp.bfloat16)
        for k, mask in enumerate(slot_masks(cols_ref[local, 1:2, :], row)):
            s_ref[local, (k + 1) * walk:(k + 2) * walk] = jnp.where(mask, ordered, 0.0).astype(jnp.bfloat16)
    swap[...] = swap_matrix()
    first = lax.broadcasted_iota(jnp.int32, (walk, LANES), 1) < BLOCK

    def step(t, carry):
        left = s_ref[lax.div(start + t, BLOCK // CHUNK)]
        tiles = []
        for i in range(0, CHUNK, 2):
            both = jnp.dot(
                left, turned_ref[start + t, :, i * LANES:(i + 2) * LANES], preferred_element_type=jnp.float32
            )
            for side in range(2):
                out = both[:, side * LANES:(side + 1) * LANES]
                near = jnp.where(first, out[0:walk], out[walk:2 * walk])
                far = jnp.where(first, pltpu.roll(out[2 * walk:3 * walk], BLOCK, 1), out[3 * walk:])
                tiles.append(jnp.concatenate([near, far], axis=1).astype(jnp.bfloat16))
        for w0 in range(0, walk, CHUNK):
            mixed = jnp.concatenate([tile[w0:w0 + CHUNK] for tile in tiles], axis=0)
            mixed = jnp.dot(swap[...], mixed, preferred_element_type=jnp.float32).astype(jnp.bfloat16)
            for w in range(CHUNK):
                chip, j = (w0 + w) // own, (w0 + w) % own
                group, inner = (chip % plane, chip // plane) if by_plane else (chip // plane, chip % plane)
                for half in range(2):
                    rows = pl.ds(pl.multiple_of((2 * t + half) * CHUNK, CHUNK), CHUNK)
                    outs[group][inner, j, rows, :] = (
                        mixed[w * CHUNK:(w + 1) * CHUNK, half * LANES:(half + 1) * LANES]
                    )
        return carry

    lax.fori_loop(0, steps, step, 0)


def potential_call(start, steps, layout, by_plane, fields, bias, others, cols, turned):
    nz, plane, own = layout
    walk, vectors = fields.shape
    groups, inner = (plane, nz) if by_plane else (nz, plane)
    rows = 2 * CHUNK
    *parts, energy = pl.pallas_call(
        functools.partial(potential_kernel, start, steps, layout, by_plane),
        out_shape=[
            *[pltpu.VMEM((inner, own, steps * rows, LANES), jnp.bfloat16)] * groups,
            pltpu.VMEM((walk, LANES), jnp.float32),
        ],
        scratch_shapes=[
            pltpu.VMEM((cols.shape[0], 4 * walk, vectors), jnp.bfloat16),
            pltpu.VMEM((CHUNK * CHUNK, CHUNK * CHUNK), jnp.bfloat16),
        ],
        compiler_params=params(16),
        name="potential",
    )(fields, *in_vmem(bias, *others), cols, *in_vmem(turned))
    return parts, energy


def sum_kernel(count, *refs):
    ins, outs = refs[:count], refs[count:]
    for k, out in enumerate(outs):
        total = ins[0][k].astype(jnp.float32)
        for ref in ins[1:]:
            total = total + ref[k].astype(jnp.float32)
        out[...] = total.astype(out.dtype)


def sum_call(arrays):
    pieces = arrays[0].shape[0]
    shape = pltpu.VMEM(arrays[0].shape[1:], jnp.bfloat16)
    return pl.pallas_call(
        functools.partial(sum_kernel, len(arrays)),
        out_shape=[shape] * pieces,
        compiler_params=params(16),
        name="sum_parts",
    )(*in_vmem(*arrays))


def series_kernel(sizes, *refs):
    n_orb, late_steps, early_steps = sizes
    late, early, start = refs[:n_orb], refs[n_orb:2 * n_orb], refs[2 * n_orb:3 * n_orb]
    plane_ref, z_ref, pot, term, total = refs[3 * n_orb:]
    me = lax.axis_index("orb")
    own, half_rows = start[0].shape[:2]
    rowblocks = half_rows // BLOCK
    per = BLOCK // CHUNK
    for d in range(n_orb):
        at = lax.rem(me + d, n_orb)
        term[pl.ds(at, 1)] = start[d][...][None]
        for t in range(rowblocks * per):
            ref, k = (early[d], t) if t < early_steps else (late[d], t - early_steps)
            for half in range(2):
                rows = slice((2 * k + half) * CHUNK, (2 * k + half + 1) * CHUNK)
                pot[pl.ds(at * rowblocks + t // per, 1), :, (t % per) * CHUNK:(t % per + 1) * CHUNK,
                    half * LANES:(half + 1) * LANES] = ref[:, rows, :][None]
    for j in range(own):
        blocks = [term[r // rowblocks, j, (r % rowblocks) * BLOCK:(r % rowblocks + 1) * BLOCK] for r in range(ROWBLK)]
        sums = [jnp.zeros(blocks[0].shape, jnp.float32)] * ROWBLK
        begin = blocks
        for degree in range(1, TAYLOR + 1):
            after = []
            for r in range(ROWBLK):
                right = jnp.concatenate([blocks[c] for c in column_order(r)], axis=0)
                product = jnp.dot(pot[r, j], right, preferred_element_type=jnp.float32)
                after.append((product / degree).astype(jnp.bfloat16))
            blocks = after
            sums = [s + b.astype(jnp.float32) for s, b in zip(sums, blocks)]
        for r in range(ROWBLK):
            moved = begin[r].astype(jnp.float32) + sums[r]
            total[r // rowblocks, j, (r % rowblocks) * BLOCK:(r % rowblocks + 1) * BLOCK] = moved.astype(jnp.bfloat16)
    mine = total[pl.ds(me, 1)][0]
    cut = z_ref.shape[1]
    z_ref[...] = mine[:, :cut]
    plane_ref[...] = mine[:, cut:]


def series_call(sizes, cut, late, early, start):
    n_orb = sizes[0]
    own, half_rows, nocc = start[0].shape
    return pl.pallas_call(
        functools.partial(series_kernel, sizes),
        out_shape=[
            pltpu.VMEM((own, half_rows - cut, nocc), jnp.bfloat16),
            pltpu.VMEM((own, cut, nocc), jnp.bfloat16),
        ],
        scratch_shapes=[
            pltpu.VMEM((ROWBLK, own, BLOCK, 2 * LANES), jnp.bfloat16),
            pltpu.VMEM((n_orb, own, half_rows, nocc), jnp.bfloat16),
            pltpu.VMEM((n_orb, own, half_rows, nocc), jnp.bfloat16),
        ],
        compiler_params=params(16),
        name="series",
    )(*in_vmem(*late, *early, *start))


def place_kernel(layout, *refs):
    nz, plane, own = layout
    z_first, plane_first = refs[:plane], refs[plane:plane + nz]
    out = refs[plane + nz]
    me = lax.axis_index("chol")
    cut = z_first[0].shape[2]
    for dp in range(plane):
        for dz in range(nz):
            chip = lax.rem(me // plane + nz - dz, nz) * plane + (lax.rem(me, plane) ^ dp)
            to = pl.ds(chip * own, own)
            out[to, :cut, :] = z_first[dp][dz]
            out[to, cut:, :] = plane_first[dz][dp]


def place_call(layout, z_first, plane_first):
    nz, plane, own = layout
    cut, rest, nocc = z_first[0].shape[2], plane_first[0].shape[2], z_first[0].shape[3]
    return pl.pallas_call(
        functools.partial(place_kernel, layout),
        out_shape=jax.ShapeDtypeStruct((nz * plane * own, cut + rest, nocc), jnp.bfloat16),
        compiler_params=params(16),
        name="place_walkers",
    )(*in_vmem(*z_first, *plane_first))


def per_device(chol_vals, chol_cols, greens, walkers, fields):
    vectors, rowblocks = chol_vals.shape[:2]
    walk, half_rows = greens.shape[:2]
    chips = lax.axis_size("chol")
    n_orb = lax.axis_size("orb")
    plane = 4 if chips % 4 == 0 else 1
    nz = chips // plane
    own = walk // chips
    layout = (nz, plane, own)
    step_factor = 72.0 / float(vectors * chips * BLOCK) ** 0.5

    def to_plane(a, dp):
        return lax.ppermute(a, "chol", [(c, (c // plane) * plane + ((c % plane) ^ dp)) for c in range(chips)])

    def to_z(a, dz):
        return lax.ppermute(a, "chol", [(c, ((c // plane + dz) % nz) * plane + c % plane) for c in range(chips)])

    def around_orb(a):
        return [a] + [lax.ppermute(a, "orb", [((c + d) % n_orb, c) for c in range(n_orb)]) for d in range(1, n_orb)]

    cols = jnp.transpose(chol_cols, (1, 2, 0))
    turned, partial_bias, mine = bias_call(chol_vals, greens, walkers, cols, own)
    start = around_orb(mine)
    bias, *others = around_orb(partial_bias)

    total_steps = rowblocks * BLOCK // CHUNK
    early_steps = total_steps * 3 // 8
    late_steps = total_steps - early_steps
    fields_t = fields.T
    early, energy = potential_call(0, early_steps, layout, False, fields_t, bias, others, cols, turned)
    early_in = [early[0]] + [to_z(early[dz], dz) for dz in range(1, nz)]
    late, _ = potential_call(early_steps, late_steps, layout, True, fields_t, bias, others, cols, turned)
    late_in = [late[0]] + [to_plane(late[dp], dp) for dp in range(1, plane)]
    energy = energy[:, 0]
    energy_in = [to_plane(energy, dp) for dp in range(1, plane)]
    start, energy_in, early_in = lax.optimization_barrier((start, energy_in, early_in))
    energy = energy + sum(energy_in)
    early_sums = sum_call(early_in)
    early_in = [early_sums[0]] + [to_plane(early_sums[dp], dp) for dp in range(1, plane)]
    late_sums = sum_call(late_in)
    late_in = [late_sums[0]] + [to_z(late_sums[dz], dz) for dz in range(1, nz)]

    energy_in = [to_z(energy, dz) for dz in range(1, nz)]
    energy_in, late_in = lax.optimization_barrier((energy_in, late_in))
    energy = energy + sum(energy_in)

    def finish(arrays):
        total = arrays[0].astype(jnp.float32)
        for a in arrays[1:]:
            total = total + a.astype(jnp.float32)
        return around_orb((step_factor * total).astype(jnp.bfloat16))

    cut = half_rows // CHUNK * 5 // 8 * CHUNK
    b_part, a_part = series_call((n_orb, late_steps, early_steps), cut, finish(late_in), finish(early_in), start)

    a_all = jnp.stack([a_part] + [to_z(a_part, dz) for dz in range(1, nz)])
    b_all = jnp.stack([b_part] + [to_plane(b_part, dp) for dp in range(1, plane)])
    z_first = [a_all] + [to_plane(a_all, dp) for dp in range(1, plane)]
    plane_first = [b_all] + [to_z(b_all, dz) for dz in range(1, nz)]
    return place_call(layout, z_first, plane_first), energy


def solution(mesh):
    in_specs = (
        P("chol", "orb", None, None),
        P("chol", "orb", None),
        P("walker", "orb", None),
        P("walker", "orb", None),
        P("chol", "walker"),
    )
    out_specs = (P("walker", "orb", None), P("walker"))
    return jax.shard_map(
        per_device, mesh=mesh, in_specs=in_specs, out_specs=out_specs, check_vma=False
    )
```

```python
import functools

import jax
import jax.numpy as jnp
from jax import lax
from jax.experimental import pallas as pl
from jax.experimental.pallas import tpu as pltpu
from jax.sharding import PartitionSpec as P

BLOCK = 64
TAYLOR = 4
ROWBLK = 4
LANES = 2 * BLOCK
CHUNK = 16
MIB = 1024 * 1024


def params(mib):
    return pltpu.CompilerParams(vmem_limit_bytes=mib * MIB)


def in_vmem(*arrays):
    return [pltpu.with_memory_space_constraint(a, pltpu.VMEM) for a in arrays]


def in_hbm(*arrays):
    return [pltpu.with_memory_space_constraint(a, pltpu.HBM) for a in arrays]


def swap_matrix():
    to = lax.broadcasted_iota(jnp.int32, (CHUNK * CHUNK, CHUNK * CHUNK), 0)
    at = lax.broadcasted_iota(jnp.int32, (CHUNK * CHUNK, CHUNK * CHUNK), 1)
    same = (to // CHUNK == at % CHUNK) & (to % CHUNK == at // CHUNK)
    return same.astype(jnp.float32).astype(jnp.bfloat16)


def column_order(row):
    other = 2 - 2 * (row // 2)
    return row, row + 1 - 2 * (row % 2), other, other + 1


def slot_masks(cols, row):
    return [cols == column for column in column_order(row)[1:]]


def bias_kernel(vals_hbm, greens_hbm, walkers_hbm, cols_ref, turned_ref, bias_ref, mine_ref, vals, greens, swap, gs, acc, vsem,
                gsem, wsem):
    total_steps, vectors = turned_ref.shape[:2]
    walk = bias_ref.shape[0]
    steps = BLOCK // CHUNK

    def copies(t):
        rows = pl.ds(lax.rem(t, steps) * CHUNK, CHUNK)
        return (
            pltpu.make_async_copy(vals_hbm.at[:, lax.div(t, steps), rows, :], vals.at[t], vsem.at[t]),
            pltpu.make_async_copy(greens_hbm.at[:, pl.ds(t * CHUNK, CHUNK), :], greens.at[t], gsem.at[t]),
        )

    def begin(t, carry):
        for copy in copies(t):
            copy.start()
        return carry

    own = mine_ref.shape[0]
    lax.fori_loop(0, total_steps, begin, 0)
    take = pltpu.make_async_copy(walkers_hbm.at[pl.ds(lax.axis_index("chol") * own, own)], mine_ref, wsem)
    take.start()
    swap[...] = swap_matrix()
    bias_ref[...] = jnp.zeros_like(bias_ref)
    first = lax.broadcasted_iota(jnp.int32, (CHUNK * CHUNK, LANES), 1) < BLOCK

    def step(t, carry):
        for copy in copies(t):
            copy.wait()
        local = lax.div(t, steps)
        row = lax.axis_index("orb") * cols_ref.shape[0] + local
        upper = row // 2 == 1
        odd = row % 2 == 1
        for w in range(0, walk, CHUNK):
            mixed = greens[t, w:w + CHUNK].reshape(CHUNK * CHUNK, 2 * LANES)
            mixed = jnp.dot(swap[...], mixed, preferred_element_type=jnp.float32)
            pair = jnp.where(upper, mixed[:, LANES:], mixed[:, :LANES])
            rest = jnp.where(upper, mixed[:, :LANES], mixed[:, LANES:])
            pair = jnp.where(odd, pltpu.roll(pair, BLOCK, 1), pair)
            pieces = (
                jnp.where(first, pair, 0.0),
                jnp.where(first, 0.0, pair),
                jnp.where(first, 0.0, pltpu.roll(rest, BLOCK, 1)),
                jnp.where(first, 0.0, rest),
            )
            for k, piece in enumerate(pieces):
                piece = piece.astype(jnp.bfloat16)
                for i in range(CHUNK):
                    gs[k * walk + w:k * walk + w + CHUNK, i * LANES:(i + 1) * LANES] = piece[i * CHUNK:(i + 1) * CHUNK]
        for g in range(0, vectors, 2 * CHUNK):
            both = [vals[t, g + side * CHUNK:g + (side + 1) * CHUNK].reshape(CHUNK * CHUNK, LANES) for side in range(2)]
            both = jnp.dot(swap[...], jnp.concatenate(both, axis=1), preferred_element_type=jnp.float32)
            both = both.astype(jnp.bfloat16)
            for i in range(CHUNK):
                for side in range(2):
                    turned_ref[t, g + side * CHUNK:g + (side + 1) * CHUNK, i * LANES:(i + 1) * LANES] = (
                        both[i * CHUNK:(i + 1) * CHUNK, side * LANES:(side + 1) * LANES]
                    )
        part = lax.dot_general(
            turned_ref[t], gs[...], (((1,), (1,)), ((), ())), preferred_element_type=jnp.float32
        )
        begins = lax.rem(t, steps) == 0
        acc[...] = jnp.where(begins, 0.0, acc[...]) + part

        @pl.when(lax.rem(t, steps) == steps - 1)
        def _():
            flat = acc[...].T
            total = flat[0:walk]
            cols = cols_ref[local, 1:2, :]
            for k, mask in enumerate(slot_masks(cols, row)):
                total = total + jnp.where(mask, flat[(k + 1) * walk:(k + 2) * walk], 0.0)
            bias_ref[...] += total

        return carry

    acc[...] = jnp.zeros_like(acc)
    lax.fori_loop(0, total_steps, step, 0)
    take.wait()


def bias_call(vals, greens, walkers, cols, own):
    vectors, rowblocks = vals.shape[:2]
    walk, half_rows, norb = greens.shape
    steps = half_rows // CHUNK
    wide = CHUNK * LANES
    return pl.pallas_call(
        bias_kernel,
        in_specs=[
            *[pl.BlockSpec(memory_space=pl.ANY)] * 3,
            pl.BlockSpec(memory_space=pltpu.VMEM),
        ],
        out_specs=[pl.BlockSpec(memory_space=pltpu.VMEM)] * 3,
        out_shape=[
            pltpu.VMEM((steps, vectors, wide), jnp.bfloat16),
            pltpu.VMEM((walk, vectors), jnp.float32),
            pltpu.VMEM((own, *walkers.shape[1:]), jnp.bfloat16),
        ],
        scratch_shapes=[
            pltpu.VMEM((steps, vectors, CHUNK, LANES), jnp.bfloat16),
            pltpu.VMEM((steps, walk, CHUNK, norb), jnp.bfloat16),
            pltpu.VMEM((CHUNK * CHUNK, CHUNK * CHUNK), jnp.bfloat16),
            pltpu.VMEM((4 * walk, wide), jnp.bfloat16),
            pltpu.VMEM((vectors, 4 * walk), jnp.float32),
            pltpu.SemaphoreType.DMA((steps,)),
            pltpu.SemaphoreType.DMA((steps,)),
            pltpu.SemaphoreType.DMA,
        ],
        compiler_params=params(24),
        name="force_bias",
    )(*in_hbm(vals, greens, walkers), cols)


def potential_kernel(early_steps, layout, fields_ref, own_ref, *refs):
    nz, plane, own = layout
    others = refs[:lax.axis_size("orb") - 1]
    cols_ref, turned_ref, early_ref, late_ref, energy_ref, s_ref, swap = refs[len(others):]
    walk, vectors = fields_ref.shape
    rowblocks = cols_ref.shape[0]

    bias = own_ref[...]
    for other in others:
        bias = bias + other[...]
    energy = 0.5 * jnp.sum(bias * bias, axis=1, keepdims=True)
    energy_ref[...] = jnp.zeros_like(energy_ref)
    energy_ref[:, :walk] = jnp.broadcast_to(energy, (walk, LANES)).T[:CHUNK]
    shifted = (fields_ref[...] - bias).astype(jnp.bfloat16).astype(jnp.float32)
    for local in range(rowblocks):
        row = lax.axis_index("orb") * rowblocks + local
        s_ref[local, 0:walk] = shifted.astype(jnp.bfloat16)
        for k, mask in enumerate(slot_masks(cols_ref[local, 1:2, :], row)):
            s_ref[local, (k + 1) * walk:(k + 2) * walk] = jnp.where(mask, shifted, 0.0).astype(jnp.bfloat16)
    swap[...] = swap_matrix()
    first = lax.broadcasted_iota(jnp.int32, (walk, LANES), 1) < BLOCK

    def steps(out_ref, start, count, by_plane):
        def step(t, carry):
            left = s_ref[lax.div(start + t, BLOCK // CHUNK)]
            tiles = []
            for i in range(0, CHUNK, 2):
                both = jnp.dot(
                    left, turned_ref[start + t, :, i * LANES:(i + 2) * LANES], preferred_element_type=jnp.float32
                )
                for side in range(2):
                    out = both[:, side * LANES:(side + 1) * LANES]
                    near = jnp.where(first, out[0:walk], out[walk:2 * walk])
                    far = jnp.where(first, pltpu.roll(out[2 * walk:3 * walk], BLOCK, 1), out[3 * walk:])
                    tiles.append(jnp.concatenate([near, far], axis=1).astype(jnp.bfloat16))
            for w0 in range(0, walk, CHUNK):
                mixed = jnp.concatenate([tile[w0:w0 + CHUNK] for tile in tiles], axis=0)
                mixed = jnp.dot(swap[...], mixed, preferred_element_type=jnp.float32).astype(jnp.bfloat16)
                for w in range(CHUNK):
                    chip, j = (w0 + w) // own, (w0 + w) % own
                    at = (chip % plane, chip // plane) if by_plane else (chip // plane, chip % plane)
                    for half in range(2):
                        rows = pl.ds(pl.multiple_of((2 * t + half) * CHUNK, CHUNK), CHUNK)
                        out_ref[(*at, j, rows)] = mixed[w * CHUNK:(w + 1) * CHUNK, half * LANES:(half + 1) * LANES]
            return carry

        lax.fori_loop(0, count, step, 0)

    steps(early_ref, 0, early_steps, False)
    steps(late_ref, early_steps, turned_ref.shape[0] - early_steps, True)


def potential_call(early_steps, layout, fields, bias, others, cols, turned):
    nz, plane, own = layout
    walk, vectors = fields.shape
    rows = 2 * CHUNK
    return pl.pallas_call(
        functools.partial(potential_kernel, early_steps, layout),
        out_shape=[
            pltpu.VMEM((nz, plane, own, early_steps * rows, LANES), jnp.bfloat16),
            pltpu.VMEM((plane, nz, own, (turned.shape[0] - early_steps) * rows, LANES), jnp.bfloat16),
            pltpu.VMEM((CHUNK, LANES), jnp.float32),
        ],
        scratch_shapes=[
            pltpu.VMEM((cols.shape[0], 4 * walk, vectors), jnp.bfloat16),
            pltpu.VMEM((CHUNK * CHUNK, CHUNK * CHUNK), jnp.bfloat16),
        ],
        compiler_params=params(16),
        name="potential",
    )(fields, *in_vmem(bias, *others), cols, *in_vmem(turned))


def sum_kernel(in_ref, out_ref):
    for k in range(out_ref.shape[0]):
        total = in_ref[0, k].astype(jnp.float32)
        for source in range(1, in_ref.shape[0]):
            total = total + in_ref[source, k].astype(jnp.float32)
        out_ref[k] = total.astype(out_ref.dtype)


def sum_call(array):
    return pl.pallas_call(
        sum_kernel,
        out_shape=pltpu.VMEM(array.shape[1:], jnp.bfloat16),
        compiler_params=params(16),
        name="sum_parts",
    )(*in_vmem(array))


def split(value):
    parts = []
    for _ in range(3):
        parts.append(value.astype(jnp.bfloat16))
        value = value - parts[-1].astype(jnp.float32)
    return parts


def series_kernel(sizes, *refs):
    n_orb, late_steps, early_steps = sizes
    late, early, start = refs[:n_orb], refs[n_orb:2 * n_orb], refs[2 * n_orb:3 * n_orb]
    energy_ref, plane_ref, z_ref, pot, term, total = refs[3 * n_orb:]
    me = lax.axis_index("orb")
    own, half_rows = start[0].shape[:2]
    rowblocks = half_rows // BLOCK
    per = BLOCK // CHUNK
    for d in range(n_orb):
        at = lax.rem(me + d, n_orb)
        term[pl.ds(at, 1)] = start[d][...][None]
        for t in range(rowblocks * per):
            ref, k = (early[d], t) if t < early_steps else (late[d], t - early_steps)
            for half in range(2):
                rows = slice((2 * k + half) * CHUNK, (2 * k + half + 1) * CHUNK)
                pot[pl.ds(at * rowblocks + t // per, 1), :, (t % per) * CHUNK:(t % per + 1) * CHUNK,
                    half * LANES:(half + 1) * LANES] = ref[:, rows, :][None]
    for j in range(own):
        blocks = [term[r // rowblocks, j, (r % rowblocks) * BLOCK:(r % rowblocks + 1) * BLOCK] for r in range(ROWBLK)]
        sums = [jnp.zeros(blocks[0].shape, jnp.float32)] * ROWBLK
        begin = blocks
        for degree in range(1, TAYLOR + 1):
            after = []
            for r in range(ROWBLK):
                right = jnp.concatenate([blocks[c] for c in column_order(r)], axis=0)
                product = jnp.dot(pot[r, j], right, preferred_element_type=jnp.float32)
                after.append((product / degree).astype(jnp.bfloat16))
            blocks = after
            sums = [s + b.astype(jnp.float32) for s, b in zip(sums, blocks)]
        for r in range(ROWBLK):
            moved = begin[r].astype(jnp.float32) + sums[r]
            total[r // rowblocks, j, (r % rowblocks) * BLOCK:(r % rowblocks + 1) * BLOCK] = moved.astype(jnp.bfloat16)
    mine = total[pl.ds(me, 1)][0]
    cut = (z_ref.shape[1] - CHUNK) // own
    tile = lax.broadcasted_iota(jnp.int32, (CHUNK, LANES), 0)
    high, middle, low = (part.astype(jnp.float32) for part in split(energy_ref[...]))
    tile = jnp.where(tile == 0, high, jnp.where(tile == 1, middle, jnp.where(tile == 2, low, 0.0))).astype(jnp.bfloat16)
    for to in range(z_ref.shape[0]):
        for j in range(own):
            z_ref[to, j * cut:(j + 1) * cut] = mine[j, :cut]
        z_ref[to, own * cut:] = tile
    for to in range(plane_ref.shape[0]):
        plane_ref[to] = mine[:, cut:]


def series_call(sizes, cut, layout, late, early, start, energy):
    nz, plane, _ = layout
    n_orb = sizes[0]
    own, half_rows, nocc = start[0].shape
    return pl.pallas_call(
        functools.partial(series_kernel, sizes),
        out_shape=[
            pltpu.VMEM((plane, own, half_rows - cut, nocc), jnp.bfloat16),
            pltpu.VMEM((nz, own * cut + CHUNK, nocc), jnp.bfloat16),
        ],
        scratch_shapes=[
            pltpu.VMEM((ROWBLK, own, BLOCK, 2 * LANES), jnp.bfloat16),
            pltpu.VMEM((n_orb, own, half_rows, nocc), jnp.bfloat16),
            pltpu.VMEM((n_orb, own, half_rows, nocc), jnp.bfloat16),
        ],
        compiler_params=params(16),
        name="series",
    )(*in_vmem(*late, *early, *start, energy))


def place_kernel(layout, z_first, plane_first, out, energy_ref):
    nz, plane, own = layout
    cut = out.shape[1] - plane_first.shape[3]
    energy = jnp.zeros((CHUNK, LANES), jnp.float32)
    for p in range(plane):
        for z in range(nz):
            for j in range(own):
                w = (z * plane + p) * own + j
                out[w, :cut] = z_first[p, z, j * cut:(j + 1) * cut]
                out[w, cut:] = plane_first[z, p, j]
            energy = energy + z_first[p, z, own * cut:].astype(jnp.float32)
    energy_ref[...] = (energy[0:1] + energy[1:2] + energy[2:3])[:, :energy_ref.shape[1]]


def place_call(layout, z_first, plane_first):
    nz, plane, own = layout
    rest, nocc = plane_first.shape[3:]
    walk = nz * plane * own
    cut = (z_first.shape[2] - CHUNK) // own
    return pl.pallas_call(
        functools.partial(place_kernel, layout),
        out_shape=[
            jax.ShapeDtypeStruct((walk, cut + rest, nocc), jnp.bfloat16),
            jax.ShapeDtypeStruct((1, walk), jnp.float32),
        ],
        compiler_params=params(16),
        name="place_walkers",
    )(*in_vmem(z_first, plane_first))


def per_device(chol_vals, chol_cols, greens, walkers, fields):
    vectors, rowblocks = chol_vals.shape[:2]
    walk, half_rows = greens.shape[:2]
    chips = lax.axis_size("chol")
    n_orb = lax.axis_size("orb")
    plane = 4 if chips % 4 == 0 else 1
    nz = chips // plane
    own = walk // chips
    layout = (nz, plane, own)
    step_factor = 72.0 / float(vectors * chips * BLOCK) ** 0.5

    plane_groups = [[z * plane + p for p in range(plane)] for z in range(nz)]
    z_groups = [[z * plane + p for z in range(nz)] for p in range(plane)]

    def swap(a, groups):
        return lax.all_to_all(a, "chol", 0, 0, axis_index_groups=groups, tiled=True)

    def around_orb(a):
        return [a] + [lax.ppermute(a, "orb", [((c + d) % n_orb, c) for c in range(n_orb)]) for d in range(1, n_orb)]

    cols = jnp.transpose(chol_cols, (1, 2, 0))
    turned, partial_bias, mine = bias_call(chol_vals, greens, walkers, cols, own)
    start = around_orb(mine)
    bias, *others = around_orb(partial_bias)
    start, others = lax.optimization_barrier((start, others))

    total_steps = rowblocks * BLOCK // CHUNK
    early_steps = total_steps * 3 // 8
    late_steps = total_steps - early_steps
    early, late, energy = potential_call(early_steps, layout, fields.T, bias, others, cols, turned)
    early = sum_call(swap(early, z_groups))
    late = sum_call(swap(late, plane_groups))

    def finish(array):
        total = jnp.sum(array.astype(jnp.float32), axis=0)
        return around_orb((step_factor * total).astype(jnp.bfloat16))

    early = finish(swap(early, plane_groups))
    late = finish(swap(late, z_groups))
    cut = half_rows // CHUNK * 5 // 8 * CHUNK
    b_part, a_part = series_call((n_orb, late_steps, early_steps), cut, layout, late, early, start, energy)

    a_all = swap(a_part, z_groups)
    b_all = swap(b_part, plane_groups)
    z_first = swap(jnp.broadcast_to(a_all[None], (plane, *a_all.shape)), plane_groups)
    plane_first = swap(jnp.broadcast_to(b_all[None], (nz, *b_all.shape)), z_groups)
    moved, energy = place_call(layout, z_first, plane_first)
    return moved, energy.reshape(walk)


def solution(mesh):
    in_specs = (
        P("chol", "orb", None, None),
        P("chol", "orb", None),
        P("walker", "orb", None),
        P("walker", "orb", None),
        P("chol", "walker"),
    )
    out_specs = (P("walker", "orb", None), P("walker"))
    return jax.shard_map(
        per_device, mesh=mesh, in_specs=in_specs, out_specs=out_specs, check_vma=False
    )
```

```python
import functools

import jax
import jax.numpy as jnp
from jax import lax
from jax.experimental import pallas as pl
from jax.experimental.pallas import tpu as pltpu
from jax.sharding import PartitionSpec as P

BLOCK = 64
TAYLOR = 4
ROWBLK = 4
LANES = 2 * BLOCK
CHUNK = 16
MIB = 1024 * 1024


FREE = pl.CostEstimate(flops=0, bytes_accessed=0, transcendentals=0)


def params(mib):
    return pltpu.CompilerParams(vmem_limit_bytes=mib * MIB)


def split(value):
    parts = []
    for _ in range(3):
        parts.append(value.astype(jnp.bfloat16))
        value = value - parts[-1].astype(jnp.float32)
    return parts


def in_vmem(*arrays):
    return [pltpu.with_memory_space_constraint(a, pltpu.VMEM) for a in arrays]


def in_hbm(*arrays):
    return [pltpu.with_memory_space_constraint(a, pltpu.HBM) for a in arrays]


def swap_matrix():
    to = lax.broadcasted_iota(jnp.int32, (CHUNK * CHUNK, CHUNK * CHUNK), 0)
    at = lax.broadcasted_iota(jnp.int32, (CHUNK * CHUNK, CHUNK * CHUNK), 1)
    same = (to // CHUNK == at % CHUNK) & (to % CHUNK == at // CHUNK)
    return same.astype(jnp.float32).astype(jnp.bfloat16)


def column_order(row):
    other = 2 - 2 * (row // 2)
    return row, row + 1 - 2 * (row % 2), other, other + 1


def slot_masks(cols, row):
    return [cols == column for column in column_order(row)[1:]]


def bias_kernel(vals_hbm, greens_hbm, walkers_hbm, cols_ref, turned_ref, bias_ref, mine_ref, vals, greens, swap, gs, acc, vsem,
                gsem, wsem):
    total_steps, vectors = turned_ref.shape[:2]
    walk = bias_ref.shape[0]
    steps = BLOCK // CHUNK

    def copies(t):
        rows = pl.ds(lax.rem(t, steps) * CHUNK, CHUNK)
        return (
            pltpu.make_async_copy(vals_hbm.at[:, lax.div(t, steps), rows, :], vals.at[t], vsem.at[t]),
            pltpu.make_async_copy(greens_hbm.at[:, pl.ds(t * CHUNK, CHUNK), :], greens.at[t], gsem.at[t]),
        )

    def begin(t, carry):
        for copy in copies(t):
            copy.start()
        return carry

    own = mine_ref.shape[0]
    lax.fori_loop(0, total_steps, begin, 0)
    take = pltpu.make_async_copy(walkers_hbm.at[pl.ds(lax.axis_index("chol") * own, own)], mine_ref, wsem)
    take.start()
    swap[...] = swap_matrix()
    bias_ref[...] = jnp.zeros_like(bias_ref)
    first = lax.broadcasted_iota(jnp.int32, (CHUNK * CHUNK, LANES), 1) < BLOCK

    def step(t, carry):
        for copy in copies(t):
            copy.wait()
        local = lax.div(t, steps)
        row = lax.axis_index("orb") * cols_ref.shape[0] + local
        upper = row // 2 == 1
        odd = row % 2 == 1
        for w in range(0, walk, CHUNK):
            mixed = greens[t, w:w + CHUNK].reshape(CHUNK * CHUNK, 2 * LANES)
            mixed = jnp.dot(swap[...], mixed, preferred_element_type=jnp.float32)
            pair = jnp.where(upper, mixed[:, LANES:], mixed[:, :LANES])
            rest = jnp.where(upper, mixed[:, :LANES], mixed[:, LANES:])
            pair = jnp.where(odd, pltpu.roll(pair, BLOCK, 1), pair)
            pieces = (
                jnp.where(first, pair, 0.0),
                jnp.where(first, 0.0, pair),
                jnp.where(first, 0.0, pltpu.roll(rest, BLOCK, 1)),
                jnp.where(first, 0.0, rest),
            )
            for k, piece in enumerate(pieces):
                piece = piece.astype(jnp.bfloat16)
                for i in range(CHUNK):
                    gs[k * walk + w:k * walk + w + CHUNK, i * LANES:(i + 1) * LANES] = piece[i * CHUNK:(i + 1) * CHUNK]
        for g in range(0, vectors, 2 * CHUNK):
            both = [vals[t, g + side * CHUNK:g + (side + 1) * CHUNK].reshape(CHUNK * CHUNK, LANES) for side in range(2)]
            both = jnp.dot(swap[...], jnp.concatenate(both, axis=1), preferred_element_type=jnp.float32)
            both = both.astype(jnp.bfloat16)
            for i in range(CHUNK):
                for side in range(2):
                    turned_ref[t, g + side * CHUNK:g + (side + 1) * CHUNK, i * LANES:(i + 1) * LANES] = (
                        both[i * CHUNK:(i + 1) * CHUNK, side * LANES:(side + 1) * LANES]
                    )
        part = lax.dot_general(
            turned_ref[t], gs[...], (((1,), (1,)), ((), ())), preferred_element_type=jnp.float32
        )
        begins = lax.rem(t, steps) == 0
        acc[...] = jnp.where(begins, 0.0, acc[...]) + part

        @pl.when(lax.rem(t, steps) == steps - 1)
        def _():
            flat = acc[...].T
            total = flat[0:walk]
            cols = cols_ref[local, 1:2, :]
            for k, mask in enumerate(slot_masks(cols, row)):
                total = total + jnp.where(mask, flat[(k + 1) * walk:(k + 2) * walk], 0.0)
            bias_ref[...] += total

        return carry

    acc[...] = jnp.zeros_like(acc)
    lax.fori_loop(0, total_steps, step, 0)
    take.wait()


def bias_call(vals, greens, walkers, cols, own):
    vectors, rowblocks = vals.shape[:2]
    walk, half_rows, norb = greens.shape
    steps = half_rows // CHUNK
    wide = CHUNK * LANES
    return pl.pallas_call(
        bias_kernel,
        in_specs=[
            *[pl.BlockSpec(memory_space=pl.ANY)] * 3,
            pl.BlockSpec(memory_space=pltpu.VMEM),
        ],
        out_specs=[pl.BlockSpec(memory_space=pltpu.VMEM)] * 3,
        out_shape=[
            pltpu.VMEM((steps, vectors, wide), jnp.bfloat16),
            pltpu.VMEM((walk, vectors), jnp.float32),
            pltpu.VMEM((own, *walkers.shape[1:]), jnp.bfloat16),
        ],
        scratch_shapes=[
            pltpu.VMEM((steps, vectors, CHUNK, LANES), jnp.bfloat16),
            pltpu.VMEM((steps, walk, CHUNK, norb), jnp.bfloat16),
            pltpu.VMEM((CHUNK * CHUNK, CHUNK * CHUNK), jnp.bfloat16),
            pltpu.VMEM((4 * walk, wide), jnp.bfloat16),
            pltpu.VMEM((vectors, 4 * walk), jnp.float32),
            pltpu.SemaphoreType.DMA((steps,)),
            pltpu.SemaphoreType.DMA((steps,)),
            pltpu.SemaphoreType.DMA,
        ],
        cost_estimate=FREE,
        compiler_params=params(24),
        name="force_bias",
    )(*in_hbm(vals, greens, walkers), cols)


def potential_kernel(start, steps, layout, by_plane, n_after, fields_ref, own_ref, *refs):
    nz, plane, own = layout
    refs = refs[n_after:]
    others = refs[:lax.axis_size("orb") - 1]
    cols_ref, turned_ref = refs[len(others):len(others) + 2]
    groups = plane if by_plane else nz
    outs = refs[len(others) + 2:len(others) + 2 + groups]
    energy_ref, s_ref, swap = refs[len(others) + 2 + groups:]
    walk, vectors = fields_ref.shape
    rowblocks = cols_ref.shape[0]

    me = lax.axis_index("chol")
    bias = own_ref[...]
    for other in others:
        bias = bias + other[...]
    energy = 0.5 * jnp.sum(bias * bias, axis=1, keepdims=True)
    energy_ref[...] = jnp.zeros_like(energy_ref)
    energy_ref[:, :walk] = jnp.broadcast_to(energy, (walk, LANES)).T[:CHUNK]
    shifted = (fields_ref[...] - bias).astype(jnp.bfloat16)
    at = lax.broadcasted_iota(jnp.int32, (walk, walk), 0)
    source = lax.broadcasted_iota(jnp.int32, (walk, walk), 1)
    chip = at // own
    z = (me // plane + chip // plane) % nz
    p = (me % plane) ^ (chip % plane)
    wanted = (z * plane + p) * own + at % own
    pick = (wanted == source).astype(jnp.float32).astype(jnp.bfloat16)
    ordered = jnp.dot(pick, shifted, preferred_element_type=jnp.float32)
    for local in range(rowblocks):
        row = lax.axis_index("orb") * rowblocks + local
        s_ref[local, 0:walk] = ordered.astype(jnp.bfloat16)
        for k, mask in enumerate(slot_masks(cols_ref[local, 1:2, :], row)):
            s_ref[local, (k + 1) * walk:(k + 2) * walk] = jnp.where(mask, ordered, 0.0).astype(jnp.bfloat16)
    swap[...] = swap_matrix()
    first = lax.broadcasted_iota(jnp.int32, (walk, LANES), 1) < BLOCK

    def step(t, carry):
        left = s_ref[lax.div(start + t, BLOCK // CHUNK)]
        tiles = []
        for i in range(0, CHUNK, 2):
            both = jnp.dot(
                left, turned_ref[start + t, :, i * LANES:(i + 2) * LANES], preferred_element_type=jnp.float32
            )
            for side in range(2):
                out = both[:, side * LANES:(side + 1) * LANES]
                near = jnp.where(first, out[0:walk], out[walk:2 * walk])
                far = jnp.where(first, pltpu.roll(out[2 * walk:3 * walk], BLOCK, 1), out[3 * walk:])
                tiles.append(jnp.concatenate([near, far], axis=1).astype(jnp.bfloat16))
        for w0 in range(0, walk, CHUNK):
            mixed = jnp.concatenate([tile[w0:w0 + CHUNK] for tile in tiles], axis=0)
            mixed = jnp.dot(swap[...], mixed, preferred_element_type=jnp.float32).astype(jnp.bfloat16)
            for w in range(CHUNK):
                chip, j = (w0 + w) // own, (w0 + w) % own
                group, inner = (chip % plane, chip // plane) if by_plane else (chip // plane, chip % plane)
                for half in range(2):
                    rows = pl.ds(pl.multiple_of((2 * t + half) * CHUNK, CHUNK), CHUNK)
                    outs[group][inner, j, rows, :] = (
                        mixed[w * CHUNK:(w + 1) * CHUNK, half * LANES:(half + 1) * LANES]
                    )
        return carry

    lax.fori_loop(0, steps, step, 0)


def potential_call(start, steps, layout, by_plane, fields, bias, others, cols, turned, after=()):
    nz, plane, own = layout
    walk, vectors = fields.shape
    groups, inner = (plane, nz) if by_plane else (nz, plane)
    rows = 2 * CHUNK
    *parts, energy = pl.pallas_call(
        functools.partial(potential_kernel, start, steps, layout, by_plane, len(after)),
        out_shape=[
            *[pltpu.VMEM((inner, own, steps * rows, LANES), jnp.bfloat16)] * groups,
            pltpu.VMEM((CHUNK, LANES), jnp.float32),
        ],
        scratch_shapes=[
            pltpu.VMEM((cols.shape[0], 4 * walk, vectors), jnp.bfloat16),
            pltpu.VMEM((CHUNK * CHUNK, CHUNK * CHUNK), jnp.bfloat16),
        ],
        cost_estimate=FREE,
        compiler_params=params(16),
        name="potential",
    )(fields, *in_vmem(bias, *after, *others), cols, *in_vmem(turned))
    return parts, energy


def sum_kernel(count, *refs):
    ins, outs = refs[:count], refs[count:]
    for k, out in enumerate(outs):
        total = ins[0][k].astype(jnp.float32)
        for ref in ins[1:]:
            total = total + ref[k].astype(jnp.float32)
        out[...] = total.astype(out.dtype)


def sum_call(arrays):
    pieces = arrays[0].shape[0]
    shape = pltpu.VMEM(arrays[0].shape[1:], jnp.bfloat16)
    return pl.pallas_call(
        functools.partial(sum_kernel, len(arrays)),
        out_shape=[shape] * pieces,
        cost_estimate=FREE,
        compiler_params=params(16),
        name="sum_parts",
    )(*in_vmem(*arrays))


def series_kernel(sizes, *refs):
    n_orb, late_steps, early_steps = sizes
    late, early, start = refs[:n_orb], refs[n_orb:2 * n_orb], refs[2 * n_orb:3 * n_orb]
    energy_ref, plane_ref, z_ref, pot, term, total = refs[3 * n_orb:]
    me = lax.axis_index("orb")
    own, half_rows = start[0].shape[:2]
    rowblocks = half_rows // BLOCK
    per = BLOCK // CHUNK
    for d in range(n_orb):
        at = lax.rem(me + d, n_orb)
        term[pl.ds(at, 1)] = start[d][...][None]
        for t in range(rowblocks * per):
            ref, k = (early[d], t) if t < early_steps else (late[d], t - early_steps)
            for half in range(2):
                rows = slice((2 * k + half) * CHUNK, (2 * k + half + 1) * CHUNK)
                pot[pl.ds(at * rowblocks + t // per, 1), :, (t % per) * CHUNK:(t % per + 1) * CHUNK,
                    half * LANES:(half + 1) * LANES] = ref[:, rows, :][None]
    for j in range(own):
        blocks = [term[r // rowblocks, j, (r % rowblocks) * BLOCK:(r % rowblocks + 1) * BLOCK] for r in range(ROWBLK)]
        sums = [jnp.zeros(blocks[0].shape, jnp.float32)] * ROWBLK
        begin = blocks
        for degree in range(1, TAYLOR + 1):
            after = []
            for r in range(ROWBLK):
                right = jnp.concatenate([blocks[c] for c in column_order(r)], axis=0)
                product = jnp.dot(pot[r, j], right, preferred_element_type=jnp.float32)
                after.append((product / degree).astype(jnp.bfloat16))
            blocks = after
            sums = [s + b.astype(jnp.float32) for s, b in zip(sums, blocks)]
        for r in range(ROWBLK):
            moved = begin[r].astype(jnp.float32) + sums[r]
            total[r // rowblocks, j, (r % rowblocks) * BLOCK:(r % rowblocks + 1) * BLOCK] = moved.astype(jnp.bfloat16)
    mine = total[pl.ds(me, 1)][0]
    cut = (z_ref.shape[0] - CHUNK) // own
    at = lax.broadcasted_iota(jnp.int32, (CHUNK, LANES), 0)
    high, middle, low = (part.astype(jnp.float32) for part in split(energy_ref[...]))
    tile = jnp.where(at == 0, high, jnp.where(at == 1, middle, jnp.where(at == 2, low, 0.0)))
    for j in range(own):
        z_ref[j * cut:(j + 1) * cut] = mine[j, :cut]
    z_ref[own * cut:] = tile.astype(jnp.bfloat16)
    plane_ref[...] = mine[:, cut:]


def series_call(sizes, cut, late, early, start, energy):
    n_orb = sizes[0]
    own, half_rows, nocc = start[0].shape
    return pl.pallas_call(
        functools.partial(series_kernel, sizes),
        out_shape=[
            pltpu.VMEM((own, half_rows - cut, nocc), jnp.bfloat16),
            pltpu.VMEM((own * cut + CHUNK, nocc), jnp.bfloat16),
        ],
        scratch_shapes=[
            pltpu.VMEM((ROWBLK, own, BLOCK, 2 * LANES), jnp.bfloat16),
            pltpu.VMEM((n_orb, own, half_rows, nocc), jnp.bfloat16),
            pltpu.VMEM((n_orb, own, half_rows, nocc), jnp.bfloat16),
        ],
        cost_estimate=FREE,
        compiler_params=params(16),
        name="series",
    )(*in_vmem(*late, *early, *start, energy))


def place_kernel(layout, *refs):
    nz, plane, own = layout
    z_first, plane_first = refs[:plane], refs[plane:plane + nz]
    out, energy_ref = refs[plane + nz:]
    me = lax.axis_index("chol")
    cut = out.shape[1] - plane_first[0].shape[2]
    energy = jnp.zeros((CHUNK, LANES), jnp.float32)
    for dp in range(plane):
        for dz in range(nz):
            chip = lax.rem(me // plane + nz - dz, nz) * plane + (lax.rem(me, plane) ^ dp)
            for j in range(own):
                out[chip * own + j, :cut] = z_first[dp][dz, j * cut:(j + 1) * cut]
                out[chip * own + j, cut:] = plane_first[dz][dp, j]
            energy = energy + z_first[dp][dz, own * cut:].astype(jnp.float32)
    energy_ref[...] = (energy[0:1] + energy[1:2] + energy[2:3])[:, :energy_ref.shape[1]]


def place_call(layout, z_first, plane_first):
    nz, plane, own = layout
    rest, nocc = plane_first[0].shape[2:]
    walk = nz * plane * own
    cut = (z_first[0].shape[1] - CHUNK) // own
    return pl.pallas_call(
        functools.partial(place_kernel, layout),
        out_shape=[
            jax.ShapeDtypeStruct((walk, cut + rest, nocc), jnp.bfloat16),
            jax.ShapeDtypeStruct((1, walk), jnp.float32),
        ],
        cost_estimate=FREE,
        compiler_params=params(16),
        name="place_walkers",
    )(*in_vmem(*z_first, *plane_first))


def per_device(chol_vals, chol_cols, greens, walkers, fields):
    vectors, rowblocks = chol_vals.shape[:2]
    walk, half_rows = greens.shape[:2]
    chips = lax.axis_size("chol")
    n_orb = lax.axis_size("orb")
    plane = 4 if chips % 4 == 0 else 1
    nz = chips // plane
    own = walk // chips
    layout = (nz, plane, own)
    step_factor = 72.0 / float(vectors * chips * BLOCK) ** 0.5

    def to_plane(a, dp):
        return lax.ppermute(a, "chol", [(c, (c // plane) * plane + ((c % plane) ^ dp)) for c in range(chips)])

    def to_z(a, dz):
        return lax.ppermute(a, "chol", [(c, ((c // plane + dz) % nz) * plane + c % plane) for c in range(chips)])

    def around_orb(a):
        return [a] + [lax.ppermute(a, "orb", [((c + d) % n_orb, c) for c in range(n_orb)]) for d in range(1, n_orb)]

    cols = jnp.transpose(chol_cols, (1, 2, 0))
    turned, partial_bias, mine = bias_call(chol_vals, greens, walkers, cols, own)
    start = around_orb(mine)
    bias, *others = around_orb(partial_bias)
    start, others = lax.optimization_barrier((start, others))

    total_steps = rowblocks * BLOCK // CHUNK
    early_steps = total_steps * 3 // 8
    late_steps = total_steps - early_steps
    fields_t = fields.T
    early, energy = potential_call(0, early_steps, layout, False, fields_t, bias, others, cols, turned)
    early_in = [early[0]] + [to_z(early[dz], dz) for dz in range(1, nz)]
    late, _ = potential_call(early_steps, late_steps, layout, True, fields_t, bias, others, cols, turned, [energy])
    late_in = [late[0]] + [to_plane(late[dp], dp) for dp in range(1, plane)]
    early_sums = sum_call(early_in)
    early_in = [early_sums[0]] + [to_plane(early_sums[dp], dp) for dp in range(1, plane)]
    late_sums = sum_call(late_in)
    late_in = [late_sums[0]] + [to_z(late_sums[dz], dz) for dz in range(1, nz)]


    def finish(arrays):
        total = arrays[0].astype(jnp.float32)
        for a in arrays[1:]:
            total = total + a.astype(jnp.float32)
        return around_orb((step_factor * total).astype(jnp.bfloat16))

    cut = half_rows // CHUNK * 5 // 8 * CHUNK
    b_part, a_part = series_call((n_orb, late_steps, early_steps), cut, finish(late_in), finish(early_in), start, energy)

    a_all = jnp.stack([a_part] + [to_z(a_part, dz) for dz in range(1, nz)])
    b_all = jnp.stack([b_part] + [to_plane(b_part, dp) for dp in range(1, plane)])
    z_first = [a_all] + [to_plane(a_all, dp) for dp in range(1, plane)]
    plane_first = [b_all] + [to_z(b_all, dz) for dz in range(1, nz)]
    moved, energy = place_call(layout, z_first, plane_first)
    return moved, energy.reshape(walk)


def solution(mesh):
    in_specs = (
        P("chol", "orb", None, None),
        P("chol", "orb", None),
        P("walker", "orb", None),
        P("walker", "orb", None),
        P("chol", "walker"),
    )
    out_specs = (P("walker", "orb", None), P("walker"))
    return jax.shard_map(
        per_device, mesh=mesh, in_specs=in_specs, out_specs=out_specs, check_vma=False
    )
```

```python
import functools

import jax
import jax.numpy as jnp
from jax import lax
from jax.experimental import pallas as pl
from jax.experimental.pallas import tpu as pltpu
from jax.sharding import PartitionSpec as P

BLOCK = 64
TAYLOR = 4
ROWBLK = 4
LANES = 2 * BLOCK
CHUNK = 16
MIB = 1024 * 1024


FREE = pl.CostEstimate(flops=0, bytes_accessed=0, transcendentals=0)


def params(mib):
    return pltpu.CompilerParams(vmem_limit_bytes=mib * MIB)


def split(value):
    parts = []
    for _ in range(3):
        parts.append(value.astype(jnp.bfloat16))
        value = value - parts[-1].astype(jnp.float32)
    return parts


def in_vmem(*arrays):
    return [pltpu.with_memory_space_constraint(a, pltpu.VMEM) for a in arrays]


def in_hbm(*arrays):
    return [pltpu.with_memory_space_constraint(a, pltpu.HBM) for a in arrays]


def hop(at, distance, count):
    return at ^ distance if count & (count - 1) == 0 else (at + distance) % count


def swap_matrix():
    to = lax.broadcasted_iota(jnp.int32, (CHUNK * CHUNK, CHUNK * CHUNK), 0)
    at = lax.broadcasted_iota(jnp.int32, (CHUNK * CHUNK, CHUNK * CHUNK), 1)
    same = (to // CHUNK == at % CHUNK) & (to % CHUNK == at // CHUNK)
    return same.astype(jnp.float32).astype(jnp.bfloat16)


def column_order(row):
    other = 2 - 2 * (row // 2)
    return row, row + 1 - 2 * (row % 2), other, other + 1


def slot_masks(cols, row):
    return [cols == column for column in column_order(row)[1:]]


def bias_kernel(vals_hbm, greens_hbm, walkers_hbm, cols_ref, turned_ref, bias_ref, mine_ref, vals, greens, swap, gs, acc, vsem,
                gsem, wsem):
    total_steps, vectors = turned_ref.shape[:2]
    walk = bias_ref.shape[0]
    steps = BLOCK // CHUNK

    def copies(t):
        rows = pl.ds(lax.rem(t, steps) * CHUNK, CHUNK)
        return (
            pltpu.make_async_copy(vals_hbm.at[:, lax.div(t, steps), rows, :], vals.at[t], vsem.at[t]),
            pltpu.make_async_copy(greens_hbm.at[:, pl.ds(t * CHUNK, CHUNK), :], greens.at[t], gsem.at[t]),
        )

    def begin(t, carry):
        for copy in copies(t):
            copy.start()
        return carry

    own = mine_ref.shape[0]
    lax.fori_loop(0, total_steps, begin, 0)
    take = pltpu.make_async_copy(walkers_hbm.at[pl.ds(lax.axis_index("chol") * own, own)], mine_ref, wsem)
    take.start()
    swap[...] = swap_matrix()
    bias_ref[...] = jnp.zeros_like(bias_ref)
    first = lax.broadcasted_iota(jnp.int32, (CHUNK * CHUNK, LANES), 1) < BLOCK

    def step(t, carry):
        for copy in copies(t):
            copy.wait()
        local = lax.div(t, steps)
        row = lax.axis_index("orb") * cols_ref.shape[0] + local
        upper = row // 2 == 1
        odd = row % 2 == 1
        for w in range(0, walk, CHUNK):
            mixed = greens[t, w:w + CHUNK].reshape(CHUNK * CHUNK, 2 * LANES)
            mixed = jnp.dot(swap[...], mixed, preferred_element_type=jnp.float32)
            pair = jnp.where(upper, mixed[:, LANES:], mixed[:, :LANES])
            rest = jnp.where(upper, mixed[:, :LANES], mixed[:, LANES:])
            pair = jnp.where(odd, pltpu.roll(pair, BLOCK, 1), pair)
            pieces = (
                jnp.where(first, pair, 0.0),
                jnp.where(first, 0.0, pair),
                jnp.where(first, 0.0, pltpu.roll(rest, BLOCK, 1)),
                jnp.where(first, 0.0, rest),
            )
            for k, piece in enumerate(pieces):
                piece = piece.astype(jnp.bfloat16)
                for i in range(CHUNK):
                    gs[k * walk + w:k * walk + w + CHUNK, i * LANES:(i + 1) * LANES] = piece[i * CHUNK:(i + 1) * CHUNK]
        for g in range(0, vectors, 2 * CHUNK):
            both = [vals[t, g + side * CHUNK:g + (side + 1) * CHUNK].reshape(CHUNK * CHUNK, LANES) for side in range(2)]
            both = jnp.dot(swap[...], jnp.concatenate(both, axis=1), preferred_element_type=jnp.float32)
            both = both.astype(jnp.bfloat16)
            for i in range(CHUNK):
                for side in range(2):
                    turned_ref[t, g + side * CHUNK:g + (side + 1) * CHUNK, i * LANES:(i + 1) * LANES] = (
                        both[i * CHUNK:(i + 1) * CHUNK, side * LANES:(side + 1) * LANES]
                    )
        part = lax.dot_general(
            turned_ref[t], gs[...], (((1,), (1,)), ((), ())), preferred_element_type=jnp.float32
        )
        begins = lax.rem(t, steps) == 0
        acc[...] = jnp.where(begins, 0.0, acc[...]) + part

        @pl.when(lax.rem(t, steps) == steps - 1)
        def _():
            flat = acc[...].T
            total = flat[0:walk]
            cols = cols_ref[local, 1:2, :]
            for k, mask in enumerate(slot_masks(cols, row)):
                total = total + jnp.where(mask, flat[(k + 1) * walk:(k + 2) * walk], 0.0)
            bias_ref[...] += total

        return carry

    acc[...] = jnp.zeros_like(acc)
    lax.fori_loop(0, total_steps, step, 0)
    take.wait()


def bias_call(vals, greens, walkers, cols, own):
    vectors, rowblocks = vals.shape[:2]
    walk, half_rows, norb = greens.shape
    steps = half_rows // CHUNK
    wide = CHUNK * LANES
    return pl.pallas_call(
        bias_kernel,
        in_specs=[
            *[pl.BlockSpec(memory_space=pl.ANY)] * 3,
            pl.BlockSpec(memory_space=pltpu.VMEM),
        ],
        out_specs=[pl.BlockSpec(memory_space=pltpu.VMEM)] * 3,
        out_shape=[
            pltpu.VMEM((steps, vectors, wide), jnp.bfloat16),
            pltpu.VMEM((walk, vectors), jnp.float32),
            pltpu.VMEM((own, *walkers.shape[1:]), jnp.bfloat16),
        ],
        scratch_shapes=[
            pltpu.VMEM((steps, vectors, CHUNK, LANES), jnp.bfloat16),
            pltpu.VMEM((steps, walk, CHUNK, norb), jnp.bfloat16),
            pltpu.VMEM((CHUNK * CHUNK, CHUNK * CHUNK), jnp.bfloat16),
            pltpu.VMEM((4 * walk, wide), jnp.bfloat16),
            pltpu.VMEM((vectors, 4 * walk), jnp.float32),
            pltpu.SemaphoreType.DMA((steps,)),
            pltpu.SemaphoreType.DMA((steps,)),
            pltpu.SemaphoreType.DMA,
        ],
        cost_estimate=FREE,
        compiler_params=params(24),
        name="force_bias",
    )(*in_hbm(vals, greens, walkers), cols)


def potential_kernel(start, steps, layout, by_plane, fields_ref, own_ref, *refs):
    nz, plane, own = layout
    others = refs[:lax.axis_size("orb") - 1]
    cols_ref, turned_ref = refs[len(others):len(others) + 2]
    groups = plane if by_plane else nz
    outs = refs[len(others) + 2:len(others) + 2 + groups]
    energy_ref, s_ref, swap = refs[len(others) + 2 + groups:]
    walk, vectors = fields_ref.shape
    rowblocks = cols_ref.shape[0]

    me = lax.axis_index("chol")
    bias = own_ref[...]
    for other in others:
        bias = bias + other[...]
    energy = 0.5 * jnp.sum(bias * bias, axis=1, keepdims=True)
    energy_ref[...] = jnp.zeros_like(energy_ref)
    energy_ref[:, :walk] = jnp.broadcast_to(energy, (walk, LANES)).T[:CHUNK]
    shifted = (fields_ref[...] - bias).astype(jnp.bfloat16)
    at = lax.broadcasted_iota(jnp.int32, (walk, walk), 0)
    source = lax.broadcasted_iota(jnp.int32, (walk, walk), 1)
    chip = at // own
    z = hop(me // plane, chip // plane, nz)
    p = hop(me % plane, chip % plane, plane)
    wanted = (z * plane + p) * own + at % own
    pick = (wanted == source).astype(jnp.float32).astype(jnp.bfloat16)
    ordered = jnp.dot(pick, shifted, preferred_element_type=jnp.float32)
    for local in range(rowblocks):
        row = lax.axis_index("orb") * rowblocks + local
        s_ref[local, 0:walk] = ordered.astype(jnp.bfloat16)
        for k, mask in enumerate(slot_masks(cols_ref[local, 1:2, :], row)):
            s_ref[local, (k + 1) * walk:(k + 2) * walk] = jnp.where(mask, ordered, 0.0).astype(jnp.bfloat16)
    swap[...] = swap_matrix()
    first = lax.broadcasted_iota(jnp.int32, (walk, LANES), 1) < BLOCK

    def step(t, carry):
        left = s_ref[lax.div(start + t, BLOCK // CHUNK)]
        tiles = []
        for i in range(0, CHUNK, 2):
            both = jnp.dot(
                left, turned_ref[start + t, :, i * LANES:(i + 2) * LANES], preferred_element_type=jnp.float32
            )
            for side in range(2):
                out = both[:, side * LANES:(side + 1) * LANES]
                near = jnp.where(first, out[0:walk], out[walk:2 * walk])
                far = jnp.where(first, pltpu.roll(out[2 * walk:3 * walk], BLOCK, 1), out[3 * walk:])
                tiles.append(jnp.concatenate([near, far], axis=1).astype(jnp.bfloat16))
        for w0 in range(0, walk, CHUNK):
            mixed = jnp.concatenate([tile[w0:w0 + CHUNK] for tile in tiles], axis=0)
            mixed = jnp.dot(swap[...], mixed, preferred_element_type=jnp.float32).astype(jnp.bfloat16)
            for w in range(CHUNK):
                chip, j = (w0 + w) // own, (w0 + w) % own
                group, inner = (chip % plane, chip // plane) if by_plane else (chip // plane, chip % plane)
                for half in range(2):
                    rows = pl.ds(pl.multiple_of((2 * t + half) * CHUNK, CHUNK), CHUNK)
                    outs[group][inner, j, rows, :] = (
                        mixed[w * CHUNK:(w + 1) * CHUNK, half * LANES:(half + 1) * LANES]
                    )
        return carry

    lax.fori_loop(0, steps, step, 0)


def potential_call(start, steps, layout, by_plane, fields, bias, others, cols, turned):
    nz, plane, own = layout
    walk, vectors = fields.shape
    groups, inner = (plane, nz) if by_plane else (nz, plane)
    rows = 2 * CHUNK
    *parts, energy = pl.pallas_call(
        functools.partial(potential_kernel, start, steps, layout, by_plane),
        out_shape=[
            *[pltpu.VMEM((inner, own, steps * rows, LANES), jnp.bfloat16)] * groups,
            pltpu.VMEM((CHUNK, LANES), jnp.float32),
        ],
        scratch_shapes=[
            pltpu.VMEM((cols.shape[0], 4 * walk, vectors), jnp.bfloat16),
            pltpu.VMEM((CHUNK * CHUNK, CHUNK * CHUNK), jnp.bfloat16),
        ],
        cost_estimate=FREE,
        compiler_params=params(16),
        name="potential",
    )(fields, *in_vmem(bias, *others), cols, *in_vmem(turned))
    return parts, energy


def sum_kernel(count, *refs):
    ins, outs = refs[:count], refs[count:]
    for k, out in enumerate(outs):
        total = ins[0][k].astype(jnp.float32)
        for ref in ins[1:]:
            total = total + ref[k].astype(jnp.float32)
        out[...] = total.astype(out.dtype)


def sum_call(arrays):
    pieces = arrays[0].shape[0]
    shape = pltpu.VMEM(arrays[0].shape[1:], jnp.bfloat16)
    return pl.pallas_call(
        functools.partial(sum_kernel, len(arrays)),
        out_shape=[shape] * pieces,
        cost_estimate=FREE,
        compiler_params=params(16),
        name="sum_parts",
    )(*in_vmem(*arrays))


def series_kernel(sizes, *refs):
    n_orb, late_steps, early_steps = sizes
    late, early, start = refs[:n_orb], refs[n_orb:2 * n_orb], refs[2 * n_orb:3 * n_orb]
    energy_ref, moved_ref, pot, term, total = refs[3 * n_orb:]
    me = lax.axis_index("orb")
    own, half_rows = start[0].shape[:2]
    rowblocks = half_rows // BLOCK
    per = BLOCK // CHUNK
    for d in range(n_orb):
        at = lax.rem(me + d, n_orb)
        term[pl.ds(at, 1)] = start[d][...][None]
        for t in range(rowblocks * per):
            ref, k = (early[d], t) if t < early_steps else (late[d], t - early_steps)
            for half in range(2):
                rows = slice((2 * k + half) * CHUNK, (2 * k + half + 1) * CHUNK)
                pot[pl.ds(at * rowblocks + t // per, 1), :, (t % per) * CHUNK:(t % per + 1) * CHUNK,
                    half * LANES:(half + 1) * LANES] = ref[:, rows, :][None]
    for j in range(own):
        blocks = [term[r // rowblocks, j, (r % rowblocks) * BLOCK:(r % rowblocks + 1) * BLOCK] for r in range(ROWBLK)]
        sums = [jnp.zeros(blocks[0].shape, jnp.float32)] * ROWBLK
        begin = blocks
        for degree in range(1, TAYLOR + 1):
            after = []
            for r in range(ROWBLK):
                right = jnp.concatenate([blocks[c] for c in column_order(r)], axis=0)
                product = jnp.dot(pot[r, j], right, preferred_element_type=jnp.float32)
                after.append((product / degree).astype(jnp.bfloat16))
            blocks = after
            sums = [s + b.astype(jnp.float32) for s, b in zip(sums, blocks)]
        for r in range(ROWBLK):
            moved = begin[r].astype(jnp.float32) + sums[r]
            total[r // rowblocks, j, (r % rowblocks) * BLOCK:(r % rowblocks + 1) * BLOCK] = moved.astype(jnp.bfloat16)
    mine = total[pl.ds(me, 1)][0]
    at = lax.broadcasted_iota(jnp.int32, (CHUNK, LANES), 0)
    high, middle, low = (part.astype(jnp.float32) for part in split(energy_ref[...]))
    tile = jnp.where(at == 0, high, jnp.where(at == 1, middle, jnp.where(at == 2, low, 0.0)))
    moved_ref[:own * half_rows] = mine.reshape(own * half_rows, mine.shape[2])
    moved_ref[own * half_rows:] = tile.astype(jnp.bfloat16)


def series_call(sizes, late, early, start, energy):
    n_orb = sizes[0]
    own, half_rows, nocc = start[0].shape
    return pl.pallas_call(
        functools.partial(series_kernel, sizes),
        out_shape=pltpu.VMEM((own * half_rows + CHUNK, nocc), jnp.bfloat16),
        scratch_shapes=[
            pltpu.VMEM((ROWBLK, own, BLOCK, 2 * LANES), jnp.bfloat16),
            pltpu.VMEM((n_orb, own, half_rows, nocc), jnp.bfloat16),
            pltpu.VMEM((n_orb, own, half_rows, nocc), jnp.bfloat16),
        ],
        cost_estimate=FREE,
        compiler_params=params(16),
        name="series",
    )(*in_vmem(*late, *early, *start, energy))


def place_kernel(layout, *refs):
    nz, plane, own = layout
    gathered = refs[:plane]
    out, energy_ref = refs[plane:]
    me = lax.axis_index("chol")
    rows = out.shape[1]
    energy = jnp.zeros((CHUNK, LANES), jnp.float32)
    for dp in range(plane):
        for dz in range(nz):
            z = hop(lax.div(me, plane), -dz if nz & (nz - 1) else dz, nz)
            p = hop(lax.rem(me, plane), -dp if plane & (plane - 1) else dp, plane)
            for j in range(own):
                out[(z * plane + p) * own + j] = gathered[dp][dz, j * rows:(j + 1) * rows]
            energy = energy + gathered[dp][dz, own * rows:].astype(jnp.float32)
    energy_ref[...] = (energy[0:1] + energy[1:2] + energy[2:3])[:, :energy_ref.shape[1]]


def place_call(layout, gathered):
    nz, plane, own = layout
    walk = nz * plane * own
    rows = (gathered[0].shape[1] - CHUNK) // own
    return pl.pallas_call(
        functools.partial(place_kernel, layout),
        out_shape=[
            jax.ShapeDtypeStruct((walk, rows, gathered[0].shape[2]), jnp.bfloat16),
            jax.ShapeDtypeStruct((1, walk), jnp.float32),
        ],
        cost_estimate=FREE,
        compiler_params=params(16),
        name="place_walkers",
    )(*in_vmem(*gathered))


def per_device(chol_vals, chol_cols, greens, walkers, fields):
    vectors, rowblocks = chol_vals.shape[:2]
    walk, half_rows = greens.shape[:2]
    chips = lax.axis_size("chol")
    n_orb = lax.axis_size("orb")
    plane = 4 if chips % 4 == 0 else 1
    nz = chips // plane
    own = walk // chips
    layout = (nz, plane, own)
    step_factor = 72.0 / float(vectors * chips * BLOCK) ** 0.5

    def to_plane(a, dp):
        return lax.ppermute(a, "chol", [(c, (c // plane) * plane + hop(c % plane, dp, plane)) for c in range(chips)])

    def to_z(a, dz):
        return lax.ppermute(a, "chol", [(c, hop(c // plane, dz, nz) * plane + c % plane) for c in range(chips)])

    def around_orb(a):
        return [a] + [lax.ppermute(a, "orb", [((c + d) % n_orb, c) for c in range(n_orb)]) for d in range(1, n_orb)]

    cols = jnp.transpose(chol_cols, (1, 2, 0))
    turned, partial_bias, mine = bias_call(chol_vals, greens, walkers, cols, own)
    start = around_orb(mine)
    bias, *others = around_orb(partial_bias)
    start, others = lax.optimization_barrier((start, others))

    total_steps = rowblocks * BLOCK // CHUNK
    early_steps = total_steps // 4
    late_steps = total_steps - early_steps
    fields_t = fields.T
    early, energy = potential_call(0, early_steps, layout, False, fields_t, bias, others, cols, turned)
    early_in = [early[0]] + [to_z(early[dz], dz) for dz in range(1, nz)]
    late, _ = potential_call(early_steps, late_steps, layout, True, fields_t, bias, others, cols, turned)
    late_in = [late[0]] + [to_plane(late[dp], dp) for dp in range(1, plane)]
    early_sums = sum_call(early_in)
    early_in = [early_sums[0]] + [to_plane(early_sums[dp], dp) for dp in range(1, plane)]
    late_sums = sum_call(late_in)
    late_in = [late_sums[0]] + [to_z(late_sums[dz], dz) for dz in range(1, nz)]


    def finish(arrays):
        total = arrays[0].astype(jnp.float32)
        for a in arrays[1:]:
            total = total + a.astype(jnp.float32)
        return around_orb((step_factor * total).astype(jnp.bfloat16))

    piece = series_call((n_orb, late_steps, early_steps), finish(late_in), finish(early_in), start, energy)
    pieces = jnp.stack([piece] + [to_z(piece, dz) for dz in range(1, nz)])
    gathered = [pieces] + [to_plane(pieces, dp) for dp in range(1, plane)]
    moved, energy = place_call(layout, gathered)
    return moved, energy.reshape(walk)


def solution(mesh):
    in_specs = (
        P("chol", "orb", None, None),
        P("chol", "orb", None),
        P("walker", "orb", None),
        P("walker", "orb", None),
        P("chol", "walker"),
    )
    out_specs = (P("walker", "orb", None), P("walker"))
    return jax.shard_map(
        per_device, mesh=mesh, in_specs=in_specs, out_specs=out_specs, check_vma=False
    )
```

```python
import functools

import jax
import jax.numpy as jnp
from jax import lax
from jax.experimental import pallas as pl
from jax.experimental.pallas import tpu as pltpu
from jax.sharding import PartitionSpec as P

BLOCK = 64
TAYLOR = 4
ROWBLK = 4
LANES = 2 * BLOCK
CHUNK = 16
MIB = 1024 * 1024


FREE = pl.CostEstimate(flops=0, bytes_accessed=0, transcendentals=0)


def params(mib):
    return pltpu.CompilerParams(vmem_limit_bytes=mib * MIB)


def split(value):
    parts = []
    for _ in range(3):
        parts.append(value.astype(jnp.bfloat16))
        value = value - parts[-1].astype(jnp.float32)
    return parts


def in_vmem(*arrays):
    return [pltpu.with_memory_space_constraint(a, pltpu.VMEM) for a in arrays]


def in_hbm(*arrays):
    return [pltpu.with_memory_space_constraint(a, pltpu.HBM) for a in arrays]


def orders(chips, early):
    bits = list(range(chips.bit_length() - 1))
    assert chips == 1 << len(bits)
    if early:
        bits = bits[len(bits) // 2:] + bits[:len(bits) // 2]
    return bits, [bits[k ^ 1] if k ^ 1 < len(bits) else bits[k] for k in range(len(bits))]


def flips(chips, early, core):
    return [jnp.where(core % 2 == 0, 1 << even, 1 << odd) for even, odd in zip(*orders(chips, early))]


def swap_matrix():
    to = lax.broadcasted_iota(jnp.int32, (CHUNK * CHUNK, CHUNK * CHUNK), 0)
    at = lax.broadcasted_iota(jnp.int32, (CHUNK * CHUNK, CHUNK * CHUNK), 1)
    same = (to // CHUNK == at % CHUNK) & (to % CHUNK == at // CHUNK)
    return same.astype(jnp.float32).astype(jnp.bfloat16)


def column_order(row):
    other = 2 - 2 * (row // 2)
    return row, row + 1 - 2 * (row % 2), other, other + 1


def slot_masks(cols, row):
    return [cols == column for column in column_order(row)[1:]]


def bias_kernel(vals_hbm, greens_hbm, walkers_hbm, cols_ref, turned_ref, bias_ref, mine_ref, vals, greens, swap, gs, acc, vsem,
                gsem, wsem):
    total_steps, vectors = turned_ref.shape[:2]
    walk = bias_ref.shape[0]
    steps = BLOCK // CHUNK

    def copies(t):
        rows = pl.ds(lax.rem(t, steps) * CHUNK, CHUNK)
        return (
            pltpu.make_async_copy(vals_hbm.at[:, lax.div(t, steps), rows, :], vals.at[t], vsem.at[t]),
            pltpu.make_async_copy(greens_hbm.at[:, pl.ds(t * CHUNK, CHUNK), :], greens.at[t], gsem.at[t]),
        )

    def begin(t, carry):
        for copy in copies(t):
            copy.start()
        return carry

    own = mine_ref.shape[0]
    lax.fori_loop(0, total_steps, begin, 0)
    take = pltpu.make_async_copy(walkers_hbm.at[pl.ds(lax.axis_index("chol") * own, own)], mine_ref, wsem)
    take.start()
    swap[...] = swap_matrix()
    bias_ref[...] = jnp.zeros_like(bias_ref)
    first = lax.broadcasted_iota(jnp.int32, (CHUNK * CHUNK, LANES), 1) < BLOCK

    def step(t, carry):
        for copy in copies(t):
            copy.wait()
        local = lax.div(t, steps)
        row = lax.axis_index("orb") * cols_ref.shape[0] + local
        upper = row // 2 == 1
        odd = row % 2 == 1
        for w in range(0, walk, CHUNK):
            mixed = greens[t, w:w + CHUNK].reshape(CHUNK * CHUNK, 2 * LANES)
            mixed = jnp.dot(swap[...], mixed, preferred_element_type=jnp.float32)
            pair = jnp.where(upper, mixed[:, LANES:], mixed[:, :LANES])
            rest = jnp.where(upper, mixed[:, :LANES], mixed[:, LANES:])
            pair = jnp.where(odd, pltpu.roll(pair, BLOCK, 1), pair)
            pieces = (
                jnp.where(first, pair, 0.0),
                jnp.where(first, 0.0, pair),
                jnp.where(first, 0.0, pltpu.roll(rest, BLOCK, 1)),
                jnp.where(first, 0.0, rest),
            )
            for k, piece in enumerate(pieces):
                piece = piece.astype(jnp.bfloat16)
                for i in range(CHUNK):
                    gs[k * walk + w:k * walk + w + CHUNK, i * LANES:(i + 1) * LANES] = piece[i * CHUNK:(i + 1) * CHUNK]
        for g in range(0, vectors, 2 * CHUNK):
            both = [vals[t, g + side * CHUNK:g + (side + 1) * CHUNK].reshape(CHUNK * CHUNK, LANES) for side in range(2)]
            both = jnp.dot(swap[...], jnp.concatenate(both, axis=1), preferred_element_type=jnp.float32)
            both = both.astype(jnp.bfloat16)
            for i in range(CHUNK):
                for side in range(2):
                    turned_ref[t, g + side * CHUNK:g + (side + 1) * CHUNK, i * LANES:(i + 1) * LANES] = (
                        both[i * CHUNK:(i + 1) * CHUNK, side * LANES:(side + 1) * LANES]
                    )
        part = lax.dot_general(
            turned_ref[t], gs[...], (((1,), (1,)), ((), ())), preferred_element_type=jnp.float32
        )
        begins = lax.rem(t, steps) == 0
        acc[...] = jnp.where(begins, 0.0, acc[...]) + part

        @pl.when(lax.rem(t, steps) == steps - 1)
        def _():
            flat = acc[...].T
            total = flat[0:walk]
            cols = cols_ref[local, 1:2, :]
            for k, mask in enumerate(slot_masks(cols, row)):
                total = total + jnp.where(mask, flat[(k + 1) * walk:(k + 2) * walk], 0.0)
            bias_ref[...] += total

        return carry

    acc[...] = jnp.zeros_like(acc)
    lax.fori_loop(0, total_steps, step, 0)
    take.wait()


def bias_call(vals, greens, walkers, cols, own):
    vectors, rowblocks = vals.shape[:2]
    walk, half_rows, norb = greens.shape
    steps = half_rows // CHUNK
    wide = CHUNK * LANES
    return pl.pallas_call(
        bias_kernel,
        in_specs=[
            *[pl.BlockSpec(memory_space=pl.ANY)] * 3,
            pl.BlockSpec(memory_space=pltpu.VMEM),
        ],
        out_specs=[pl.BlockSpec(memory_space=pltpu.VMEM)] * 3,
        out_shape=[
            pltpu.VMEM((steps, vectors, wide), jnp.bfloat16),
            pltpu.VMEM((walk, vectors), jnp.float32),
            pltpu.VMEM((own, *walkers.shape[1:]), jnp.bfloat16),
        ],
        scratch_shapes=[
            pltpu.VMEM((steps, vectors, CHUNK, LANES), jnp.bfloat16),
            pltpu.VMEM((steps, walk, CHUNK, norb), jnp.bfloat16),
            pltpu.VMEM((CHUNK * CHUNK, CHUNK * CHUNK), jnp.bfloat16),
            pltpu.VMEM((4 * walk, wide), jnp.bfloat16),
            pltpu.VMEM((vectors, 4 * walk), jnp.float32),
            pltpu.SemaphoreType.DMA((steps,)),
            pltpu.SemaphoreType.DMA((steps,)),
            pltpu.SemaphoreType.DMA,
        ],
        cost_estimate=FREE,
        compiler_params=params(24),
        name="force_bias",
    )(*in_hbm(vals, greens, walkers), cols)


def potential_kernel(start, steps, chips, early, fields_ref, own_ref, *refs):
    others = refs[:lax.axis_size("orb") - 1]
    cols_ref, turned_ref = refs[len(others):len(others) + 2]
    outs = refs[len(others) + 2:len(others) + 4]
    energy_ref, s_ref, swap = refs[len(others) + 4:]
    walk, vectors = fields_ref.shape
    own = walk // chips
    bits = chips.bit_length() - 1
    rowblocks = cols_ref.shape[0]

    me = lax.axis_index("chol")
    bias = own_ref[...]
    for other in others:
        bias = bias + other[...]
    energy = 0.5 * jnp.sum(bias * bias, axis=1, keepdims=True)
    energy_ref[...] = jnp.zeros_like(energy_ref)
    energy_ref[:, :walk] = jnp.broadcast_to(energy, (walk, LANES)).T[:CHUNK]
    shifted = (fields_ref[...] - bias).astype(jnp.bfloat16)
    at = lax.broadcasted_iota(jnp.int32, (walk, walk), 0)
    source = lax.broadcasted_iota(jnp.int32, (walk, walk), 1)
    chip = at // own
    to = jnp.broadcast_to(me, chip.shape)
    for k, flip in enumerate(flips(chips, early, lax.axis_index("orb"))):
        to = to ^ (((chip >> (bits - 1 - k)) & 1) * flip)
    wanted = to * own + at % own
    pick = (wanted == source).astype(jnp.float32).astype(jnp.bfloat16)
    ordered = jnp.dot(pick, shifted, preferred_element_type=jnp.float32)
    for local in range(rowblocks):
        row = lax.axis_index("orb") * rowblocks + local
        s_ref[local, 0:walk] = ordered.astype(jnp.bfloat16)
        for k, mask in enumerate(slot_masks(cols_ref[local, 1:2, :], row)):
            s_ref[local, (k + 1) * walk:(k + 2) * walk] = jnp.where(mask, ordered, 0.0).astype(jnp.bfloat16)
    swap[...] = swap_matrix()
    lower = lax.broadcasted_iota(jnp.int32, (walk, LANES), 1) < BLOCK

    def step(t, carry):
        left = s_ref[lax.div(start + t, BLOCK // CHUNK)]
        tiles = []
        for i in range(0, CHUNK, 2):
            both = jnp.dot(
                left, turned_ref[start + t, :, i * LANES:(i + 2) * LANES], preferred_element_type=jnp.float32
            )
            for side in range(2):
                out = both[:, side * LANES:(side + 1) * LANES]
                near = jnp.where(lower, out[0:walk], out[walk:2 * walk])
                far = jnp.where(lower, pltpu.roll(out[2 * walk:3 * walk], BLOCK, 1), out[3 * walk:])
                tiles.append(jnp.concatenate([near, far], axis=1).astype(jnp.bfloat16))
        for w0 in range(0, walk, CHUNK):
            mixed = jnp.concatenate([tile[w0:w0 + CHUNK] for tile in tiles], axis=0)
            mixed = jnp.dot(swap[...], mixed, preferred_element_type=jnp.float32).astype(jnp.bfloat16)
            for w in range(CHUNK):
                chip, j = (w0 + w) // own, (w0 + w) % own
                place = [(chip >> (bits - 1 - k)) & 1 for k in range(bits)]
                for half in range(2):
                    rows = pl.ds(pl.multiple_of((2 * t + half) * CHUNK, CHUNK), CHUNK)
                    outs[place[0]][(*place[1:], j, rows)] = (
                        mixed[w * CHUNK:(w + 1) * CHUNK, half * LANES:(half + 1) * LANES]
                    )
        return carry

    lax.fori_loop(0, steps, step, 0)


def potential_call(start, steps, chips, early, fields, bias, others, cols, turned):
    walk, vectors = fields.shape
    inner = (2,) * (chips.bit_length() - 2)
    rows = 2 * CHUNK
    *parts, energy = pl.pallas_call(
        functools.partial(potential_kernel, start, steps, chips, early),
        out_shape=[
            *[pltpu.VMEM((*inner, walk // chips, steps * rows, LANES), jnp.bfloat16)] * 2,
            pltpu.VMEM((CHUNK, LANES), jnp.float32),
        ],
        scratch_shapes=[
            pltpu.VMEM((cols.shape[0], 4 * walk, vectors), jnp.bfloat16),
            pltpu.VMEM((CHUNK * CHUNK, CHUNK * CHUNK), jnp.bfloat16),
        ],
        cost_estimate=FREE,
        compiler_params=params(16),
        name="potential",
    )(fields, *in_vmem(bias, *others), cols, *in_vmem(turned))
    return parts, energy


def sum_kernel(count, skip, *refs):
    ins, outs = refs[:count], refs[count + skip:]
    for k, out in enumerate(outs):
        total = ins[0][k].astype(jnp.float32)
        for ref in ins[1:]:
            total = total + ref[k].astype(jnp.float32)
        out[...] = total.astype(out.dtype)


def sum_call(arrays, after=()):
    pieces = arrays[0].shape[0]
    shape = pltpu.VMEM(arrays[0].shape[1:], jnp.bfloat16)
    return pl.pallas_call(
        functools.partial(sum_kernel, len(arrays), len(after)),
        out_shape=[shape] * pieces,
        cost_estimate=FREE,
        compiler_params=params(16),
        name="sum_parts",
    )(*in_vmem(*arrays, *after))


def series_kernel(sizes, *refs):
    n_orb, late_steps, early_steps = sizes
    late, early, start = refs[:n_orb], refs[n_orb:2 * n_orb], refs[2 * n_orb:3 * n_orb]
    energy_ref, moved_ref, pot, term, total = refs[3 * n_orb:]
    me = lax.axis_index("orb")
    own, half_rows = start[0].shape[:2]
    rowblocks = half_rows // BLOCK
    per = BLOCK // CHUNK
    for d in range(n_orb):
        at = lax.rem(me + d, n_orb)
        term[pl.ds(at, 1)] = start[d][...][None]
        for t in range(rowblocks * per):
            ref, k = (early[d], t) if t < early_steps else (late[d], t - early_steps)
            for half in range(2):
                rows = slice((2 * k + half) * CHUNK, (2 * k + half + 1) * CHUNK)
                pot[pl.ds(at * rowblocks + t // per, 1), :, (t % per) * CHUNK:(t % per + 1) * CHUNK,
                    half * LANES:(half + 1) * LANES] = ref[:, rows, :][None]
    for j in range(own):
        blocks = [term[r // rowblocks, j, (r % rowblocks) * BLOCK:(r % rowblocks + 1) * BLOCK] for r in range(ROWBLK)]
        sums = [jnp.zeros(blocks[0].shape, jnp.float32)] * ROWBLK
        begin = blocks
        for degree in range(1, TAYLOR + 1):
            after = []
            for r in range(ROWBLK):
                right = jnp.concatenate([blocks[c] for c in column_order(r)], axis=0)
                product = jnp.dot(pot[r, j], right, preferred_element_type=jnp.float32)
                after.append((product / degree).astype(jnp.bfloat16))
            blocks = after
            sums = [s + b.astype(jnp.float32) for s, b in zip(sums, blocks)]
        for r in range(ROWBLK):
            moved = begin[r].astype(jnp.float32) + sums[r]
            total[r // rowblocks, j, (r % rowblocks) * BLOCK:(r % rowblocks + 1) * BLOCK] = moved.astype(jnp.bfloat16)
    mine = total[pl.ds(me, 1)][0]
    at = lax.broadcasted_iota(jnp.int32, (CHUNK, LANES), 0)
    high, middle, low = (part.astype(jnp.float32) for part in split(energy_ref[...]))
    tile = jnp.where(at == 0, high, jnp.where(at == 1, middle, jnp.where(at == 2, low, 0.0)))
    moved_ref[:own * half_rows] = mine.reshape(own * half_rows, mine.shape[2])
    moved_ref[own * half_rows:] = tile.astype(jnp.bfloat16)


def series_call(sizes, late, early, start, energy):
    n_orb = sizes[0]
    own, half_rows, nocc = start[0].shape
    return pl.pallas_call(
        functools.partial(series_kernel, sizes),
        out_shape=pltpu.VMEM((own * half_rows + CHUNK, nocc), jnp.bfloat16),
        scratch_shapes=[
            pltpu.VMEM((ROWBLK, own, BLOCK, 2 * LANES), jnp.bfloat16),
            pltpu.VMEM((n_orb, own, half_rows, nocc), jnp.bfloat16),
            pltpu.VMEM((n_orb, own, half_rows, nocc), jnp.bfloat16),
        ],
        cost_estimate=FREE,
        compiler_params=params(16),
        name="series",
    )(*in_vmem(*late, *early, *start, energy))


def place_kernel(chips, mine_ref, theirs_ref, out, energy_ref):
    bits = chips.bit_length() - 1
    own = out.shape[0] // chips
    rows = out.shape[1]
    me = lax.axis_index("chol")
    flip = flips(chips, False, lax.axis_index("orb"))
    energy = jnp.zeros((CHUNK, LANES), jnp.float32)
    for n in range(chips):
        place = [(n >> (bits - 1 - k)) & 1 for k in range(bits)]
        chip = me
        for k in range(bits):
            chip = chip ^ (place[k] * flip[k])
        piece = (theirs_ref if place[0] else mine_ref).at[*place[1:]]
        for j in range(own):
            out[chip * own + j] = piece[j * rows:(j + 1) * rows]
        energy = energy + piece[own * rows:].astype(jnp.float32)
    energy_ref[...] = (energy[0:1] + energy[1:2] + energy[2:3])[:, :energy_ref.shape[1]]


def place_call(chips, own, mine, theirs):
    rows = (mine.shape[-2] - CHUNK) // own
    return pl.pallas_call(
        functools.partial(place_kernel, chips),
        out_shape=[
            jax.ShapeDtypeStruct((chips * own, rows, mine.shape[-1]), jnp.bfloat16),
            jax.ShapeDtypeStruct((1, chips * own), jnp.float32),
        ],
        cost_estimate=FREE,
        compiler_params=params(16),
        name="place_walkers",
    )(*in_vmem(mine, theirs))


def per_device(chol_vals, chol_cols, greens, walkers, fields):
    vectors, rowblocks = chol_vals.shape[:2]
    walk, half_rows = greens.shape[:2]
    chips = lax.axis_size("chol")
    n_orb = lax.axis_size("orb")
    own = walk // chips
    bits = chips.bit_length() - 1
    step_factor = 72.0 / float(vectors * chips * BLOCK) ** 0.5

    def exchange(a, step, early):
        order = orders(chips, early)
        pairs = [(c, c ^ (1 << order[core % 2][step]), core) for c in range(chips) for core in range(n_orb)]
        return lax.ppermute(a, ("chol", "orb"), [(c * n_orb + core, to * n_orb + core) for c, to, core in pairs])

    def around_orb(a):
        return [a] + [lax.ppermute(a, "orb", [((c + d) % n_orb, c) for c in range(n_orb)]) for d in range(1, n_orb)]

    cols = jnp.transpose(chol_cols, (1, 2, 0))
    turned, partial_bias, mine = bias_call(chol_vals, greens, walkers, cols, own)
    start = around_orb(mine)
    bias, *others = around_orb(partial_bias)
    start, others = lax.optimization_barrier((start, others))

    total_steps = rowblocks * BLOCK // CHUNK
    early_steps = total_steps * 3 // 8
    late_steps = total_steps - early_steps
    fields_t = fields.T
    late, energy = potential_call(early_steps, late_steps, chips, False, fields_t, bias, others, cols, turned)
    early, again = potential_call(0, early_steps, chips, True, fields_t, bias, others, cols, turned)
    for step in range(bits - 1):
        late = sum_call([late[0], exchange(late[1], step, False)], after=[again] if step == 0 else [])
    for step in range(bits - 1):
        early = sum_call([early[0], exchange(early[1], step, True)])
    late_in = [late[0], exchange(late[1], bits - 1, False)]
    early_in = [early[0], exchange(early[1], bits - 1, True)]

    def finish(arrays):
        total = arrays[0].astype(jnp.float32)
        for a in arrays[1:]:
            total = total + a.astype(jnp.float32)
        return around_orb((step_factor * total).astype(jnp.bfloat16))

    piece = series_call((n_orb, late_steps, early_steps), finish(late_in), finish(early_in), start, energy)
    for step in reversed(range(1, bits)):
        piece = jnp.stack([piece, exchange(piece, step, False)])
    moved, energy = place_call(chips, own, piece, exchange(piece, 0, False))
    return moved, energy.reshape(walk)


def solution(mesh):
    in_specs = (
        P("chol", "orb", None, None),
        P("chol", "orb", None),
        P("walker", "orb", None),
        P("walker", "orb", None),
        P("chol", "walker"),
    )
    out_specs = (P("walker", "orb", None), P("walker"))
    return jax.shard_map(
        per_device, mesh=mesh, in_specs=in_specs, out_specs=out_specs, check_vma=False
    )
```

```python
import functools

import jax
import jax.numpy as jnp
from jax import lax
from jax.experimental import pallas as pl
from jax.experimental.pallas import tpu as pltpu
from jax.sharding import PartitionSpec as P

BLOCK = 64
TAYLOR = 4
ROWBLK = 4
LANES = 2 * BLOCK
CHUNK = 16
MIB = 1024 * 1024


FREE = pl.CostEstimate(flops=0, bytes_accessed=0, transcendentals=0)


def params(mib):
    return pltpu.CompilerParams(vmem_limit_bytes=mib * MIB)


def split(value):
    parts = []
    for _ in range(3):
        parts.append(value.astype(jnp.bfloat16))
        value = value - parts[-1].astype(jnp.float32)
    return parts


def in_vmem(*arrays):
    return [pltpu.with_memory_space_constraint(a, pltpu.VMEM) for a in arrays]


def in_hbm(*arrays):
    return [pltpu.with_memory_space_constraint(a, pltpu.HBM) for a in arrays]


def hop(at, distance, count):
    return at ^ distance if count & (count - 1) == 0 else (at + distance) % count


def swap_matrix():
    to = lax.broadcasted_iota(jnp.int32, (CHUNK * CHUNK, CHUNK * CHUNK), 0)
    at = lax.broadcasted_iota(jnp.int32, (CHUNK * CHUNK, CHUNK * CHUNK), 1)
    same = (to // CHUNK == at % CHUNK) & (to % CHUNK == at // CHUNK)
    return same.astype(jnp.float32).astype(jnp.bfloat16)


def column_order(row):
    other = 2 - 2 * (row // 2)
    return row, row + 1 - 2 * (row % 2), other, other + 1


def slot_masks(cols, row):
    return [cols == column for column in column_order(row)[1:]]


def bias_kernel(vals_hbm, greens_hbm, walkers_hbm, cols_hbm, turned_ref, bias_ref, mine_ref, cols_ref, vals, greens, swap, gs,
                acc, vsem, gsem, wsem, csem):
    total_steps, vectors = turned_ref.shape[:2]
    walk = bias_ref.shape[0]
    steps = BLOCK // CHUNK

    def copies(t):
        rows = pl.ds(lax.rem(t, steps) * CHUNK, CHUNK)
        return (
            pltpu.make_async_copy(vals_hbm.at[:, lax.div(t, steps), rows, :], vals.at[t], vsem.at[t]),
            pltpu.make_async_copy(greens_hbm.at[:, pl.ds(t * CHUNK, CHUNK), :], greens.at[t], gsem.at[t]),
        )

    def begin(t, carry):
        for copy in copies(t):
            copy.start()
        return carry

    own = mine_ref.shape[0]
    lax.fori_loop(0, total_steps, begin, 0)
    take = pltpu.make_async_copy(walkers_hbm.at[pl.ds(lax.axis_index("chol") * own, own)], mine_ref, wsem)
    take.start()
    take_cols = pltpu.make_async_copy(cols_hbm, cols_ref, csem)
    take_cols.start()
    swap[...] = swap_matrix()
    bias_ref[...] = jnp.zeros_like(bias_ref)
    first = lax.broadcasted_iota(jnp.int32, (CHUNK * CHUNK, LANES), 1) < BLOCK

    def turn(t):
        for copy in copies(t):
            copy.wait()
        slot = lax.rem(t, 2)
        row = lax.axis_index("orb") * cols_ref.shape[0] + lax.div(t, steps)
        upper = row // 2 == 1
        odd = row % 2 == 1
        for w in range(0, walk, CHUNK):
            mixed = greens[t, w:w + CHUNK].reshape(CHUNK * CHUNK, 2 * LANES)
            mixed = jnp.dot(swap[...], mixed, preferred_element_type=jnp.float32)
            pair = jnp.where(upper, mixed[:, LANES:], mixed[:, :LANES])
            rest = jnp.where(upper, mixed[:, :LANES], mixed[:, LANES:])
            pair = jnp.where(odd, pltpu.roll(pair, BLOCK, 1), pair)
            pieces = (
                jnp.where(first, pair, 0.0),
                jnp.where(first, 0.0, pair),
                jnp.where(first, 0.0, pltpu.roll(rest, BLOCK, 1)),
                jnp.where(first, 0.0, rest),
            )
            for k, piece in enumerate(pieces):
                piece = piece.astype(jnp.bfloat16)
                for i in range(CHUNK):
                    gs[slot, k * walk + w:k * walk + w + CHUNK, i * LANES:(i + 1) * LANES] = (
                        piece[i * CHUNK:(i + 1) * CHUNK]
                    )
        for g in range(0, vectors, 2 * CHUNK):
            both = [vals[t, g + side * CHUNK:g + (side + 1) * CHUNK].reshape(CHUNK * CHUNK, LANES) for side in range(2)]
            both = jnp.dot(swap[...], jnp.concatenate(both, axis=1), preferred_element_type=jnp.float32)
            both = both.astype(jnp.bfloat16)
            for i in range(CHUNK):
                for side in range(2):
                    turned_ref[t, g + side * CHUNK:g + (side + 1) * CHUNK, i * LANES:(i + 1) * LANES] = (
                        both[i * CHUNK:(i + 1) * CHUNK, side * LANES:(side + 1) * LANES]
                    )

    def product(t):
        return lax.dot_general(
            turned_ref[t], gs[lax.rem(t, 2)], (((1,), (1,)), ((), ())), preferred_element_type=jnp.float32
        )

    def close(t):
        local = lax.div(t, steps)
        row = lax.axis_index("orb") * cols_ref.shape[0] + local
        flat = acc[...].T
        total = flat[0:walk]
        for k, mask in enumerate(slot_masks(cols_ref[local, 1:2, :], row)):
            total = total + jnp.where(mask, flat[(k + 1) * walk:(k + 2) * walk], 0.0)
        bias_ref[...] += total

    def step(t, carry):
        part = product(t - 1)
        turn(t)
        acc[...] = jnp.where(lax.rem(t - 1, steps) == 0, 0.0, acc[...]) + part

        @pl.when(lax.rem(t, steps) == 0)
        def _():
            close(t - 1)

        return carry

    acc[...] = jnp.zeros_like(acc)
    turn(0)
    take_cols.wait()
    lax.fori_loop(1, total_steps, step, 0)
    acc[...] += product(total_steps - 1)
    close(total_steps - 1)
    take.wait()


def bias_call(vals, greens, walkers, cols, own):
    vectors, rowblocks = vals.shape[:2]
    walk, half_rows, norb = greens.shape
    steps = half_rows // CHUNK
    wide = CHUNK * LANES
    return pl.pallas_call(
        bias_kernel,
        in_specs=[
            *[pl.BlockSpec(memory_space=pl.ANY)] * 4,
        ],
        out_specs=[pl.BlockSpec(memory_space=pltpu.VMEM)] * 4,
        out_shape=[
            pltpu.VMEM((steps, vectors, wide), jnp.bfloat16),
            pltpu.VMEM((walk, vectors), jnp.float32),
            pltpu.VMEM((own, *walkers.shape[1:]), jnp.bfloat16),
            pltpu.VMEM(cols.shape, jnp.int32),
        ],
        scratch_shapes=[
            pltpu.VMEM((steps, vectors, CHUNK, LANES), jnp.bfloat16),
            pltpu.VMEM((steps, walk, CHUNK, norb), jnp.bfloat16),
            pltpu.VMEM((CHUNK * CHUNK, CHUNK * CHUNK), jnp.bfloat16),
            pltpu.VMEM((2, 4 * walk, wide), jnp.bfloat16),
            pltpu.VMEM((vectors, 4 * walk), jnp.float32),
            pltpu.SemaphoreType.DMA((steps,)),
            pltpu.SemaphoreType.DMA((steps,)),
            pltpu.SemaphoreType.DMA,
            pltpu.SemaphoreType.DMA,
        ],
        cost_estimate=FREE,
        compiler_params=params(24),
        name="force_bias",
    )(*in_hbm(vals, greens, walkers, cols))


def potential_kernel(start, steps, layout, by_plane, fields_ref, own_ref, *refs):
    nz, plane, own = layout
    others = refs[:lax.axis_size("orb") - 1]
    cols_ref, turned_ref = refs[len(others):len(others) + 2]
    groups = plane if by_plane else nz
    outs = refs[len(others) + 2:len(others) + 2 + groups]
    energy_ref, s_ref, swap = refs[len(others) + 2 + groups:]
    walk, vectors = fields_ref.shape
    rowblocks = cols_ref.shape[0]

    me = lax.axis_index("chol")
    bias = own_ref[...]
    for other in others:
        bias = bias + other[...]
    energy = 0.5 * jnp.sum(bias * bias, axis=1, keepdims=True)
    energy_ref[...] = jnp.zeros_like(energy_ref)
    energy_ref[:, :walk] = jnp.broadcast_to(energy, (walk, LANES)).T[:CHUNK]
    shifted = (fields_ref[...] - bias).astype(jnp.bfloat16)
    at = lax.broadcasted_iota(jnp.int32, (walk, walk), 0)
    source = lax.broadcasted_iota(jnp.int32, (walk, walk), 1)
    chip = at // own
    z = hop(me // plane, chip // plane, nz)
    p = hop(me % plane, chip % plane, plane)
    wanted = (z * plane + p) * own + at % own
    pick = (wanted == source).astype(jnp.float32).astype(jnp.bfloat16)
    ordered = jnp.dot(pick, shifted, preferred_element_type=jnp.float32)
    for local in range(rowblocks):
        row = lax.axis_index("orb") * rowblocks + local
        s_ref[local, 0:walk] = ordered.astype(jnp.bfloat16)
        for k, mask in enumerate(slot_masks(cols_ref[local, 1:2, :], row)):
            s_ref[local, (k + 1) * walk:(k + 2) * walk] = jnp.where(mask, ordered, 0.0).astype(jnp.bfloat16)
    swap[...] = swap_matrix()
    first = lax.broadcasted_iota(jnp.int32, (walk, LANES), 1) < BLOCK

    def step(t, carry):
        left = s_ref[lax.div(start + t, BLOCK // CHUNK)]
        tiles = []
        for i in range(0, CHUNK, 2):
            both = jnp.dot(
                left, turned_ref[start + t, :, i * LANES:(i + 2) * LANES], preferred_element_type=jnp.float32
            )
            for side in range(2):
                out = both[:, side * LANES:(side + 1) * LANES]
                near = jnp.where(first, out[0:walk], out[walk:2 * walk])
                far = jnp.where(first, pltpu.roll(out[2 * walk:3 * walk], BLOCK, 1), out[3 * walk:])
                tiles.append(jnp.concatenate([near, far], axis=1).astype(jnp.bfloat16))
        for w0 in range(0, walk, CHUNK):
            mixed = jnp.concatenate([tile[w0:w0 + CHUNK] for tile in tiles], axis=0)
            mixed = jnp.dot(swap[...], mixed, preferred_element_type=jnp.float32).astype(jnp.bfloat16)
            for w in range(CHUNK):
                chip, j = (w0 + w) // own, (w0 + w) % own
                dz, dp = chip // plane, chip % plane
                out, inner = (outs[dp], dz) if by_plane else (outs[dz], dp)
                for half in range(2):
                    rows = pl.ds(pl.multiple_of((2 * t + half) * CHUNK, CHUNK), CHUNK)
                    out[inner, j, rows] = mixed[w * CHUNK:(w + 1) * CHUNK, half * LANES:(half + 1) * LANES]
        return carry

    lax.fori_loop(0, steps // 2, lambda t, carry: step(2 * t + 1, step(2 * t, carry)), 0)
    if steps % 2:
        step(steps - 1, 0)


def potential_call(start, steps, layout, by_plane, fields, bias, others, cols, turned):
    nz, plane, own = layout
    walk, vectors = fields.shape
    groups, inner = (plane, nz) if by_plane else (nz, plane)
    rows = 2 * CHUNK
    *parts, energy = pl.pallas_call(
        functools.partial(potential_kernel, start, steps, layout, by_plane),
        out_shape=[
            *[pltpu.VMEM((inner, own, steps * rows, LANES), jnp.bfloat16)] * groups,
            pltpu.VMEM((CHUNK, LANES), jnp.float32),
        ],
        scratch_shapes=[
            pltpu.VMEM((cols.shape[0], 4 * walk, vectors), jnp.bfloat16),
            pltpu.VMEM((CHUNK * CHUNK, CHUNK * CHUNK), jnp.bfloat16),
        ],
        cost_estimate=FREE,
        compiler_params=params(16),
        name="potential",
    )(fields, *in_vmem(bias, *others, cols, turned))
    return parts, energy


def add(refs, *at):
    total = refs[0][at].astype(jnp.float32)
    for ref in refs[1:]:
        total = total + ref[at].astype(jnp.float32)
    return total


def vmem_call(kernel, name, out_shape, *arrays):
    return pl.pallas_call(
        kernel, out_shape=out_shape, cost_estimate=FREE, compiler_params=params(16), name=name
    )(*in_vmem(*arrays))


def sum_call(arrays):
    def kernel(*refs):
        for k, out in enumerate(refs[len(arrays):]):
            out[...] = add(refs[:len(arrays)], k).astype(out.dtype)

    out_shape = [pltpu.VMEM(arrays[0].shape[1:], jnp.bfloat16)] * arrays[0].shape[0]
    return vmem_call(kernel, "sum_parts", out_shape, *arrays)


def finish_call(factor, early, late):
    own, rows, lanes = early[0].shape

    def kernel(*refs):
        out = refs[-1]
        out[:, :rows] = (factor * add(refs[:len(early)], Ellipsis)).astype(out.dtype)
        out[:, rows:] = (factor * add(refs[len(early):-1], Ellipsis)).astype(out.dtype)

    out_shape = pltpu.VMEM((own, rows + late[0].shape[1], lanes), jnp.bfloat16)
    return vmem_call(kernel, "finish", out_shape, *early, *late)


def stack_call(pieces, slots, near):
    def kernel(*refs):
        ins, outs = refs[:len(pieces) + len(near)], refs[len(pieces) + len(near):]
        for ref, slot in zip(ins, slots):
            outs[0][slot] = ref[...]
        for ref, out in zip(ins[len(pieces):], outs[1:]):
            out[...] = ref[...]

    one = pltpu.VMEM(pieces[0].shape, jnp.bfloat16)
    out_shape = [pltpu.VMEM((len(pieces), *pieces[0].shape), jnp.bfloat16)] + [one] * len(near)
    return vmem_call(kernel, "stack_pieces", out_shape, *pieces, *near)


def series_kernel(n_orb, *refs):
    found, start = refs[:n_orb], refs[n_orb:2 * n_orb]
    energy_ref, moved_ref, pot, term, total = refs[2 * n_orb:]
    me = lax.axis_index("orb")
    own, half_rows = start[0].shape[:2]
    rowblocks = half_rows // BLOCK
    per = BLOCK // CHUNK
    for d in range(n_orb):
        at = lax.rem(me + d, n_orb)
        term[pl.ds(at, 1)] = start[d][...][None]
        for t in range(rowblocks * per):
            for half in range(2):
                rows = slice((2 * t + half) * CHUNK, (2 * t + half + 1) * CHUNK)
                pot[pl.ds(at * rowblocks + t // per, 1), :, (t % per) * CHUNK:(t % per + 1) * CHUNK,
                    half * LANES:(half + 1) * LANES] = found[d][:, rows, :][None]
    for j in range(own):
        blocks = [term[r // rowblocks, j, (r % rowblocks) * BLOCK:(r % rowblocks + 1) * BLOCK] for r in range(ROWBLK)]
        sums = [jnp.zeros(blocks[0].shape, jnp.float32)] * ROWBLK
        begin = blocks
        for degree in range(1, TAYLOR + 1):
            after = []
            for r in range(ROWBLK):
                right = jnp.concatenate([blocks[c] for c in column_order(r)], axis=0)
                product = jnp.dot(pot[r, j], right, preferred_element_type=jnp.float32)
                after.append((product / degree).astype(jnp.bfloat16))
            blocks = after
            sums = [s + b.astype(jnp.float32) for s, b in zip(sums, blocks)]
        for r in range(ROWBLK):
            moved = begin[r].astype(jnp.float32) + sums[r]
            total[r // rowblocks, j, (r % rowblocks) * BLOCK:(r % rowblocks + 1) * BLOCK] = moved.astype(jnp.bfloat16)
    mine = total[pl.ds(me, 1)][0]
    at = lax.broadcasted_iota(jnp.int32, (CHUNK, LANES), 0)
    high, middle, low = (part.astype(jnp.float32) for part in split(energy_ref[...]))
    tile = jnp.where(at == 0, high, jnp.where(at == 1, middle, jnp.where(at == 2, low, 0.0)))
    moved_ref[:own * half_rows] = mine.reshape(own * half_rows, mine.shape[2])
    moved_ref[own * half_rows:] = tile.astype(jnp.bfloat16)


def series_call(found, start, energy):
    n_orb = len(found)
    own, half_rows, nocc = start[0].shape
    return pl.pallas_call(
        functools.partial(series_kernel, n_orb),
        out_shape=pltpu.VMEM((own * half_rows + CHUNK, nocc), jnp.bfloat16),
        scratch_shapes=[
            pltpu.VMEM((ROWBLK, own, BLOCK, 2 * LANES), jnp.bfloat16),
            pltpu.VMEM((n_orb, own, half_rows, nocc), jnp.bfloat16),
            pltpu.VMEM((n_orb, own, half_rows, nocc), jnp.bfloat16),
        ],
        cost_estimate=FREE,
        compiler_params=params(16),
        name="series",
    )(*in_vmem(*found, *start, energy))


def place_kernel(layout, *refs):
    nz, plane, own = layout
    near, far = refs[:plane], refs[plane:2 * plane]
    out, energy_ref = refs[2 * plane:]
    me = lax.axis_index("chol")
    rows = out.shape[1]
    energy = jnp.zeros((CHUNK, LANES), jnp.float32)
    for dp in range(plane):
        for dz in range(nz):
            z = hop(lax.div(me, plane), -dz if nz & (nz - 1) else dz, nz)
            p = hop(lax.rem(me, plane), -dp if plane & (plane - 1) else dp, plane)
            piece = far[dp].at[dz - 1] if dz else near[dp]
            for j in range(own):
                out[(z * plane + p) * own + j] = piece[j * rows:(j + 1) * rows]
            energy = energy + piece[own * rows:].astype(jnp.float32)
    energy_ref[...] = (energy[0:1] + energy[1:2] + energy[2:3])[:, :energy_ref.shape[1]]


def place_call(layout, near, far):
    nz, plane, own = layout
    walk = nz * plane * own
    rows = (near[0].shape[0] - CHUNK) // own
    return pl.pallas_call(
        functools.partial(place_kernel, layout),
        out_shape=[
            jax.ShapeDtypeStruct((walk, rows, near[0].shape[1]), jnp.bfloat16),
            jax.ShapeDtypeStruct((1, walk), jnp.float32),
        ],
        cost_estimate=FREE,
        compiler_params=params(16),
        name="place_walkers",
    )(*in_vmem(*near, *far))


def per_device(chol_vals, chol_cols, greens, walkers, fields):
    vectors, rowblocks = chol_vals.shape[:2]
    walk, half_rows = greens.shape[:2]
    chips = lax.axis_size("chol")
    n_orb = lax.axis_size("orb")
    plane = 4 if chips % 4 == 0 else 1
    nz = chips // plane
    own = walk // chips
    layout = (nz, plane, own)
    step_factor = 72.0 / float(vectors * chips * BLOCK) ** 0.5

    def to_plane(a, dp):
        return lax.ppermute(a, "chol", [(c, (c // plane) * plane + hop(c % plane, dp, plane)) for c in range(chips)])

    def to_z(a, dz):
        return lax.ppermute(a, "chol", [(c, hop(c // plane, dz, nz) * plane + c % plane) for c in range(chips)])

    def around_orb(a):
        return [a] + [lax.ppermute(a, "orb", [((c + d) % n_orb, c) for c in range(n_orb)]) for d in range(1, n_orb)]

    cols = jnp.transpose(chol_cols, (1, 2, 0))
    turned, partial_bias, mine, cols = bias_call(chol_vals, greens, walkers, cols, own)
    start = around_orb(mine)
    bias, *others = around_orb(partial_bias)
    start, others = lax.optimization_barrier((start, others))

    total_steps = rowblocks * BLOCK // CHUNK
    early_steps = total_steps // 4
    late_steps = total_steps - early_steps
    fields_t = fields.T
    def all_plane(arrays):
        return [to_plane(arrays[dp - 1], dp) for dp in reversed(range(1, plane))]

    z_order = [*range(2, nz), 1]

    def all_z(arrays):
        return [to_z(arrays[dz - 1], dz) for dz in z_order]

    late, energy = potential_call(early_steps, late_steps, layout, True, fields_t, bias, others, cols, turned)
    early, _ = potential_call(0, early_steps, layout, False, fields_t, bias, others, cols, turned)
    early_came = all_z(early[1:])
    late = sum_call([late[0], *all_plane(late[1:])])
    late_came = all_z(late[1:])
    early = sum_call([early[0], *early_came])
    found = finish_call(step_factor, [early[0], *all_plane(early[1:])], [late[0], *late_came])

    piece = series_call(around_orb(found), start, energy)
    near = [piece, *(to_plane(piece, dp) for dp in range(1, plane))]
    came = all_z([piece] * (nz - 1))
    pieces, *near[1:] = stack_call(came, [dz - 1 for dz in z_order], near[1:])
    far = {dp: to_plane(pieces, dp) for dp in reversed(range(1, plane))}
    moved, energy = place_call(layout, near, [pieces, *(far[dp] for dp in range(1, plane))])
    return moved, energy.reshape(walk)


def solution(mesh):
    in_specs = (
        P("chol", "orb", None, None),
        P("chol", "orb", None),
        P("walker", "orb", None),
        P("walker", "orb", None),
        P("chol", "walker"),
    )
    out_specs = (P("walker", "orb", None), P("walker"))
    return jax.shard_map(
        per_device, mesh=mesh, in_specs=in_specs, out_specs=out_specs, check_vma=False
    )
```

```python
import functools

import jax
import jax.numpy as jnp
from jax import lax
from jax.experimental import pallas as pl
from jax.experimental.pallas import tpu as pltpu
from jax.sharding import PartitionSpec as P

BLOCK = 64
TAYLOR = 4
ROWBLK = 4
LANES = 2 * BLOCK
CHUNK = 16
MIB = 1024 * 1024


FREE = pl.CostEstimate(flops=0, bytes_accessed=0, transcendentals=0)


def params(mib):
    return pltpu.CompilerParams(vmem_limit_bytes=mib * MIB)


def split(value):
    parts = []
    for _ in range(3):
        parts.append(value.astype(jnp.bfloat16))
        value = value - parts[-1].astype(jnp.float32)
    return parts


def in_vmem(*arrays):
    return [pltpu.with_memory_space_constraint(a, pltpu.VMEM) for a in arrays]


def in_hbm(*arrays):
    return [pltpu.with_memory_space_constraint(a, pltpu.HBM) for a in arrays]


def hop(at, distance, count):
    return at ^ distance if count & (count - 1) == 0 else (at + distance) % count


def swap_matrix():
    to = lax.broadcasted_iota(jnp.int32, (CHUNK * CHUNK, CHUNK * CHUNK), 0)
    at = lax.broadcasted_iota(jnp.int32, (CHUNK * CHUNK, CHUNK * CHUNK), 1)
    same = (to // CHUNK == at % CHUNK) & (to % CHUNK == at // CHUNK)
    return same.astype(jnp.float32).astype(jnp.bfloat16)


def column_order(row):
    other = 2 - 2 * (row // 2)
    return row, row + 1 - 2 * (row % 2), other, other + 1


def slot_masks(cols, row):
    return [cols == column for column in column_order(row)[1:]]


def bias_kernel(vals_hbm, greens_hbm, walkers_hbm, cols_hbm, turned_ref, bias_ref, mine_ref, cols_ref, vals, greens, swap, gs,
                acc, vsem, gsem, wsem, csem):
    total_steps, vectors = turned_ref.shape[:2]
    walk = bias_ref.shape[0]
    steps = BLOCK // CHUNK

    def copies(t):
        rows = pl.ds(lax.rem(t, steps) * CHUNK, CHUNK)
        return (
            pltpu.make_async_copy(vals_hbm.at[:, lax.div(t, steps), rows, :], vals.at[t], vsem.at[t]),
            pltpu.make_async_copy(greens_hbm.at[:, pl.ds(t * CHUNK, CHUNK), :], greens.at[t], gsem.at[t]),
        )

    def begin(t, carry):
        for copy in copies(t):
            copy.start()
        return carry

    own = mine_ref.shape[0]
    lax.fori_loop(0, total_steps, begin, 0)
    take = pltpu.make_async_copy(walkers_hbm.at[pl.ds(lax.axis_index("chol") * own, own)], mine_ref, wsem)
    take.start()
    take_cols = pltpu.make_async_copy(cols_hbm, cols_ref, csem)
    take_cols.start()
    swap[...] = swap_matrix()
    bias_ref[...] = jnp.zeros_like(bias_ref)
    first = lax.broadcasted_iota(jnp.int32, (CHUNK * CHUNK, LANES), 1) < BLOCK

    def step(t, carry):
        for copy in copies(t):
            copy.wait()
        local = lax.div(t, steps)
        row = lax.axis_index("orb") * cols_ref.shape[0] + local
        upper = row // 2 == 1
        odd = row % 2 == 1
        for w in range(0, walk, CHUNK):
            mixed = greens[t, w:w + CHUNK].reshape(CHUNK * CHUNK, 2 * LANES)
            mixed = jnp.dot(swap[...], mixed, preferred_element_type=jnp.float32)
            pair = jnp.where(upper, mixed[:, LANES:], mixed[:, :LANES])
            rest = jnp.where(upper, mixed[:, :LANES], mixed[:, LANES:])
            pair = jnp.where(odd, pltpu.roll(pair, BLOCK, 1), pair)
            pieces = (
                jnp.where(first, pair, 0.0),
                jnp.where(first, 0.0, pair),
                jnp.where(first, 0.0, pltpu.roll(rest, BLOCK, 1)),
                jnp.where(first, 0.0, rest),
            )
            for k, piece in enumerate(pieces):
                piece = piece.astype(jnp.bfloat16)
                for i in range(CHUNK):
                    gs[k * walk + w:k * walk + w + CHUNK, i * LANES:(i + 1) * LANES] = piece[i * CHUNK:(i + 1) * CHUNK]
        for g in range(0, vectors, 2 * CHUNK):
            both = [vals[t, g + side * CHUNK:g + (side + 1) * CHUNK].reshape(CHUNK * CHUNK, LANES) for side in range(2)]
            both = jnp.dot(swap[...], jnp.concatenate(both, axis=1), preferred_element_type=jnp.float32)
            both = both.astype(jnp.bfloat16)
            for i in range(CHUNK):
                for side in range(2):
                    turned_ref[t, g + side * CHUNK:g + (side + 1) * CHUNK, i * LANES:(i + 1) * LANES] = (
                        both[i * CHUNK:(i + 1) * CHUNK, side * LANES:(side + 1) * LANES]
                    )
        part = lax.dot_general(
            turned_ref[t], gs[...], (((1,), (1,)), ((), ())), preferred_element_type=jnp.float32
        )
        begins = lax.rem(t, steps) == 0
        acc[...] = jnp.where(begins, 0.0, acc[...]) + part

        @pl.when(lax.rem(t, steps) == steps - 1)
        def _():
            flat = acc[...].T
            total = flat[0:walk]
            cols = cols_ref[local, 1:2, :]
            for k, mask in enumerate(slot_masks(cols, row)):
                total = total + jnp.where(mask, flat[(k + 1) * walk:(k + 2) * walk], 0.0)
            bias_ref[...] += total

        return carry

    acc[...] = jnp.zeros_like(acc)
    take_cols.wait()
    lax.fori_loop(0, total_steps, step, 0)
    take.wait()


def bias_call(vals, greens, walkers, cols, own):
    vectors, rowblocks = vals.shape[:2]
    walk, half_rows, norb = greens.shape
    steps = half_rows // CHUNK
    wide = CHUNK * LANES
    return pl.pallas_call(
        bias_kernel,
        in_specs=[
            *[pl.BlockSpec(memory_space=pl.ANY)] * 4,
        ],
        out_specs=[pl.BlockSpec(memory_space=pltpu.VMEM)] * 4,
        out_shape=[
            pltpu.VMEM((steps, vectors, wide), jnp.bfloat16),
            pltpu.VMEM((walk, vectors), jnp.float32),
            pltpu.VMEM((own, *walkers.shape[1:]), jnp.bfloat16),
            pltpu.VMEM(cols.shape, jnp.int32),
        ],
        scratch_shapes=[
            pltpu.VMEM((steps, vectors, CHUNK, LANES), jnp.bfloat16),
            pltpu.VMEM((steps, walk, CHUNK, norb), jnp.bfloat16),
            pltpu.VMEM((CHUNK * CHUNK, CHUNK * CHUNK), jnp.bfloat16),
            pltpu.VMEM((4 * walk, wide), jnp.bfloat16),
            pltpu.VMEM((vectors, 4 * walk), jnp.float32),
            pltpu.SemaphoreType.DMA((steps,)),
            pltpu.SemaphoreType.DMA((steps,)),
            pltpu.SemaphoreType.DMA,
            pltpu.SemaphoreType.DMA,
        ],
        cost_estimate=FREE,
        compiler_params=params(24),
        name="force_bias",
    )(*in_hbm(vals, greens, walkers, cols))


def potential_kernel(layout, fields_ref, own_ref, *refs):
    nz, plane, own = layout
    others = refs[:lax.axis_size("orb") - 1]
    cols_ref, turned_ref = refs[len(others):len(others) + 2]
    *outs, energy_ref, s_ref, swap = refs[len(others) + 2:]
    steps = turned_ref.shape[0]
    walk, vectors = fields_ref.shape
    rowblocks = cols_ref.shape[0]

    me = lax.axis_index("chol")
    bias = own_ref[...]
    for other in others:
        bias = bias + other[...]
    energy = 0.5 * jnp.sum(bias * bias, axis=1, keepdims=True)
    energy_ref[...] = jnp.zeros_like(energy_ref)
    energy_ref[:, :walk] = jnp.broadcast_to(energy, (walk, LANES)).T[:CHUNK]
    shifted = (fields_ref[...] - bias).astype(jnp.bfloat16)
    at = lax.broadcasted_iota(jnp.int32, (walk, walk), 0)
    source = lax.broadcasted_iota(jnp.int32, (walk, walk), 1)
    chip = at // own
    z = hop(me // plane, chip // plane, nz)
    p = hop(me % plane, chip % plane, plane)
    wanted = (z * plane + p) * own + at % own
    pick = (wanted == source).astype(jnp.float32).astype(jnp.bfloat16)
    ordered = jnp.dot(pick, shifted, preferred_element_type=jnp.float32)
    for local in range(rowblocks):
        row = lax.axis_index("orb") * rowblocks + local
        s_ref[local, 0:walk] = ordered.astype(jnp.bfloat16)
        for k, mask in enumerate(slot_masks(cols_ref[local, 1:2, :], row)):
            s_ref[local, (k + 1) * walk:(k + 2) * walk] = jnp.where(mask, ordered, 0.0).astype(jnp.bfloat16)
    swap[...] = swap_matrix()
    first = lax.broadcasted_iota(jnp.int32, (walk, LANES), 1) < BLOCK

    def step(t, carry):
        left = s_ref[lax.div(t, BLOCK // CHUNK)]
        tiles = []
        for i in range(0, CHUNK, 2):
            both = jnp.dot(
                left, turned_ref[t, :, i * LANES:(i + 2) * LANES], preferred_element_type=jnp.float32
            )
            for side in range(2):
                out = both[:, side * LANES:(side + 1) * LANES]
                near = jnp.where(first, out[0:walk], out[walk:2 * walk])
                far = jnp.where(first, pltpu.roll(out[2 * walk:3 * walk], BLOCK, 1), out[3 * walk:])
                tiles.append(jnp.concatenate([near, far], axis=1).astype(jnp.bfloat16))
        for w0 in range(0, walk, CHUNK):
            mixed = jnp.concatenate([tile[w0:w0 + CHUNK] for tile in tiles], axis=0)
            mixed = jnp.dot(swap[...], mixed, preferred_element_type=jnp.float32).astype(jnp.bfloat16)
            for w in range(CHUNK):
                chip, j = (w0 + w) // own, (w0 + w) % own
                dz, dp = chip // plane, chip % plane
                for half in range(2):
                    rows = pl.ds(pl.multiple_of((2 * t + half) * CHUNK, CHUNK), CHUNK)
                    outs[j * plane + dp][dz, rows] = mixed[w * CHUNK:(w + 1) * CHUNK, half * LANES:(half + 1) * LANES]
        return carry

    lax.fori_loop(0, steps // 2, lambda t, carry: step(2 * t + 1, step(2 * t, carry)), 0)
    if steps % 2:
        step(steps - 1, 0)


def potential_call(layout, fields, bias, others, cols, turned):
    nz, plane, own = layout
    walk, vectors = fields.shape
    rows = turned.shape[0] * 2 * CHUNK
    *parts, energy = pl.pallas_call(
        functools.partial(potential_kernel, layout),
        out_shape=[
            *[pltpu.VMEM((nz, rows, LANES), jnp.bfloat16)] * (own * plane),
            pltpu.VMEM((CHUNK, LANES), jnp.float32),
        ],
        scratch_shapes=[
            pltpu.VMEM((cols.shape[0], 4 * walk, vectors), jnp.bfloat16),
            pltpu.VMEM((CHUNK * CHUNK, CHUNK * CHUNK), jnp.bfloat16),
        ],
        cost_estimate=FREE,
        compiler_params=params(16),
        name="potential",
    )(fields, *in_vmem(bias, *others, cols, turned))
    return [parts[j * plane:(j + 1) * plane] for j in range(own)], energy


def add(refs, *at):
    total = refs[0][at].astype(jnp.float32)
    for ref in refs[1:]:
        total = total + ref[at].astype(jnp.float32)
    return total


def vmem_call(kernel, name, out_shape, *arrays):
    return pl.pallas_call(
        kernel, out_shape=out_shape, cost_estimate=FREE, compiler_params=params(16), name=name
    )(*in_vmem(*arrays))


def sum_call(arrays):
    def kernel(*refs):
        for k, out in enumerate(refs[len(arrays):]):
            out[...] = add(refs[:len(arrays)], k).astype(out.dtype)

    out_shape = [pltpu.VMEM(arrays[0].shape[1:], jnp.bfloat16)] * arrays[0].shape[0]
    return vmem_call(kernel, "sum_parts", out_shape, *arrays)


def finish_call(factor, arrays):
    def kernel(*refs):
        refs[-1][...] = (factor * add(refs[:-1], Ellipsis)).astype(jnp.bfloat16)

    return vmem_call(kernel, "finish", pltpu.VMEM(arrays[0].shape, jnp.bfloat16), *arrays)


def stack_call(pieces, slots, after):
    def kernel(*refs):
        for ref, slot in zip(refs, slots):
            refs[-1][slot] = ref[...]

    out_shape = pltpu.VMEM((len(pieces), *pieces[0].shape), jnp.bfloat16)
    return vmem_call(kernel, "stack_pieces", out_shape, *pieces, *after)


def series_kernel(n_orb, j, *refs):
    found, start = refs[:n_orb], refs[n_orb:2 * n_orb]
    energy_refs, (moved_ref, pot, term, total) = refs[2 * n_orb:-4], refs[-4:]
    me = lax.axis_index("orb")
    half_rows = start[0].shape[1]
    rowblocks = half_rows // BLOCK
    per = BLOCK // CHUNK
    for d in range(n_orb):
        at = lax.rem(me + d, n_orb)
        term[at] = start[d][j]
        for t in range(rowblocks * per):
            for half in range(2):
                rows = slice((2 * t + half) * CHUNK, (2 * t + half + 1) * CHUNK)
                pot[at * rowblocks + t // per, (t % per) * CHUNK:(t % per + 1) * CHUNK,
                    half * LANES:(half + 1) * LANES] = found[d][rows, :]
    blocks = [term[r // rowblocks, (r % rowblocks) * BLOCK:(r % rowblocks + 1) * BLOCK] for r in range(ROWBLK)]
    sums = [jnp.zeros(blocks[0].shape, jnp.float32)] * ROWBLK
    begin = blocks
    for degree in range(1, TAYLOR + 1):
        after = []
        for r in range(ROWBLK):
            right = jnp.concatenate([blocks[c] for c in column_order(r)], axis=0)
            product = jnp.dot(pot[r], right, preferred_element_type=jnp.float32)
            after.append((product / degree).astype(jnp.bfloat16))
        blocks = after
        sums = [s + b.astype(jnp.float32) for s, b in zip(sums, blocks)]
    for r in range(ROWBLK):
        moved = begin[r].astype(jnp.float32) + sums[r]
        total[r // rowblocks, (r % rowblocks) * BLOCK:(r % rowblocks + 1) * BLOCK] = moved.astype(jnp.bfloat16)
    moved_ref[:half_rows] = total[me]
    for energy_ref in energy_refs:
        at = lax.broadcasted_iota(jnp.int32, (CHUNK, LANES), 0)
        high, middle, low = (part.astype(jnp.float32) for part in split(energy_ref[...]))
        tile = jnp.where(at == 0, high, jnp.where(at == 1, middle, jnp.where(at == 2, low, 0.0)))
        moved_ref[half_rows:] = tile.astype(jnp.bfloat16)


def series_call(j, found, start, energies):
    n_orb = len(found)
    half_rows, nocc = start[0].shape[1:]
    return pl.pallas_call(
        functools.partial(series_kernel, n_orb, j),
        out_shape=pltpu.VMEM((half_rows + CHUNK * len(energies), nocc), jnp.bfloat16),
        scratch_shapes=[
            pltpu.VMEM((ROWBLK, BLOCK, 2 * LANES), jnp.bfloat16),
            pltpu.VMEM((n_orb, half_rows, nocc), jnp.bfloat16),
            pltpu.VMEM((n_orb, half_rows, nocc), jnp.bfloat16),
        ],
        cost_estimate=FREE,
        compiler_params=params(16),
        name="series",
    )(*in_vmem(*found, *start, *energies))


def place_kernel(layout, *refs):
    nz, plane, own = layout
    *gathered, out, energy_ref = refs
    me = lax.axis_index("chol")
    rows = out.shape[1]
    energy = jnp.zeros((CHUNK, LANES), jnp.float32)
    for dp in range(plane):
        for dz in range(nz):
            z = hop(lax.div(me, plane), -dz if nz & (nz - 1) else dz, nz)
            p = hop(lax.rem(me, plane), -dp if plane & (plane - 1) else dp, plane)
            for j in range(own):
                out[(z * plane + p) * own + j] = gathered[j * plane + dp][dz, :rows]
            energy = energy + gathered[dp][dz, rows:].astype(jnp.float32)
    energy_ref[...] = (energy[0:1] + energy[1:2] + energy[2:3])[:, :energy_ref.shape[1]]


def place_call(layout, rows, gathered):
    nz, plane, own = layout
    walk = nz * plane * own
    out_shape = [
        jax.ShapeDtypeStruct((walk, rows, gathered[0].shape[2]), jnp.bfloat16),
        jax.ShapeDtypeStruct((1, walk), jnp.float32),
    ]
    return vmem_call(functools.partial(place_kernel, layout), "place_walkers", out_shape, *gathered)


def per_device(chol_vals, chol_cols, greens, walkers, fields):
    vectors, rowblocks = chol_vals.shape[:2]
    walk, half_rows = greens.shape[:2]
    chips = lax.axis_size("chol")
    n_orb = lax.axis_size("orb")
    plane = 4 if chips % 4 == 0 else 1
    nz = chips // plane
    own = walk // chips
    layout = (nz, plane, own)
    step_factor = 72.0 / float(vectors * chips * BLOCK) ** 0.5

    def to_plane(a, dp):
        return lax.ppermute(a, "chol", [(c, (c // plane) * plane + hop(c % plane, dp, plane)) for c in range(chips)])

    def to_z(a, dz):
        return lax.ppermute(a, "chol", [(c, hop(c // plane, dz, nz) * plane + c % plane) for c in range(chips)])

    def around_orb(a):
        return [a] + [lax.ppermute(a, "orb", [((c + d) % n_orb, c) for c in range(n_orb)]) for d in range(1, n_orb)]

    cols = jnp.transpose(chol_cols, (1, 2, 0))
    turned, partial_bias, mine, cols = bias_call(chol_vals, greens, walkers, cols, own)
    start = around_orb(mine)
    bias, *others = around_orb(partial_bias)
    start, others = lax.optimization_barrier((start, others))

    def all_plane(arrays):
        return [to_plane(arrays[dp - 1], dp) for dp in reversed(range(1, plane))]

    z_order = [*range(2, nz), 1]

    def all_z(arrays):
        return [to_z(arrays[dz - 1], dz) for dz in z_order]

    parts, energy = potential_call(layout, fields.T, bias, others, cols, turned)
    sums = [sum_call([part[0], *all_plane(part[1:])]) for part in parts]
    gathered = {}
    for j in reversed(range(own)):
        found = finish_call(step_factor, [sums[j][0], *all_z(sums[j][1:])])
        piece = series_call(j, around_orb(found), start, [] if j else [energy])
        came = all_z([piece] * (nz - 1))
        pieces = stack_call([piece, *reversed(came)], [0, *reversed(z_order)], gathered.get(j + 1, [])[1:])
        gathered[j] = [pieces, *reversed(all_plane([pieces] * (plane - 1)))]
    moved, energy = place_call(layout, half_rows, sum((gathered[j] for j in range(own)), []))
    return moved, energy.reshape(walk)


def solution(mesh):
    in_specs = (
        P("chol", "orb", None, None),
        P("chol", "orb", None),
        P("walker", "orb", None),
        P("walker", "orb", None),
        P("chol", "walker"),
    )
    out_specs = (P("walker", "orb", None), P("walker"))
    return jax.shard_map(
        per_device, mesh=mesh, in_specs=in_specs, out_specs=out_specs, check_vma=False
    )
```

```python
import functools

import jax
import jax.numpy as jnp
from jax import lax
from jax.experimental import pallas as pl
from jax.experimental.pallas import tpu as pltpu
from jax.sharding import PartitionSpec as P

BLOCK = 64
TAYLOR = 4
ROWBLK = 4
LANES = 2 * BLOCK
CHUNK = 16
MIB = 1024 * 1024


FREE = pl.CostEstimate(flops=0, bytes_accessed=0, transcendentals=0)


def params(mib):
    return pltpu.CompilerParams(vmem_limit_bytes=mib * MIB)


def split(value):
    parts = []
    for _ in range(3):
        parts.append(value.astype(jnp.bfloat16))
        value = value - parts[-1].astype(jnp.float32)
    return parts


def in_vmem(*arrays):
    return [pltpu.with_memory_space_constraint(a, pltpu.VMEM) for a in arrays]


def in_hbm(*arrays):
    return [pltpu.with_memory_space_constraint(a, pltpu.HBM) for a in arrays]


def hop(at, distance, count):
    return at ^ distance if count & (count - 1) == 0 else (at + distance) % count


def swap_matrix():
    to = lax.broadcasted_iota(jnp.int32, (CHUNK * CHUNK, CHUNK * CHUNK), 0)
    at = lax.broadcasted_iota(jnp.int32, (CHUNK * CHUNK, CHUNK * CHUNK), 1)
    same = (to // CHUNK == at % CHUNK) & (to % CHUNK == at // CHUNK)
    return same.astype(jnp.float32).astype(jnp.bfloat16)


def column_order(row):
    other = 2 - 2 * (row // 2)
    return row, row + 1 - 2 * (row % 2), other, other + 1


def slot_masks(cols, row):
    return [cols == column for column in column_order(row)[1:]]


def bias_kernel(vals_hbm, greens_hbm, walkers_hbm, cols_hbm, turned_ref, bias_ref, mine_ref, cols_ref, vals, greens, swap, gs,
                acc, vsem, gsem, wsem, csem):
    total_steps, vectors = turned_ref.shape[:2]
    walk = bias_ref.shape[0]
    steps = BLOCK // CHUNK

    def copies(t):
        rows = pl.ds(lax.rem(t, steps) * CHUNK, CHUNK)
        return (
            pltpu.make_async_copy(vals_hbm.at[:, lax.div(t, steps), rows, :], vals.at[t], vsem.at[t]),
            pltpu.make_async_copy(greens_hbm.at[:, pl.ds(t * CHUNK, CHUNK), :], greens.at[t], gsem.at[t]),
        )

    def begin(t, carry):
        for copy in copies(t):
            copy.start()
        return carry

    own = mine_ref.shape[0]
    take = pltpu.make_async_copy(walkers_hbm.at[pl.ds(lax.axis_index("chol") * own, own)], mine_ref, wsem)
    take.start()
    take_cols = pltpu.make_async_copy(cols_hbm, cols_ref, csem)
    take_cols.start()
    lax.fori_loop(0, total_steps, begin, 0)
    swap[...] = swap_matrix()
    bias_ref[...] = jnp.zeros_like(bias_ref)
    first = lax.broadcasted_iota(jnp.int32, (CHUNK * CHUNK, LANES), 1) < BLOCK

    def step(t, carry):
        for copy in copies(t):
            copy.wait()
        local = lax.div(t, steps)
        row = lax.axis_index("orb") * cols_ref.shape[0] + local
        upper = row // 2 == 1
        odd = row % 2 == 1
        for w in range(0, walk, CHUNK):
            mixed = greens[t, w:w + CHUNK].reshape(CHUNK * CHUNK, 2 * LANES)
            mixed = jnp.dot(swap[...], mixed, preferred_element_type=jnp.float32)
            pair = jnp.where(upper, mixed[:, LANES:], mixed[:, :LANES])
            rest = jnp.where(upper, mixed[:, :LANES], mixed[:, LANES:])
            pair = jnp.where(odd, pltpu.roll(pair, BLOCK, 1), pair)
            pieces = (
                jnp.where(first, pair, 0.0),
                jnp.where(first, 0.0, pair),
                jnp.where(first, 0.0, pltpu.roll(rest, BLOCK, 1)),
                jnp.where(first, 0.0, rest),
            )
            for k, piece in enumerate(pieces):
                piece = piece.astype(jnp.bfloat16)
                for i in range(CHUNK):
                    gs[k * walk + w:k * walk + w + CHUNK, i * LANES:(i + 1) * LANES] = piece[i * CHUNK:(i + 1) * CHUNK]
        for g in range(0, vectors, 2 * CHUNK):
            both = [vals[t, g + side * CHUNK:g + (side + 1) * CHUNK].reshape(CHUNK * CHUNK, LANES) for side in range(2)]
            both = jnp.dot(swap[...], jnp.concatenate(both, axis=1), preferred_element_type=jnp.float32)
            both = both.astype(jnp.bfloat16)
            for i in range(CHUNK):
                for side in range(2):
                    turned_ref[t, g + side * CHUNK:g + (side + 1) * CHUNK, i * LANES:(i + 1) * LANES] = (
                        both[i * CHUNK:(i + 1) * CHUNK, side * LANES:(side + 1) * LANES]
                    )
        part = lax.dot_general(
            turned_ref[t], gs[...], (((1,), (1,)), ((), ())), preferred_element_type=jnp.float32
        )
        begins = lax.rem(t, steps) == 0
        acc[...] = jnp.where(begins, 0.0, acc[...]) + part

        @pl.when(lax.rem(t, steps) == steps - 1)
        def _():
            flat = acc[...].T
            total = flat[0:walk]
            cols = cols_ref[local, 1:2, :]
            for k, mask in enumerate(slot_masks(cols, row)):
                total = total + jnp.where(mask, flat[(k + 1) * walk:(k + 2) * walk], 0.0)
            bias_ref[...] += total

        return carry

    acc[...] = jnp.zeros_like(acc)
    take_cols.wait()
    lax.fori_loop(0, total_steps, step, 0)
    take.wait()


def bias_call(vals, greens, walkers, cols, own):
    vectors, rowblocks = vals.shape[:2]
    walk, half_rows, norb = greens.shape
    steps = half_rows // CHUNK
    wide = CHUNK * LANES
    return pl.pallas_call(
        bias_kernel,
        in_specs=[
            *[pl.BlockSpec(memory_space=pl.ANY)] * 4,
        ],
        out_specs=[pl.BlockSpec(memory_space=pltpu.VMEM)] * 4,
        out_shape=[
            pltpu.VMEM((steps, vectors, wide), jnp.bfloat16),
            pltpu.VMEM((walk, vectors), jnp.float32),
            pltpu.VMEM((own, *walkers.shape[1:]), jnp.bfloat16),
            pltpu.VMEM(cols.shape, jnp.int32),
        ],
        scratch_shapes=[
            pltpu.VMEM((steps, vectors, CHUNK, LANES), jnp.bfloat16),
            pltpu.VMEM((steps, walk, CHUNK, norb), jnp.bfloat16),
            pltpu.VMEM((CHUNK * CHUNK, CHUNK * CHUNK), jnp.bfloat16),
            pltpu.VMEM((4 * walk, wide), jnp.bfloat16),
            pltpu.VMEM((vectors, 4 * walk), jnp.float32),
            pltpu.SemaphoreType.DMA((steps,)),
            pltpu.SemaphoreType.DMA((steps,)),
            pltpu.SemaphoreType.DMA,
            pltpu.SemaphoreType.DMA,
        ],
        cost_estimate=FREE,
        compiler_params=params(24),
        name="force_bias",
    )(*in_hbm(vals, greens, walkers, cols))


def potential_kernel(start, steps, layout, by_plane, fields_ref, own_ref, *refs):
    nz, plane, own = layout
    others = refs[:lax.axis_size("orb") - 1]
    cols_ref, turned_ref = refs[len(others):len(others) + 2]
    groups = 2 * plane if by_plane else nz
    outs = refs[len(others) + 2:len(others) + 2 + groups]
    energy_ref, s_ref, swap = refs[len(others) + 2 + groups:]
    walk, vectors = fields_ref.shape
    rowblocks = cols_ref.shape[0]

    me = lax.axis_index("chol")
    bias = own_ref[...]
    for other in others:
        bias = bias + other[...]
    energy = 0.5 * jnp.sum(bias * bias, axis=1, keepdims=True)
    energy_ref[...] = jnp.zeros_like(energy_ref)
    energy_ref[:, :walk] = jnp.broadcast_to(energy, (walk, LANES)).T[:CHUNK]
    shifted = (fields_ref[...] - bias).astype(jnp.bfloat16)
    at = lax.broadcasted_iota(jnp.int32, (walk, walk), 0)
    source = lax.broadcasted_iota(jnp.int32, (walk, walk), 1)
    chip = at // own
    z = hop(me // plane, chip // plane, nz)
    p = hop(me % plane, chip % plane, plane)
    wanted = (z * plane + p) * own + at % own
    pick = (wanted == source).astype(jnp.float32).astype(jnp.bfloat16)
    ordered = jnp.dot(pick, shifted, preferred_element_type=jnp.float32)
    for local in range(rowblocks):
        row = lax.axis_index("orb") * rowblocks + local
        s_ref[local, 0:walk] = ordered.astype(jnp.bfloat16)
        for k, mask in enumerate(slot_masks(cols_ref[local, 1:2, :], row)):
            s_ref[local, (k + 1) * walk:(k + 2) * walk] = jnp.where(mask, ordered, 0.0).astype(jnp.bfloat16)
    swap[...] = swap_matrix()
    first = lax.broadcasted_iota(jnp.int32, (walk, LANES), 1) < BLOCK

    def step(t, carry):
        left = s_ref[lax.div(start + t, BLOCK // CHUNK)]
        tiles = []
        for i in range(0, CHUNK, 2):
            both = jnp.dot(
                left, turned_ref[start + t, :, i * LANES:(i + 2) * LANES], preferred_element_type=jnp.float32
            )
            for side in range(2):
                out = both[:, side * LANES:(side + 1) * LANES]
                near = jnp.where(first, out[0:walk], out[walk:2 * walk])
                far = jnp.where(first, pltpu.roll(out[2 * walk:3 * walk], BLOCK, 1), out[3 * walk:])
                tiles.append(jnp.concatenate([near, far], axis=1).astype(jnp.bfloat16))
        for w0 in range(0, walk, CHUNK):
            mixed = jnp.concatenate([tile[w0:w0 + CHUNK] for tile in tiles], axis=0)
            mixed = jnp.dot(swap[...], mixed, preferred_element_type=jnp.float32).astype(jnp.bfloat16)
            for w in range(CHUNK):
                chip, j = (w0 + w) // own, (w0 + w) % own
                dz, dp = chip // plane, chip % plane
                if not by_plane:
                    out, inner = outs[dz], (dp,)
                elif dz:
                    out, inner = outs[dp], (dz - 1,)
                else:
                    out, inner = outs[plane + dp], ()
                for half in range(2):
                    rows = pl.ds(pl.multiple_of((2 * t + half) * CHUNK, CHUNK), CHUNK)
                    out[(*inner, j, rows)] = mixed[w * CHUNK:(w + 1) * CHUNK, half * LANES:(half + 1) * LANES]
        return carry

    lax.fori_loop(0, steps // 2, lambda t, carry: step(2 * t + 1, step(2 * t, carry)), 0)
    if steps % 2:
        step(steps - 1, 0)


def potential_call(start, steps, layout, by_plane, fields, bias, others, cols, turned):
    nz, plane, own = layout
    walk, vectors = fields.shape
    leading = [(nz - 1,)] * plane + [()] * plane if by_plane else [(plane,)] * nz
    rows = 2 * CHUNK
    *parts, energy = pl.pallas_call(
        functools.partial(potential_kernel, start, steps, layout, by_plane),
        out_shape=[
            *[pltpu.VMEM((*inner, own, steps * rows, LANES), jnp.bfloat16) for inner in leading],
            pltpu.VMEM((CHUNK, LANES), jnp.float32),
        ],
        scratch_shapes=[
            pltpu.VMEM((cols.shape[0], 4 * walk, vectors), jnp.bfloat16),
            pltpu.VMEM((CHUNK * CHUNK, CHUNK * CHUNK), jnp.bfloat16),
        ],
        cost_estimate=FREE,
        compiler_params=params(16),
        name="potential",
    )(fields, *in_vmem(bias, *others, cols, turned))
    return parts, energy


def add(refs, *at):
    total = refs[0][at].astype(jnp.float32)
    for ref in refs[1:]:
        total = total + ref[at].astype(jnp.float32)
    return total


def vmem_call(kernel, name, out_shape, *arrays):
    return pl.pallas_call(
        kernel, out_shape=out_shape, cost_estimate=FREE, compiler_params=params(16), name=name
    )(*in_vmem(*arrays))


def sum_call(arrays, after):
    def kernel(*refs):
        for k, out in enumerate(refs[len(arrays) + len(after):]):
            out[...] = add(refs[:len(arrays)], k).astype(out.dtype)

    out_shape = [pltpu.VMEM(arrays[0].shape[1:], jnp.bfloat16)] * arrays[0].shape[0]
    return vmem_call(kernel, "sum_parts", out_shape, *arrays, *after)


def merge_call(early, near):
    own, rows, lanes = early[0].shape[1:]

    def kernel(*refs):
        early_refs, near_refs, outs = refs[:len(early)], refs[len(early):len(early) + len(near)], refs[-len(near):]
        for k, (ref, out) in enumerate(zip(near_refs, outs)):
            out[:, :rows] = add(early_refs, k).astype(out.dtype)
            out[:, rows:] = ref[...]

    out_shape = [pltpu.VMEM((own, rows + near[0].shape[1], lanes), jnp.bfloat16)] * len(near)
    return vmem_call(kernel, "merge_parts", out_shape, *early, *near)


def finish_call(factor, far, merged):
    rows = merged[0].shape[1] - far[0].shape[1]

    def kernel(*refs):
        far_refs, merged_refs, out = refs[:len(far)], refs[len(far):-1], refs[-1]
        total = add(merged_refs, slice(None), slice(0, rows))
        out[:, :rows] = (factor * total).astype(out.dtype)
        total = add(merged_refs, slice(None), slice(rows, None)) + add(far_refs, Ellipsis)
        out[:, rows:] = (factor * total).astype(out.dtype)

    return vmem_call(kernel, "finish", pltpu.VMEM(merged[0].shape, jnp.bfloat16), *far, *merged)


def stack_call(near, pieces, slots):
    def kernel(*refs):
        ins, outs = refs[:len(pieces) + len(near)], refs[len(pieces) + len(near):]
        for ref, slot in zip(ins[len(near):], slots):
            outs[0][slot] = ref[...]
        for ref, out in zip(ins, outs[1:]):
            out[...] = ref[...]

    one = pltpu.VMEM(pieces[0].shape, jnp.bfloat16)
    out_shape = [pltpu.VMEM((len(pieces), *pieces[0].shape), jnp.bfloat16)] + [one] * len(near)
    return vmem_call(kernel, "stack_pieces", out_shape, *near, *pieces)


def series_kernel(n_orb, *refs):
    found, start = refs[:n_orb], refs[n_orb:2 * n_orb]
    energy_ref, moved_ref, pot, term, total = refs[2 * n_orb:]
    me = lax.axis_index("orb")
    own, half_rows = start[0].shape[:2]
    rowblocks = half_rows // BLOCK
    per = BLOCK // CHUNK
    for d in range(n_orb):
        at = lax.rem(me + d, n_orb)
        term[pl.ds(at, 1)] = start[d][...][None]
        for t in range(rowblocks * per):
            for half in range(2):
                rows = slice((2 * t + half) * CHUNK, (2 * t + half + 1) * CHUNK)
                pot[pl.ds(at * rowblocks + t // per, 1), :, (t % per) * CHUNK:(t % per + 1) * CHUNK,
                    half * LANES:(half + 1) * LANES] = found[d][:, rows, :][None]
    for j in range(own):
        blocks = [term[r // rowblocks, j, (r % rowblocks) * BLOCK:(r % rowblocks + 1) * BLOCK] for r in range(ROWBLK)]
        sums = [jnp.zeros(blocks[0].shape, jnp.float32)] * ROWBLK
        begin = blocks
        for degree in range(1, TAYLOR + 1):
            after = []
            for r in range(ROWBLK):
                right = jnp.concatenate([blocks[c] for c in column_order(r)], axis=0)
                product = jnp.dot(pot[r, j], right, preferred_element_type=jnp.float32)
                after.append((product / degree).astype(jnp.bfloat16))
            blocks = after
            sums = [s + b.astype(jnp.float32) for s, b in zip(sums, blocks)]
        for r in range(ROWBLK):
            moved = begin[r].astype(jnp.float32) + sums[r]
            total[r // rowblocks, j, (r % rowblocks) * BLOCK:(r % rowblocks + 1) * BLOCK] = moved.astype(jnp.bfloat16)
    mine = total[pl.ds(me, 1)][0]
    at = lax.broadcasted_iota(jnp.int32, (CHUNK, LANES), 0)
    high, middle, low = (part.astype(jnp.float32) for part in split(energy_ref[...]))
    tile = jnp.where(at == 0, high, jnp.where(at == 1, middle, jnp.where(at == 2, low, 0.0)))
    moved_ref[:own * half_rows] = mine.reshape(own * half_rows, mine.shape[2])
    moved_ref[own * half_rows:] = tile.astype(jnp.bfloat16)


def series_call(found, start, energy):
    n_orb = len(found)
    own, half_rows, nocc = start[0].shape
    return pl.pallas_call(
        functools.partial(series_kernel, n_orb),
        out_shape=pltpu.VMEM((own * half_rows + CHUNK, nocc), jnp.bfloat16),
        scratch_shapes=[
            pltpu.VMEM((ROWBLK, own, BLOCK, 2 * LANES), jnp.bfloat16),
            pltpu.VMEM((n_orb, own, half_rows, nocc), jnp.bfloat16),
            pltpu.VMEM((n_orb, own, half_rows, nocc), jnp.bfloat16),
        ],
        cost_estimate=FREE,
        compiler_params=params(16),
        name="series",
    )(*in_vmem(*found, *start, energy))


def place_kernel(layout, *refs):
    nz, plane, own = layout
    near, far = refs[:plane], refs[plane:2 * plane]
    out, energy_ref = refs[2 * plane:]
    me = lax.axis_index("chol")
    rows = out.shape[1]
    energy = jnp.zeros((CHUNK, LANES), jnp.float32)
    for dp in range(plane):
        for dz in range(nz):
            z = hop(lax.div(me, plane), -dz if nz & (nz - 1) else dz, nz)
            p = hop(lax.rem(me, plane), -dp if plane & (plane - 1) else dp, plane)
            piece = far[dp].at[dz - 1] if dz else near[dp]
            for j in range(own):
                out[(z * plane + p) * own + j] = piece[j * rows:(j + 1) * rows]
            energy = energy + piece[own * rows:].astype(jnp.float32)
    energy_ref[...] = (energy[0:1] + energy[1:2] + energy[2:3])[:, :energy_ref.shape[1]]


def place_call(layout, near, far):
    nz, plane, own = layout
    walk = nz * plane * own
    rows = (near[0].shape[0] - CHUNK) // own
    return pl.pallas_call(
        functools.partial(place_kernel, layout),
        out_shape=[
            jax.ShapeDtypeStruct((walk, rows, near[0].shape[1]), jnp.bfloat16),
            jax.ShapeDtypeStruct((1, walk), jnp.float32),
        ],
        cost_estimate=FREE,
        compiler_params=params(16),
        name="place_walkers",
    )(*in_vmem(*near, *far))


def per_device(chol_vals, chol_cols, greens, walkers, fields):
    vectors, rowblocks = chol_vals.shape[:2]
    walk, half_rows = greens.shape[:2]
    chips = lax.axis_size("chol")
    n_orb = lax.axis_size("orb")
    plane = 4 if chips % 4 == 0 else 1
    nz = chips // plane
    own = walk // chips
    layout = (nz, plane, own)
    step_factor = 72.0 / float(vectors * chips * BLOCK) ** 0.5

    def to_plane(a, dp):
        return lax.ppermute(a, "chol", [(c, (c // plane) * plane + hop(c % plane, dp, plane)) for c in range(chips)])

    def to_z(a, dz):
        return lax.ppermute(a, "chol", [(c, hop(c // plane, dz, nz) * plane + c % plane) for c in range(chips)])

    def around_orb(a):
        return [a] + [lax.ppermute(a, "orb", [((c + d) % n_orb, c) for c in range(n_orb)]) for d in range(1, n_orb)]

    cols = jnp.transpose(chol_cols, (1, 2, 0))
    turned, partial_bias, mine, cols = bias_call(chol_vals, greens, walkers, cols, own)
    start = around_orb(mine)
    bias, *others = around_orb(partial_bias)
    start, others = lax.optimization_barrier((start, others))

    total_steps = rowblocks * BLOCK // CHUNK
    early_steps = total_steps // 8
    late_steps = total_steps - early_steps
    fields_t = fields.T
    def all_plane(arrays):
        return [to_plane(arrays[dp - 1], dp) for dp in reversed(range(1, plane))]

    z_order = [*range(2, nz), 1]

    def all_z(arrays):
        return [to_z(arrays[dz - 1], dz) for dz in z_order]

    late, energy = potential_call(early_steps, late_steps, layout, True, fields_t, bias, others, cols, turned)
    far, near = late[:plane], late[plane:]
    early, _ = potential_call(0, early_steps, layout, False, fields_t, bias, others, cols, turned)
    early_came = all_z(early[1:])
    merged = merge_call([early[0], *early_came], near)
    far_came = all_z(sum_call([far[0], *all_plane(far[1:])], merged[:1]))
    found = finish_call(step_factor, far_came, [merged[0], *all_plane(merged[1:])])

    piece = series_call(around_orb(found), start, energy)
    near = [piece, *(to_plane(piece, dp) for dp in range(1, plane))]
    came = all_z([piece] * (nz - 1))
    pieces, *near[1:] = stack_call(near[1:], came[::-1], [dz - 1 for dz in z_order[::-1]])
    far = {dp: to_plane(pieces, dp) for dp in reversed(range(1, plane))}
    moved, energy = place_call(layout, near, [pieces, *(far[dp] for dp in range(1, plane))])
    return moved, energy.reshape(walk)


def solution(mesh):
    in_specs = (
        P("chol", "orb", None, None),
        P("chol", "orb", None),
        P("walker", "orb", None),
        P("walker", "orb", None),
        P("chol", "walker"),
    )
    out_specs = (P("walker", "orb", None), P("walker"))
    return jax.shard_map(
        per_device, mesh=mesh, in_specs=in_specs, out_specs=out_specs, check_vma=False
    )
```

```python
import functools

import jax
import jax.numpy as jnp
from jax import lax
from jax.experimental import pallas as pl
from jax.experimental.pallas import tpu as pltpu
from jax.sharding import PartitionSpec as P

BLOCK = 64
TAYLOR = 4
ROWBLK = 4
LANES = 2 * BLOCK
CHUNK = 16
EXTRA = 8
MIB = 1024 * 1024


FREE = pl.CostEstimate(flops=0, bytes_accessed=0, transcendentals=0)


def params(mib):
    return pltpu.CompilerParams(vmem_limit_bytes=mib * MIB)


def split(value):
    parts = []
    for _ in range(3):
        parts.append(value.astype(jnp.bfloat16))
        value = value - parts[-1].astype(jnp.float32)
    return parts


def in_vmem(*arrays):
    return [pltpu.with_memory_space_constraint(a, pltpu.VMEM) for a in arrays]


def in_hbm(*arrays):
    return [pltpu.with_memory_space_constraint(a, pltpu.HBM) for a in arrays]


def hop(at, distance, count):
    return at ^ distance if count & (count - 1) == 0 else (at + distance) % count


def swap_matrix():
    to = lax.broadcasted_iota(jnp.int32, (CHUNK * CHUNK, CHUNK * CHUNK), 0)
    at = lax.broadcasted_iota(jnp.int32, (CHUNK * CHUNK, CHUNK * CHUNK), 1)
    same = (to // CHUNK == at % CHUNK) & (to % CHUNK == at // CHUNK)
    return same.astype(jnp.float32).astype(jnp.bfloat16)


def column_order(row):
    other = 2 - 2 * (row // 2)
    return row, row + 1 - 2 * (row % 2), other, other + 1


def slot_masks(cols, row):
    return [cols == column for column in column_order(row)[1:]]


def bias_kernel(vals_hbm, greens_hbm, walkers_hbm, cols_hbm, turned_ref, bias_ref, mine_ref, cols_ref, vals, greens, swap, gs,
                acc, vsem, gsem, wsem, csem):
    total_steps, vectors = turned_ref.shape[:2]
    walk = bias_ref.shape[0]
    steps = BLOCK // CHUNK

    def copies(t):
        rows = pl.ds(lax.rem(t, steps) * CHUNK, CHUNK)
        return (
            pltpu.make_async_copy(vals_hbm.at[:, lax.div(t, steps), rows, :], vals.at[t], vsem.at[t]),
            pltpu.make_async_copy(greens_hbm.at[:, pl.ds(t * CHUNK, CHUNK), :], greens.at[t], gsem.at[t]),
        )

    def begin(t, carry):
        for copy in copies(t):
            copy.start()
        return carry

    own = mine_ref.shape[0]
    take = pltpu.make_async_copy(walkers_hbm.at[pl.ds(lax.axis_index("chol") * own, own)], mine_ref, wsem)
    take.start()
    take_cols = pltpu.make_async_copy(cols_hbm, cols_ref, csem)
    take_cols.start()
    lax.fori_loop(0, total_steps, begin, 0)
    swap[...] = swap_matrix()
    bias_ref[...] = jnp.zeros_like(bias_ref)
    first = lax.broadcasted_iota(jnp.int32, (CHUNK * CHUNK, LANES), 1) < BLOCK

    def step(t, carry):
        for copy in copies(t):
            copy.wait()
        local = lax.div(t, steps)
        row = lax.axis_index("orb") * cols_ref.shape[0] + local
        upper = row // 2 == 1
        odd = row % 2 == 1
        for w in range(0, walk, CHUNK):
            mixed = greens[t, w:w + CHUNK].reshape(CHUNK * CHUNK, 2 * LANES)
            mixed = jnp.dot(swap[...], mixed, preferred_element_type=jnp.float32)
            pair = jnp.where(upper, mixed[:, LANES:], mixed[:, :LANES])
            rest = jnp.where(upper, mixed[:, :LANES], mixed[:, LANES:])
            pair = jnp.where(odd, pltpu.roll(pair, BLOCK, 1), pair)
            pieces = (
                jnp.where(first, pair, 0.0),
                jnp.where(first, 0.0, pair),
                jnp.where(first, 0.0, pltpu.roll(rest, BLOCK, 1)),
                jnp.where(first, 0.0, rest),
            )
            for k, piece in enumerate(pieces):
                piece = piece.astype(jnp.bfloat16)
                for i in range(CHUNK):
                    gs[k * walk + w:k * walk + w + CHUNK, i * LANES:(i + 1) * LANES] = piece[i * CHUNK:(i + 1) * CHUNK]
        for g in range(0, vectors, 2 * CHUNK):
            both = [vals[t, g + side * CHUNK:g + (side + 1) * CHUNK].reshape(CHUNK * CHUNK, LANES) for side in range(2)]
            both = jnp.dot(swap[...], jnp.concatenate(both, axis=1), preferred_element_type=jnp.float32)
            both = both.astype(jnp.bfloat16)
            for i in range(CHUNK):
                for side in range(2):
                    turned_ref[t, g + side * CHUNK:g + (side + 1) * CHUNK, i * LANES:(i + 1) * LANES] = (
                        both[i * CHUNK:(i + 1) * CHUNK, side * LANES:(side + 1) * LANES]
                    )
        part = lax.dot_general(
            gs[...], turned_ref[t], (((1,), (1,)), ((), ())), preferred_element_type=jnp.float32
        )
        begins = lax.rem(t, steps) == 0
        acc[...] = jnp.where(begins, 0.0, acc[...]) + part

        @pl.when(lax.rem(t, steps) == steps - 1)
        def _():
            flat = acc[...]
            total = flat[0:walk]
            cols = cols_ref[local, 1:2, :]
            for k, mask in enumerate(slot_masks(cols, row)):
                total = total + jnp.where(mask, flat[(k + 1) * walk:(k + 2) * walk], 0.0)
            bias_ref[...] += total

        return carry

    acc[...] = jnp.zeros_like(acc)
    take_cols.wait()
    lax.fori_loop(0, total_steps, step, 0)
    take.wait()


def bias_call(vals, greens, walkers, cols, own):
    vectors, rowblocks = vals.shape[:2]
    walk, half_rows, norb = greens.shape
    steps = half_rows // CHUNK
    wide = CHUNK * LANES
    return pl.pallas_call(
        bias_kernel,
        in_specs=[
            *[pl.BlockSpec(memory_space=pl.ANY)] * 4,
        ],
        out_specs=[pl.BlockSpec(memory_space=pltpu.VMEM)] * 4,
        out_shape=[
            pltpu.VMEM((steps, vectors, wide), jnp.bfloat16),
            pltpu.VMEM((walk, vectors), jnp.float32),
            pltpu.VMEM((own, *walkers.shape[1:]), jnp.bfloat16),
            pltpu.VMEM(cols.shape, jnp.int32),
        ],
        scratch_shapes=[
            pltpu.VMEM((steps, vectors, CHUNK, LANES), jnp.bfloat16),
            pltpu.VMEM((steps, walk, CHUNK, norb), jnp.bfloat16),
            pltpu.VMEM((CHUNK * CHUNK, CHUNK * CHUNK), jnp.bfloat16),
            pltpu.VMEM((4 * walk, wide), jnp.bfloat16),
            pltpu.VMEM((4 * walk, vectors), jnp.float32),
            pltpu.SemaphoreType.DMA((steps,)),
            pltpu.SemaphoreType.DMA((steps,)),
            pltpu.SemaphoreType.DMA,
            pltpu.SemaphoreType.DMA,
        ],
        cost_estimate=FREE,
        compiler_params=params(24),
        name="force_bias",
    )(*in_hbm(vals, greens, walkers, cols))


def potential_kernel(start, steps, layout, by_plane, fields_ref, own_ref, *refs):
    nz, plane, own = layout
    others = refs[:lax.axis_size("orb") - 1]
    cols_ref, turned_ref = refs[len(others):len(others) + 2]
    groups = 2 * plane if by_plane else nz
    outs = refs[len(others) + 2:len(others) + 2 + groups]
    energy_ref, s_ref, swap = refs[len(others) + 2 + groups:]
    walk, vectors = fields_ref.shape
    rowblocks = cols_ref.shape[0]

    me = lax.axis_index("chol")
    bias = own_ref[...]
    for other in others:
        bias = bias + other[...]
    energy = 0.5 * jnp.sum(bias * bias, axis=1, keepdims=True)
    energy_ref[...] = jnp.zeros_like(energy_ref)
    energy_ref[:, :walk] = jnp.broadcast_to(energy, (walk, LANES)).T[:CHUNK]
    shifted = (fields_ref[...] - bias).astype(jnp.bfloat16)
    at = lax.broadcasted_iota(jnp.int32, (walk, walk), 0)
    source = lax.broadcasted_iota(jnp.int32, (walk, walk), 1)
    chip = at // own
    z = hop(me // plane, chip // plane, nz)
    p = hop(me % plane, chip % plane, plane)
    wanted = (z * plane + p) * own + at % own
    pick = (wanted == source).astype(jnp.float32).astype(jnp.bfloat16)
    ordered = jnp.dot(pick, shifted, preferred_element_type=jnp.float32)
    for local in range(rowblocks):
        row = lax.axis_index("orb") * rowblocks + local
        s_ref[local, 0:walk] = ordered.astype(jnp.bfloat16)
        for k, mask in enumerate(slot_masks(cols_ref[local, 1:2, :], row)):
            s_ref[local, (k + 1) * walk:(k + 2) * walk] = jnp.where(mask, ordered, 0.0).astype(jnp.bfloat16)
    swap[...] = swap_matrix()
    first = lax.broadcasted_iota(jnp.int32, (walk, LANES), 1) < BLOCK

    def step(t, carry):
        left = s_ref[lax.div(start + t, BLOCK // CHUNK)]
        tiles = []
        for i in range(0, CHUNK, 2):
            both = jnp.dot(
                left, turned_ref[start + t, :, i * LANES:(i + 2) * LANES], preferred_element_type=jnp.float32
            )
            for side in range(2):
                out = both[:, side * LANES:(side + 1) * LANES]
                near = jnp.where(first, out[0:walk], out[walk:2 * walk])
                far = jnp.where(first, pltpu.roll(out[2 * walk:3 * walk], BLOCK, 1), out[3 * walk:])
                tiles.append(jnp.concatenate([near, far], axis=1).astype(jnp.bfloat16))
        for w0 in range(0, walk, CHUNK):
            mixed = jnp.concatenate([tile[w0:w0 + CHUNK] for tile in tiles], axis=0)
            mixed = jnp.dot(swap[...], mixed, preferred_element_type=jnp.float32).astype(jnp.bfloat16)
            for w in range(CHUNK):
                chip, j = (w0 + w) // own, (w0 + w) % own
                dz, dp = chip // plane, chip % plane
                if not by_plane:
                    out, inner = outs[dz], (dp,)
                elif dz:
                    out, inner = outs[dp], (dz - 1,)
                else:
                    out, inner = outs[plane + dp], ()
                for half in range(2):
                    rows = pl.ds(pl.multiple_of((2 * t + half) * CHUNK, CHUNK), CHUNK)
                    out[(*inner, j, rows)] = mixed[w * CHUNK:(w + 1) * CHUNK, half * LANES:(half + 1) * LANES]
        return carry

    lax.fori_loop(0, steps // 2, lambda t, carry: step(2 * t + 1, step(2 * t, carry)), 0)
    if steps % 2:
        step(steps - 1, 0)


def potential_call(start, steps, layout, by_plane, fields, bias, others, cols, turned):
    nz, plane, own = layout
    walk, vectors = fields.shape
    leading = [(nz - 1,)] * plane + [()] * plane if by_plane else [(plane,)] * nz
    rows = 2 * CHUNK
    *parts, energy = pl.pallas_call(
        functools.partial(potential_kernel, start, steps, layout, by_plane),
        out_shape=[
            *[pltpu.VMEM((*inner, own, steps * rows, LANES), jnp.bfloat16) for inner in leading],
            pltpu.VMEM((CHUNK, LANES), jnp.float32),
        ],
        scratch_shapes=[
            pltpu.VMEM((cols.shape[0], 4 * walk, vectors), jnp.bfloat16),
            pltpu.VMEM((CHUNK * CHUNK, CHUNK * CHUNK), jnp.bfloat16),
        ],
        cost_estimate=FREE,
        compiler_params=params(16),
        name="potential",
    )(fields, *in_vmem(bias, *others, cols, turned))
    return parts, energy


def add(refs, *at):
    total = refs[0][at].astype(jnp.float32)
    for ref in refs[1:]:
        total = total + ref[at].astype(jnp.float32)
    return total


def vmem_call(kernel, name, out_shape, *arrays):
    return pl.pallas_call(
        kernel, out_shape=out_shape, cost_estimate=FREE, compiler_params=params(16), name=name
    )(*in_vmem(*arrays))


def sum_call(arrays, after):
    def kernel(*refs):
        for k, out in enumerate(refs[len(arrays) + len(after):]):
            out[...] = add(refs[:len(arrays)], k).astype(out.dtype)

    out_shape = [pltpu.VMEM(arrays[0].shape[1:], jnp.bfloat16)] * arrays[0].shape[0]
    return vmem_call(kernel, "sum_parts", out_shape, *arrays, *after)


def merge_call(early, near):
    own, rows, lanes = early[0].shape[1:]

    def kernel(*refs):
        early_refs, near_refs, outs = refs[:len(early)], refs[len(early):len(early) + len(near)], refs[-len(near):]
        for k, (ref, out) in enumerate(zip(near_refs, outs)):
            out[:, :rows] = add(early_refs, k).astype(out.dtype)
            out[:, rows:] = ref[...]

    out_shape = [pltpu.VMEM((own, rows + near[0].shape[1], lanes), jnp.bfloat16)] * len(near)
    return vmem_call(kernel, "merge_parts", out_shape, *early, *near)


def finish_call(factor, far, merged):
    rows = merged[0].shape[1] - far[0].shape[1]

    def kernel(*refs):
        far_refs, merged_refs, out = refs[:len(far)], refs[len(far):-1], refs[-1]
        total = add(merged_refs, slice(None), slice(0, rows))
        out[:, :rows] = (factor * total).astype(out.dtype)
        total = add(merged_refs, slice(None), slice(rows, None)) + add(far_refs, Ellipsis)
        out[:, rows:] = (factor * total).astype(out.dtype)

    return vmem_call(kernel, "finish", pltpu.VMEM(merged[0].shape, jnp.bfloat16), *far, *merged)


def stack_call(near, pieces, slots):
    def kernel(*refs):
        ins, outs = refs[:len(pieces) + len(near)], refs[len(pieces) + len(near):]
        for ref, slot in zip(ins[len(near):], slots):
            outs[0][slot] = ref[...]
        for ref, out in zip(ins, outs[1:]):
            out[...] = ref[...]

    one = pltpu.VMEM(pieces[0].shape, jnp.bfloat16)
    out_shape = [pltpu.VMEM((len(pieces), *pieces[0].shape), jnp.bfloat16)] + [one] * len(near)
    return vmem_call(kernel, "stack_pieces", out_shape, *near, *pieces)


def series_kernel(n_orb, *refs):
    found, start = refs[:n_orb], refs[n_orb:2 * n_orb]
    energy_ref, moved_ref, pot, term, total = refs[2 * n_orb:]
    me = lax.axis_index("orb")
    own, half_rows = start[0].shape[:2]
    rowblocks = half_rows // BLOCK
    per = BLOCK // CHUNK
    for d in range(n_orb):
        at = lax.rem(me + d, n_orb)
        term[pl.ds(at, 1)] = start[d][...][None]
        for t in range(rowblocks * per):
            for half in range(2):
                rows = slice((2 * t + half) * CHUNK, (2 * t + half + 1) * CHUNK)
                pot[pl.ds(at * rowblocks + t // per, 1), :, (t % per) * CHUNK:(t % per + 1) * CHUNK,
                    half * LANES:(half + 1) * LANES] = found[d][:, rows, :][None]
    for j in range(own):
        blocks = [term[r // rowblocks, j, (r % rowblocks) * BLOCK:(r % rowblocks + 1) * BLOCK] for r in range(ROWBLK)]
        sums = [jnp.zeros(blocks[0].shape, jnp.float32)] * ROWBLK
        begin = blocks
        for degree in range(1, TAYLOR + 1):
            after = []
            for r in range(ROWBLK):
                right = jnp.concatenate([blocks[c] for c in column_order(r)], axis=0)
                product = jnp.dot(pot[r, j], right, preferred_element_type=jnp.float32)
                after.append((product / degree).astype(jnp.bfloat16))
            blocks = after
            sums = [s + b.astype(jnp.float32) for s, b in zip(sums, blocks)]
        for r in range(ROWBLK):
            moved = begin[r].astype(jnp.float32) + sums[r]
            total[r // rowblocks, j, (r % rowblocks) * BLOCK:(r % rowblocks + 1) * BLOCK] = moved.astype(jnp.bfloat16)
    mine = total[pl.ds(me, 1)][0]
    at = lax.broadcasted_iota(jnp.int32, (EXTRA, LANES), 0)
    high, middle, low = (part.astype(jnp.float32) for part in split(energy_ref[:EXTRA]))
    tile = jnp.where(at == 0, high, jnp.where(at == 1, middle, jnp.where(at == 2, low, 0.0)))
    moved_ref[:own * half_rows] = mine.reshape(own * half_rows, mine.shape[2])
    moved_ref[own * half_rows:] = tile.astype(jnp.bfloat16)


def series_call(found, start, energy):
    n_orb = len(found)
    own, half_rows, nocc = start[0].shape
    return pl.pallas_call(
        functools.partial(series_kernel, n_orb),
        out_shape=pltpu.VMEM((own * half_rows + EXTRA, nocc), jnp.bfloat16),
        scratch_shapes=[
            pltpu.VMEM((ROWBLK, own, BLOCK, 2 * LANES), jnp.bfloat16),
            pltpu.VMEM((n_orb, own, half_rows, nocc), jnp.bfloat16),
            pltpu.VMEM((n_orb, own, half_rows, nocc), jnp.bfloat16),
        ],
        cost_estimate=FREE,
        compiler_params=params(16),
        name="series",
    )(*in_vmem(*found, *start, energy))


def place_kernel(layout, *refs):
    nz, plane, own = layout
    near, far = refs[:plane], refs[plane:2 * plane]
    out, energy_ref, sems = refs[2 * plane:]
    me = lax.axis_index("chol")
    rows = out.shape[1]
    copies = []
    for dp in range(plane):
        for dz in range(nz):
            z = hop(lax.div(me, plane), -dz if nz & (nz - 1) else dz, nz)
            p = hop(lax.rem(me, plane), -dp if plane & (plane - 1) else dp, plane)
            piece = far[dp].at[dz - 1] if dz else near[dp]
            for j in range(own):
                copy = pltpu.make_async_copy(
                    piece.at[pl.ds(j * rows, rows)], out.at[(z * plane + p) * own + j], sems.at[len(copies)]
                )
                copy.start()
                copies.append(copy)
    energy = jnp.zeros((EXTRA, LANES), jnp.float32)
    for dp in range(plane):
        for dz in range(nz):
            piece = far[dp].at[dz - 1] if dz else near[dp]
            energy = energy + piece[own * rows:].astype(jnp.float32)
    energy_ref[...] = (energy[0:1] + energy[1:2] + energy[2:3])[:, :energy_ref.shape[1]]
    for copy in copies:
        copy.wait()


def place_call(layout, near, far):
    nz, plane, own = layout
    walk = nz * plane * own
    rows = (near[0].shape[0] - EXTRA) // own
    return pl.pallas_call(
        functools.partial(place_kernel, layout),
        out_specs=[pl.BlockSpec(memory_space=pl.ANY), pl.BlockSpec(memory_space=pltpu.VMEM)],
        out_shape=[
            pltpu.HBM((walk, rows, near[0].shape[1]), jnp.bfloat16),
            jax.ShapeDtypeStruct((1, walk), jnp.float32),
        ],
        scratch_shapes=[pltpu.SemaphoreType.DMA((walk,))],
        cost_estimate=FREE,
        compiler_params=params(16),
        name="place_walkers",
    )(*in_vmem(*near, *far))


def per_device(chol_vals, chol_cols, greens, walkers, fields):
    vectors, rowblocks = chol_vals.shape[:2]
    walk, half_rows = greens.shape[:2]
    chips = lax.axis_size("chol")
    n_orb = lax.axis_size("orb")
    plane = 4 if chips % 4 == 0 else 1
    nz = chips // plane
    own = walk // chips
    layout = (nz, plane, own)
    step_factor = 72.0 / float(vectors * chips * BLOCK) ** 0.5

    def to_plane(a, dp):
        return lax.ppermute(a, "chol", [(c, (c // plane) * plane + hop(c % plane, dp, plane)) for c in range(chips)])

    def to_z(a, dz):
        return lax.ppermute(a, "chol", [(c, hop(c // plane, dz, nz) * plane + c % plane) for c in range(chips)])

    def around_orb(a):
        return [a] + [lax.ppermute(a, "orb", [((c + d) % n_orb, c) for c in range(n_orb)]) for d in range(1, n_orb)]

    cols = jnp.transpose(chol_cols, (1, 2, 0))
    turned, partial_bias, mine, cols = bias_call(chol_vals, greens, walkers, cols, own)
    start = around_orb(mine)
    bias, *others = around_orb(partial_bias)
    start, others = lax.optimization_barrier((start, others))

    total_steps = rowblocks * BLOCK // CHUNK
    early_steps = total_steps // 8
    late_steps = total_steps - early_steps
    fields_t = fields.T
    def all_plane(arrays):
        return [to_plane(arrays[dp - 1], dp) for dp in reversed(range(1, plane))]

    z_order = [*range(2, nz), 1]

    def all_z(arrays):
        return [to_z(arrays[dz - 1], dz) for dz in z_order]

    late, energy = potential_call(early_steps, late_steps, layout, True, fields_t, bias, others, cols, turned)
    far, near = late[:plane], late[plane:]
    early, _ = potential_call(0, early_steps, layout, False, fields_t, bias, others, cols, turned)
    early_came = all_z(early[1:])
    merged = merge_call([early[0], *early_came], near)
    far_came = all_z(sum_call([far[0], *all_plane(far[1:])], merged[:1]))
    found = finish_call(step_factor, far_came, [merged[0], *all_plane(merged[1:])])

    piece = series_call(around_orb(found), start, energy)
    near = [piece, *(to_plane(piece, dp) for dp in range(1, plane))]
    came = all_z([piece] * (nz - 1))
    pieces, *near[2:] = stack_call(near[2:], came[::-1], [dz - 1 for dz in z_order[::-1]])
    far = {dp: to_plane(pieces, dp) for dp in reversed(range(1, plane))}
    moved, energy = place_call(layout, near, [pieces, *(far[dp] for dp in range(1, plane))])
    return moved, energy.reshape(walk)


def solution(mesh):
    in_specs = (
        P("chol", "orb", None, None),
        P("chol", "orb", None),
        P("walker", "orb", None),
        P("walker", "orb", None),
        P("chol", "walker"),
    )
    out_specs = (P("walker", "orb", None), P("walker"))
    return jax.shard_map(
        per_device, mesh=mesh, in_specs=in_specs, out_specs=out_specs, check_vma=False
    )
```

```python
import functools

import jax
import jax.numpy as jnp
from jax import lax
from jax.experimental import pallas as pl
from jax.experimental.pallas import tpu as pltpu
from jax.sharding import PartitionSpec as P

BLOCK = 64
TAYLOR = 4
ROWBLK = 4
LANES = 2 * BLOCK
CHUNK = 16
EXTRA = 8
MIB = 1024 * 1024


FREE = pl.CostEstimate(flops=0, bytes_accessed=0, transcendentals=0)


def params(mib):
    return pltpu.CompilerParams(vmem_limit_bytes=mib * MIB)


def split(value):
    parts = []
    for _ in range(3):
        parts.append(value.astype(jnp.bfloat16))
        value = value - parts[-1].astype(jnp.float32)
    return parts


def in_vmem(*arrays):
    return [pltpu.with_memory_space_constraint(a, pltpu.VMEM) for a in arrays]


def in_hbm(*arrays):
    return [pltpu.with_memory_space_constraint(a, pltpu.HBM) for a in arrays]


def hop(at, distance, count):
    return at ^ distance if count & (count - 1) == 0 else (at + distance) % count


def swap_matrix():
    to = lax.broadcasted_iota(jnp.int32, (CHUNK * CHUNK, CHUNK * CHUNK), 0)
    at = lax.broadcasted_iota(jnp.int32, (CHUNK * CHUNK, CHUNK * CHUNK), 1)
    same = (to // CHUNK == at % CHUNK) & (to % CHUNK == at // CHUNK)
    return same.astype(jnp.float32).astype(jnp.bfloat16)


def column_order(row):
    other = 2 - 2 * (row // 2)
    return row, row + 1 - 2 * (row % 2), other, other + 1


def slot_masks(cols, row):
    return [cols == column for column in column_order(row)[1:]]


def bias_kernel(vals_hbm, greens_hbm, walkers_hbm, cols_hbm, turned_ref, bias_ref, mine_ref, cols_ref, vals, greens, swap, gs,
                acc, vsem, gsem, wsem, csem):
    total_steps, vectors = turned_ref.shape[:2]
    walk = bias_ref.shape[0]
    steps = BLOCK // CHUNK

    def copies(t):
        rows = pl.ds(lax.rem(t, steps) * CHUNK, CHUNK)
        return (
            pltpu.make_async_copy(vals_hbm.at[:, lax.div(t, steps), rows, :], vals.at[t], vsem.at[t]),
            pltpu.make_async_copy(greens_hbm.at[:, pl.ds(t * CHUNK, CHUNK), :], greens.at[t], gsem.at[t]),
        )

    def begin(t, carry):
        for copy in copies(t):
            copy.start()
        return carry

    own = mine_ref.shape[0]
    take = pltpu.make_async_copy(walkers_hbm.at[pl.ds(lax.axis_index("chol") * own, own)], mine_ref, wsem)
    take.start()
    take_cols = pltpu.make_async_copy(cols_hbm, cols_ref, csem)
    take_cols.start()
    lax.fori_loop(0, total_steps, begin, 0)
    swap[...] = swap_matrix()
    bias_ref[...] = jnp.zeros_like(bias_ref)
    first = lax.broadcasted_iota(jnp.int32, (CHUNK * CHUNK, LANES), 1) < BLOCK

    def step(t, side):
        for copy in copies(t):
            copy.wait()
        local = lax.div(t, steps)
        row = lax.axis_index("orb") * cols_ref.shape[0] + local
        upper = row // 2 == 1
        odd = row % 2 == 1
        for w in range(0, walk, CHUNK):
            mixed = greens[t, w:w + CHUNK].reshape(CHUNK * CHUNK, 2 * LANES)
            mixed = jnp.dot(swap[...], mixed, preferred_element_type=jnp.float32)
            pair = jnp.where(upper, mixed[:, LANES:], mixed[:, :LANES])
            rest = jnp.where(upper, mixed[:, :LANES], mixed[:, LANES:])
            pair = jnp.where(odd, pltpu.roll(pair, BLOCK, 1), pair)
            pieces = (
                jnp.where(first, pair, 0.0),
                jnp.where(first, 0.0, pair),
                jnp.where(first, 0.0, pltpu.roll(rest, BLOCK, 1)),
                jnp.where(first, 0.0, rest),
            )
            for k, piece in enumerate(pieces):
                piece = piece.astype(jnp.bfloat16)
                for i in range(CHUNK):
                    gs[side, k * walk + w:k * walk + w + CHUNK, i * LANES:(i + 1) * LANES] = (
                        piece[i * CHUNK:(i + 1) * CHUNK]
                    )
        for g in range(0, vectors, 2 * CHUNK):
            both = [vals[t, g + k * CHUNK:g + (k + 1) * CHUNK].reshape(CHUNK * CHUNK, LANES) for k in range(2)]
            both = jnp.dot(swap[...], jnp.concatenate(both, axis=1), preferred_element_type=jnp.float32)
            both = both.astype(jnp.bfloat16)
            for i in range(CHUNK):
                for k in range(2):
                    turned_ref[t, g + k * CHUNK:g + (k + 1) * CHUNK, i * LANES:(i + 1) * LANES] = (
                        both[i * CHUNK:(i + 1) * CHUNK, k * LANES:(k + 1) * LANES]
                    )
        part = lax.dot_general(
            turned_ref[t], gs[side], (((1,), (1,)), ((), ())), preferred_element_type=jnp.float32
        )
        begins = lax.rem(t, steps) == 0
        acc[...] = jnp.where(begins, 0.0, acc[...]) + part

        @pl.when(lax.rem(t, steps) == steps - 1)
        def _():
            flat = acc[...].T
            total = flat[0:walk]
            cols = cols_ref[local, 1:2, :]
            for k, mask in enumerate(slot_masks(cols, row)):
                total = total + jnp.where(mask, flat[(k + 1) * walk:(k + 2) * walk], 0.0)
            bias_ref[...] += total

    def pair(t, carry):
        step(2 * t, 0)
        step(2 * t + 1, 1)
        return carry

    acc[...] = jnp.zeros_like(acc)
    take_cols.wait()
    lax.fori_loop(0, total_steps // 2, pair, 0)
    take.wait()


def bias_call(vals, greens, walkers, cols, own):
    vectors, rowblocks = vals.shape[:2]
    walk, half_rows, norb = greens.shape
    steps = half_rows // CHUNK
    wide = CHUNK * LANES
    return pl.pallas_call(
        bias_kernel,
        in_specs=[
            *[pl.BlockSpec(memory_space=pl.ANY)] * 4,
        ],
        out_specs=[pl.BlockSpec(memory_space=pltpu.VMEM)] * 4,
        out_shape=[
            pltpu.VMEM((steps, vectors, wide), jnp.bfloat16),
            pltpu.VMEM((walk, vectors), jnp.float32),
            pltpu.VMEM((own, *walkers.shape[1:]), jnp.bfloat16),
            pltpu.VMEM(cols.shape, jnp.int32),
        ],
        scratch_shapes=[
            pltpu.VMEM((steps, vectors, CHUNK, LANES), jnp.bfloat16),
            pltpu.VMEM((steps, walk, CHUNK, norb), jnp.bfloat16),
            pltpu.VMEM((CHUNK * CHUNK, CHUNK * CHUNK), jnp.bfloat16),
            pltpu.VMEM((2, 4 * walk, wide), jnp.bfloat16),
            pltpu.VMEM((vectors, 4 * walk), jnp.float32),
            pltpu.SemaphoreType.DMA((steps,)),
            pltpu.SemaphoreType.DMA((steps,)),
            pltpu.SemaphoreType.DMA,
            pltpu.SemaphoreType.DMA,
        ],
        cost_estimate=FREE,
        compiler_params=params(24),
        name="force_bias",
    )(*in_hbm(vals, greens, walkers, cols))


def potential_kernel(begin, end, layout, by_plane, fields_ref, own_ref, *refs):
    nz, plane, own = layout
    others = refs[:lax.axis_size("orb") - 1]
    cols_ref, turned_ref = refs[len(others):len(others) + 2]
    groups = 2 * plane if by_plane else nz
    outs = refs[len(others) + 2:len(others) + 2 + groups]
    energy_ref, s_ref, swap = refs[len(others) + 2 + groups:]
    walk, vectors = fields_ref.shape
    rowblocks = cols_ref.shape[0]

    me = lax.axis_index("chol")
    bias = own_ref[...]
    for other in others:
        bias = bias + other[...]
    energy = 0.5 * jnp.sum(bias * bias, axis=1, keepdims=True)
    energy_ref[...] = jnp.zeros_like(energy_ref)
    energy_ref[:, :walk] = jnp.broadcast_to(energy, (walk, LANES)).T[:CHUNK]
    shifted = (fields_ref[...] - bias).astype(jnp.bfloat16)
    at = lax.broadcasted_iota(jnp.int32, (walk, walk), 0)
    source = lax.broadcasted_iota(jnp.int32, (walk, walk), 1)
    chip = at // own
    z = hop(me // plane, chip // plane, nz)
    p = hop(me % plane, chip % plane, plane)
    wanted = (z * plane + p) * own + at % own
    pick = (wanted == source).astype(jnp.float32).astype(jnp.bfloat16)
    ordered = jnp.dot(pick, shifted, preferred_element_type=jnp.float32)
    for local in range(rowblocks):
        row = lax.axis_index("orb") * rowblocks + local
        s_ref[local, 0:walk] = ordered.astype(jnp.bfloat16)
        for k, mask in enumerate(slot_masks(cols_ref[local, 1:2, :], row)):
            s_ref[local, (k + 1) * walk:(k + 2) * walk] = jnp.where(mask, ordered, 0.0).astype(jnp.bfloat16)
    swap[...] = swap_matrix()
    first = lax.broadcasted_iota(jnp.int32, (walk, LANES), 1) < BLOCK

    def step(t, halves=(0, 1)):
        left = s_ref[lax.div(t, BLOCK // CHUNK)]
        tiles = []
        for i in range(0, CHUNK, 2):
            both = jnp.dot(left, turned_ref[t, :, i * LANES:(i + 2) * LANES], preferred_element_type=jnp.float32)
            for side in range(2):
                out = both[:, side * LANES:(side + 1) * LANES]
                near = jnp.where(first, out[0:walk], out[walk:2 * walk])
                far = jnp.where(first, pltpu.roll(out[2 * walk:3 * walk], BLOCK, 1), out[3 * walk:])
                wanted = [(near, far)[half] for half in halves]
                tiles.append(jnp.concatenate(wanted, axis=1).astype(jnp.bfloat16))
        for w0 in range(0, walk, CHUNK):
            mixed = jnp.concatenate([tile[w0:w0 + CHUNK] for tile in tiles], axis=0)
            mixed = jnp.dot(swap[...], mixed, preferred_element_type=jnp.float32).astype(jnp.bfloat16)
            for w in range(CHUNK):
                chip, j = (w0 + w) // own, (w0 + w) % own
                dz, dp = chip // plane, chip % plane
                if not by_plane:
                    out, inner = outs[dz], (dp,)
                elif dz:
                    out, inner = outs[dp], (dz - 1,)
                else:
                    out, inner = outs[plane + dp], ()
                for k, half in enumerate(halves):
                    at = (2 * t + half - begin) * CHUNK
                    rows = pl.ds(at if isinstance(t, int) else pl.multiple_of(at, CHUNK), CHUNK)
                    out[(*inner, j, rows)] = mixed[w * CHUNK:(w + 1) * CHUNK, k * LANES:(k + 1) * LANES]

    def pair(t, carry):
        step(from_step + 2 * t)
        step(from_step + 2 * t + 1)
        return carry

    from_step, to_step = (begin + 1) // 2, end // 2
    if begin % 2:
        step(begin // 2, (1,))
    lax.fori_loop(0, (to_step - from_step) // 2, pair, 0)
    if (to_step - from_step) % 2:
        step(to_step - 1)
    if end % 2:
        step(end // 2, (0,))


def potential_call(begin, end, layout, by_plane, fields, bias, others, cols, turned):
    nz, plane, own = layout
    walk, vectors = fields.shape
    leading = [(nz - 1,)] * plane + [()] * plane if by_plane else [(plane,)] * nz
    rows = (end - begin) * CHUNK
    *parts, energy = pl.pallas_call(
        functools.partial(potential_kernel, begin, end, layout, by_plane),
        out_shape=[
            *[pltpu.VMEM((*inner, own, rows, LANES), jnp.bfloat16) for inner in leading],
            pltpu.VMEM((CHUNK, LANES), jnp.float32),
        ],
        scratch_shapes=[
            pltpu.VMEM((cols.shape[0], 4 * walk, vectors), jnp.bfloat16),
            pltpu.VMEM((CHUNK * CHUNK, CHUNK * CHUNK), jnp.bfloat16),
        ],
        cost_estimate=FREE,
        compiler_params=params(16),
        name="potential",
    )(fields, *in_vmem(bias, *others, cols, turned))
    return parts, energy


def add(refs, *at):
    total = refs[0][at].astype(jnp.float32)
    for ref in refs[1:]:
        total = total + ref[at].astype(jnp.float32)
    return total


def vmem_call(kernel, name, out_shape, *arrays):
    return pl.pallas_call(
        kernel, out_shape=out_shape, cost_estimate=FREE, compiler_params=params(16), name=name
    )(*in_vmem(*arrays))


def sum_call(arrays, after):
    def kernel(*refs):
        for k, out in enumerate(refs[len(arrays) + len(after):]):
            out[...] = add(refs[:len(arrays)], k).astype(out.dtype)

    out_shape = [pltpu.VMEM(arrays[0].shape[1:], jnp.bfloat16)] * arrays[0].shape[0]
    return vmem_call(kernel, "sum_parts", out_shape, *arrays, *after)


def merge_call(early, near):
    own, rows, lanes = early[0].shape[1:]

    def kernel(*refs):
        early_refs, near_refs, outs = refs[:len(early)], refs[len(early):len(early) + len(near)], refs[-len(near):]
        for k, (ref, out) in enumerate(zip(near_refs, outs)):
            out[:, :rows] = add(early_refs, k).astype(out.dtype)
            out[:, rows:] = ref[...]

    out_shape = [pltpu.VMEM((own, rows + near[0].shape[1], lanes), jnp.bfloat16)] * len(near)
    return vmem_call(kernel, "merge_parts", out_shape, *early, *near)


def finish_call(factor, far, merged):
    rows = merged[0].shape[1] - far[0].shape[1]

    def kernel(*refs):
        far_refs, merged_refs, out = refs[:len(far)], refs[len(far):-1], refs[-1]
        total = add(merged_refs, slice(None), slice(0, rows))
        out[:, :rows] = (factor * total).astype(out.dtype)
        total = add(merged_refs, slice(None), slice(rows, None)) + add(far_refs, Ellipsis)
        out[:, rows:] = (factor * total).astype(out.dtype)

    return vmem_call(kernel, "finish", pltpu.VMEM(merged[0].shape, jnp.bfloat16), *far, *merged)


def stack_call(near, pieces, slots):
    def kernel(*refs):
        ins, outs = refs[:len(pieces) + len(near)], refs[len(pieces) + len(near):]
        for ref, slot in zip(ins[len(near):], slots):
            outs[0][slot] = ref[...]
        for ref, out in zip(ins, outs[1:]):
            out[...] = ref[...]

    one = pltpu.VMEM(pieces[0].shape, jnp.bfloat16)
    out_shape = [pltpu.VMEM((len(pieces), *pieces[0].shape), jnp.bfloat16)] + [one] * len(near)
    return vmem_call(kernel, "stack_pieces", out_shape, *near, *pieces)


def series_kernel(n_orb, *refs):
    found, start = refs[:n_orb], refs[n_orb:2 * n_orb]
    energy_ref, moved_ref, pot, term, total = refs[2 * n_orb:]
    me = lax.axis_index("orb")
    own, half_rows = start[0].shape[:2]
    rowblocks = half_rows // BLOCK
    per = BLOCK // CHUNK
    for d in range(n_orb):
        at = lax.rem(me + d, n_orb)
        term[pl.ds(at, 1)] = start[d][...][None]
        for t in range(rowblocks * per):
            for half in range(2):
                rows = slice((2 * t + half) * CHUNK, (2 * t + half + 1) * CHUNK)
                pot[pl.ds(at * rowblocks + t // per, 1), :, (t % per) * CHUNK:(t % per + 1) * CHUNK,
                    half * LANES:(half + 1) * LANES] = found[d][:, rows, :][None]
    for j in range(own):
        blocks = [term[r // rowblocks, j, (r % rowblocks) * BLOCK:(r % rowblocks + 1) * BLOCK] for r in range(ROWBLK)]
        sums = [jnp.zeros(blocks[0].shape, jnp.float32)] * ROWBLK
        begin = blocks
        for degree in range(1, TAYLOR + 1):
            after = []
            for r in range(ROWBLK):
                right = jnp.concatenate([blocks[c] for c in column_order(r)], axis=0)
                product = jnp.dot(pot[r, j], right, preferred_element_type=jnp.float32)
                after.append((product / degree).astype(jnp.bfloat16))
            blocks = after
            sums = [s + b.astype(jnp.float32) for s, b in zip(sums, blocks)]
        for r in range(ROWBLK):
            moved = begin[r].astype(jnp.float32) + sums[r]
            total[r // rowblocks, j, (r % rowblocks) * BLOCK:(r % rowblocks + 1) * BLOCK] = moved.astype(jnp.bfloat16)
    mine = total[pl.ds(me, 1)][0]
    at = lax.broadcasted_iota(jnp.int32, (EXTRA, LANES), 0)
    high, middle, low = (part.astype(jnp.float32) for part in split(energy_ref[:EXTRA]))
    tile = jnp.where(at == 0, high, jnp.where(at == 1, middle, jnp.where(at == 2, low, 0.0)))
    moved_ref[:own * half_rows] = mine.reshape(own * half_rows, mine.shape[2])
    moved_ref[own * half_rows:] = tile.astype(jnp.bfloat16)


def series_call(found, start, energy):
    n_orb = len(found)
    own, half_rows, nocc = start[0].shape
    return pl.pallas_call(
        functools.partial(series_kernel, n_orb),
        out_shape=pltpu.VMEM((own * half_rows + EXTRA, nocc), jnp.bfloat16),
        scratch_shapes=[
            pltpu.VMEM((ROWBLK, own, BLOCK, 2 * LANES), jnp.bfloat16),
            pltpu.VMEM((n_orb, own, half_rows, nocc), jnp.bfloat16),
            pltpu.VMEM((n_orb, own, half_rows, nocc), jnp.bfloat16),
        ],
        cost_estimate=FREE,
        compiler_params=params(16),
        name="series",
    )(*in_vmem(*found, *start, energy))


def place_kernel(layout, *refs):
    nz, plane, own = layout
    near, far = refs[:plane], refs[plane:2 * plane]
    out, energy_ref = refs[2 * plane:]
    me = lax.axis_index("chol")
    rows = out.shape[1]
    energy = jnp.zeros((EXTRA, LANES), jnp.float32)
    for dp in range(plane):
        for dz in range(nz):
            z = hop(lax.div(me, plane), -dz if nz & (nz - 1) else dz, nz)
            p = hop(lax.rem(me, plane), -dp if plane & (plane - 1) else dp, plane)
            piece = far[dp].at[dz - 1] if dz else near[dp]
            for j in range(own):
                out[(z * plane + p) * own + j] = piece[j * rows:(j + 1) * rows]
            energy = energy + piece[own * rows:].astype(jnp.float32)
    energy_ref[...] = (energy[0:1] + energy[1:2] + energy[2:3])[:, :energy_ref.shape[1]]


def place_call(layout, near, far):
    nz, plane, own = layout
    walk = nz * plane * own
    rows = (near[0].shape[0] - EXTRA) // own
    return pl.pallas_call(
        functools.partial(place_kernel, layout),
        out_shape=[
            jax.ShapeDtypeStruct((walk, rows, near[0].shape[1]), jnp.bfloat16),
            jax.ShapeDtypeStruct((1, walk), jnp.float32),
        ],
        cost_estimate=FREE,
        compiler_params=params(16),
        name="place_walkers",
    )(*in_vmem(*near, *far))


def per_device(chol_vals, chol_cols, greens, walkers, fields):
    vectors, rowblocks = chol_vals.shape[:2]
    walk, half_rows = greens.shape[:2]
    chips = lax.axis_size("chol")
    n_orb = lax.axis_size("orb")
    plane = 4 if chips % 4 == 0 else 1
    nz = chips // plane
    own = walk // chips
    layout = (nz, plane, own)
    step_factor = 72.0 / float(vectors * chips * BLOCK) ** 0.5

    def to_plane(a, dp):
        return lax.ppermute(a, "chol", [(c, (c // plane) * plane + hop(c % plane, dp, plane)) for c in range(chips)])

    def to_z(a, dz):
        return lax.ppermute(a, "chol", [(c, hop(c // plane, dz, nz) * plane + c % plane) for c in range(chips)])

    def around_orb(a):
        return [a] + [lax.ppermute(a, "orb", [((c + d) % n_orb, c) for c in range(n_orb)]) for d in range(1, n_orb)]

    cols = jnp.transpose(chol_cols, (1, 2, 0))
    turned, partial_bias, mine, cols = bias_call(chol_vals, greens, walkers, cols, own)
    start = around_orb(mine)
    bias, *others = around_orb(partial_bias)
    start, others = lax.optimization_barrier((start, others))

    units = 2 * rowblocks * BLOCK // CHUNK
    early_units = units * 3 // 16
    fields_t = fields.T
    def all_plane(arrays):
        return [to_plane(arrays[dp - 1], dp) for dp in reversed(range(1, plane))]

    z_order = [*range(2, nz), 1]

    def all_z(arrays):
        return [to_z(arrays[dz - 1], dz) for dz in z_order]

    late, energy = potential_call(early_units, units, layout, True, fields_t, bias, others, cols, turned)
    far, near = late[:plane], late[plane:]
    early, _ = potential_call(0, early_units, layout, False, fields_t, bias, others, cols, turned)
    early_came = all_z(early[1:])
    merged = merge_call([early[0], *early_came], near)
    far_came = all_z(sum_call([far[0], *all_plane(far[1:])], merged[:1]))
    found = finish_call(step_factor, far_came, [merged[0], *all_plane(merged[1:])])

    piece = series_call(around_orb(found), start, energy)
    near = [piece, *(to_plane(piece, dp) for dp in range(1, plane))]
    came = all_z([piece] * (nz - 1))
    pieces, *near[2:] = stack_call(near[2:], came[::-1], [dz - 1 for dz in z_order[::-1]])
    far = {dp: to_plane(pieces, dp) for dp in reversed(range(1, plane))}
    moved, energy = place_call(layout, near, [pieces, *(far[dp] for dp in range(1, plane))])
    return moved, energy.reshape(walk)


def solution(mesh):
    in_specs = (
        P("chol", "orb", None, None),
        P("chol", "orb", None),
        P("walker", "orb", None),
        P("walker", "orb", None),
        P("chol", "walker"),
    )
    out_specs = (P("walker", "orb", None), P("walker"))
    return jax.shard_map(
        per_device, mesh=mesh, in_specs=in_specs, out_specs=out_specs, check_vma=False
    )
```

```python
import functools

import jax
import jax.numpy as jnp
from jax import lax
from jax.experimental import pallas as pl
from jax.experimental.pallas import tpu as pltpu
from jax.sharding import PartitionSpec as P

BLOCK = 64
TAYLOR = 4
LANES = 2 * BLOCK
CHUNK = 16
EXTRA = 8
MIB = 1024 * 1024


FREE = pl.CostEstimate(flops=0, bytes_accessed=0, transcendentals=0)


def params(mib):
    return pltpu.CompilerParams(vmem_limit_bytes=mib * MIB)


def split(value):
    parts = []
    for _ in range(3):
        parts.append(value.astype(jnp.bfloat16))
        value = value - parts[-1].astype(jnp.float32)
    return parts


def in_vmem(*arrays):
    return [pltpu.with_memory_space_constraint(a, pltpu.VMEM) for a in arrays]


def in_hbm(*arrays):
    return [pltpu.with_memory_space_constraint(a, pltpu.HBM) for a in arrays]


def hop(at, distance, count):
    return at ^ distance if count & (count - 1) == 0 else (at + distance) % count


def swap_matrix():
    to = lax.broadcasted_iota(jnp.int32, (CHUNK * CHUNK, CHUNK * CHUNK), 0)
    at = lax.broadcasted_iota(jnp.int32, (CHUNK * CHUNK, CHUNK * CHUNK), 1)
    same = (to // CHUNK == at % CHUNK) & (to % CHUNK == at // CHUNK)
    return same.astype(jnp.float32).astype(jnp.bfloat16)


def column_order(row):
    other = 2 - 2 * (row // 2)
    return row, row + 1 - 2 * (row % 2), other, other + 1


def slot_masks(cols, row):
    return [cols == column for column in column_order(row)[1:]]


def bias_kernel(vals_hbm, greens_hbm, walkers_hbm, cols_hbm, turned_ref, bias_ref, mine_ref, cols_ref, vals, greens, swap, gs,
                acc, vsem, gsem, wsem, csem):
    total_steps, vectors = turned_ref.shape[:2]
    walk = bias_ref.shape[0]
    steps = BLOCK // CHUNK

    def copies(t):
        rows = pl.ds(lax.rem(t, steps) * CHUNK, CHUNK)
        return (
            pltpu.make_async_copy(vals_hbm.at[:, lax.div(t, steps), rows, :], vals.at[t], vsem.at[t]),
            pltpu.make_async_copy(greens_hbm.at[:, pl.ds(t * CHUNK, CHUNK), :], greens.at[t], gsem.at[t]),
        )

    def begin(t, carry):
        for copy in copies(t):
            copy.start()
        return carry

    own = mine_ref.shape[0]
    take = pltpu.make_async_copy(walkers_hbm.at[pl.ds(lax.axis_index("chol") * own, own)], mine_ref, wsem)
    take.start()
    take_cols = pltpu.make_async_copy(cols_hbm, cols_ref, csem)
    take_cols.start()
    lax.fori_loop(0, total_steps, begin, 0)
    swap[...] = swap_matrix()
    bias_ref[...] = jnp.zeros_like(bias_ref)
    first = lax.broadcasted_iota(jnp.int32, (CHUNK * CHUNK, LANES), 1) < BLOCK

    def step(t, side):
        for copy in copies(t):
            copy.wait()
        local = lax.div(t, steps)
        row = lax.axis_index("orb") * cols_ref.shape[0] + local
        upper = row // 2 == 1
        odd = row % 2 == 1
        for w in range(0, walk, CHUNK):
            mixed = greens[t, w:w + CHUNK].reshape(CHUNK * CHUNK, 2 * LANES)
            mixed = jnp.dot(swap[...], mixed, preferred_element_type=jnp.float32)
            pair = jnp.where(upper, mixed[:, LANES:], mixed[:, :LANES])
            rest = jnp.where(upper, mixed[:, :LANES], mixed[:, LANES:])
            pair = jnp.where(odd, pltpu.roll(pair, BLOCK, 1), pair)
            pieces = (
                jnp.where(first, pair, 0.0),
                jnp.where(first, 0.0, pair),
                jnp.where(first, 0.0, pltpu.roll(rest, BLOCK, 1)),
                jnp.where(first, 0.0, rest),
            )
            for k, piece in enumerate(pieces):
                piece = piece.astype(jnp.bfloat16)
                for i in range(CHUNK):
                    gs[side, k * walk + w:k * walk + w + CHUNK, i * LANES:(i + 1) * LANES] = (
                        piece[i * CHUNK:(i + 1) * CHUNK]
                    )
        for g in range(0, vectors, 2 * CHUNK):
            both = [vals[t, g + k * CHUNK:g + (k + 1) * CHUNK].reshape(CHUNK * CHUNK, LANES) for k in range(2)]
            both = jnp.dot(swap[...], jnp.concatenate(both, axis=1), preferred_element_type=jnp.float32)
            both = both.astype(jnp.bfloat16)
            for i in range(CHUNK):
                for k in range(2):
                    turned_ref[t, g + k * CHUNK:g + (k + 1) * CHUNK, i * LANES:(i + 1) * LANES] = (
                        both[i * CHUNK:(i + 1) * CHUNK, k * LANES:(k + 1) * LANES]
                    )
        part = lax.dot_general(
            turned_ref[t], gs[side], (((1,), (1,)), ((), ())), preferred_element_type=jnp.float32
        )
        begins = lax.rem(t, steps) == 0
        acc[...] = jnp.where(begins, 0.0, acc[...]) + part

        @pl.when(lax.rem(t, steps) == steps - 1)
        def _():
            flat = acc[...].T
            total = flat[0:walk]
            cols = cols_ref[local, 1:2, :]
            for k, mask in enumerate(slot_masks(cols, row)):
                total = total + jnp.where(mask, flat[(k + 1) * walk:(k + 2) * walk], 0.0)
            bias_ref[...] += total

    def pair(t, carry):
        step(2 * t, 0)
        step(2 * t + 1, 1)
        return carry

    acc[...] = jnp.zeros_like(acc)
    take_cols.wait()
    lax.fori_loop(0, total_steps // 2, pair, 0)
    take.wait()


def bias_call(vals, greens, walkers, cols, own):
    vectors, rowblocks = vals.shape[:2]
    walk, half_rows, norb = greens.shape
    steps = half_rows // CHUNK
    wide = CHUNK * LANES
    return pl.pallas_call(
        bias_kernel,
        in_specs=[
            *[pl.BlockSpec(memory_space=pl.ANY)] * 4,
        ],
        out_specs=[pl.BlockSpec(memory_space=pltpu.VMEM)] * 4,
        out_shape=[
            pltpu.VMEM((steps, vectors, wide), jnp.bfloat16),
            pltpu.VMEM((walk, vectors), jnp.float32),
            pltpu.VMEM((own, *walkers.shape[1:]), jnp.bfloat16),
            pltpu.VMEM(cols.shape, jnp.int32),
        ],
        scratch_shapes=[
            pltpu.VMEM((steps, vectors, CHUNK, LANES), jnp.bfloat16),
            pltpu.VMEM((steps, walk, CHUNK, norb), jnp.bfloat16),
            pltpu.VMEM((CHUNK * CHUNK, CHUNK * CHUNK), jnp.bfloat16),
            pltpu.VMEM((2, 4 * walk, wide), jnp.bfloat16),
            pltpu.VMEM((vectors, 4 * walk), jnp.float32),
            pltpu.SemaphoreType.DMA((steps,)),
            pltpu.SemaphoreType.DMA((steps,)),
            pltpu.SemaphoreType.DMA,
            pltpu.SemaphoreType.DMA,
        ],
        cost_estimate=FREE,
        compiler_params=params(24),
        name="force_bias",
    )(*in_hbm(vals, greens, walkers, cols))


def potential_kernel(begin, end, layout, by_plane, fields_ref, own_ref, *refs):
    nz, plane, own = layout
    others = refs[:lax.axis_size("orb") - 1]
    cols_ref, turned_ref = refs[len(others):len(others) + 2]
    groups = 2 * plane if by_plane else nz
    outs = refs[len(others) + 2:len(others) + 2 + groups]
    energy_ref, s_ref, swap = refs[len(others) + 2 + groups:]
    walk, vectors = fields_ref.shape
    rowblocks = cols_ref.shape[0]

    me = lax.axis_index("chol")
    bias = own_ref[...]
    for other in others:
        bias = bias + other[...]
    energy = 0.5 * jnp.sum(bias * bias, axis=1, keepdims=True)
    energy_ref[...] = jnp.zeros_like(energy_ref)
    energy_ref[:, :walk] = jnp.broadcast_to(energy, (walk, LANES)).T[:CHUNK]
    shifted = (fields_ref[...] - bias).astype(jnp.bfloat16)
    at = lax.broadcasted_iota(jnp.int32, (walk, walk), 0)
    source = lax.broadcasted_iota(jnp.int32, (walk, walk), 1)
    chip = at // own
    z = hop(me // plane, chip // plane, nz)
    p = hop(me % plane, chip % plane, plane)
    wanted = (z * plane + p) * own + at % own
    pick = (wanted == source).astype(jnp.float32).astype(jnp.bfloat16)
    ordered = jnp.dot(pick, shifted, preferred_element_type=jnp.float32)
    for local in range(rowblocks):
        row = lax.axis_index("orb") * rowblocks + local
        s_ref[local, 0:walk] = ordered.astype(jnp.bfloat16)
        for k, mask in enumerate(slot_masks(cols_ref[local, 1:2, :], row)):
            s_ref[local, (k + 1) * walk:(k + 2) * walk] = jnp.where(mask, ordered, 0.0).astype(jnp.bfloat16)
    swap[...] = swap_matrix()
    first = lax.broadcasted_iota(jnp.int32, (walk, LANES), 1) < BLOCK

    def step(t, halves=(0, 1)):
        left = s_ref[lax.div(t, BLOCK // CHUNK)]
        tiles = []
        for i in range(0, CHUNK, 2):
            both = jnp.dot(left, turned_ref[t, :, i * LANES:(i + 2) * LANES], preferred_element_type=jnp.float32)
            for side in range(2):
                out = both[:, side * LANES:(side + 1) * LANES]
                near = jnp.where(first, out[0:walk], out[walk:2 * walk])
                far = jnp.where(first, pltpu.roll(out[2 * walk:3 * walk], BLOCK, 1), out[3 * walk:])
                wanted = [(near, far)[half] for half in halves]
                tiles.append(jnp.concatenate(wanted, axis=1).astype(jnp.bfloat16))
        for w0 in range(0, walk, CHUNK):
            mixed = jnp.concatenate([tile[w0:w0 + CHUNK] for tile in tiles], axis=0)
            mixed = jnp.dot(swap[...], mixed, preferred_element_type=jnp.float32).astype(jnp.bfloat16)
            for w in range(CHUNK):
                chip, j = (w0 + w) // own, (w0 + w) % own
                dz, dp = chip // plane, chip % plane
                if not by_plane:
                    out, inner = outs[dz], (dp,)
                elif dz:
                    out, inner = outs[dp], (dz - 1,)
                else:
                    out, inner = outs[plane + dp], ()
                for k, half in enumerate(halves):
                    at = (2 * t + half - begin) * CHUNK
                    rows = pl.ds(at if isinstance(t, int) else pl.multiple_of(at, CHUNK), CHUNK)
                    out[(*inner, j, rows)] = mixed[w * CHUNK:(w + 1) * CHUNK, k * LANES:(k + 1) * LANES]

    def pair(t, carry):
        step(from_step + 2 * t)
        step(from_step + 2 * t + 1)
        return carry

    from_step, to_step = (begin + 1) // 2, end // 2
    if begin % 2:
        step(begin // 2, (1,))
    lax.fori_loop(0, (to_step - from_step) // 2, pair, 0)
    if (to_step - from_step) % 2:
        step(to_step - 1)
    if end % 2:
        step(end // 2, (0,))


def potential_call(begin, end, layout, by_plane, fields, bias, others, cols, turned):
    nz, plane, own = layout
    walk, vectors = fields.shape
    leading = [(nz - 1,)] * plane + [()] * plane if by_plane else [(plane,)] * nz
    rows = (end - begin) * CHUNK
    *parts, energy = pl.pallas_call(
        functools.partial(potential_kernel, begin, end, layout, by_plane),
        out_shape=[
            *[pltpu.VMEM((*inner, own, rows, LANES), jnp.bfloat16) for inner in leading],
            pltpu.VMEM((CHUNK, LANES), jnp.float32),
        ],
        scratch_shapes=[
            pltpu.VMEM((cols.shape[0], 4 * walk, vectors), jnp.bfloat16),
            pltpu.VMEM((CHUNK * CHUNK, CHUNK * CHUNK), jnp.bfloat16),
        ],
        cost_estimate=FREE,
        compiler_params=params(16),
        name="potential",
    )(fields, *in_vmem(bias, *others, cols, turned))
    return parts, energy


def add(refs, *at):
    total = refs[0][at].astype(jnp.float32)
    for ref in refs[1:]:
        total = total + ref[at].astype(jnp.float32)
    return total


def vmem_call(kernel, name, out_shape, *arrays):
    return pl.pallas_call(
        kernel, out_shape=out_shape, cost_estimate=FREE, compiler_params=params(16), name=name
    )(*in_vmem(*arrays))


def sum_call(arrays, after):
    def kernel(*refs):
        for k, out in enumerate(refs[len(arrays) + len(after):]):
            out[...] = add(refs[:len(arrays)], k).astype(out.dtype)

    out_shape = [pltpu.VMEM(arrays[0].shape[1:], jnp.bfloat16)] * arrays[0].shape[0]
    return vmem_call(kernel, "sum_parts", out_shape, *arrays, *after)


def merge_call(early, near):
    own, rows, lanes = early[0].shape[1:]

    def kernel(*refs):
        early_refs, near_refs, outs = refs[:len(early)], refs[len(early):len(early) + len(near)], refs[-len(near):]
        for k, (ref, out) in enumerate(zip(near_refs, outs)):
            out[:, :rows] = add(early_refs, k).astype(out.dtype)
            out[:, rows:] = ref[...]

    out_shape = [pltpu.VMEM((own, rows + near[0].shape[1], lanes), jnp.bfloat16)] * len(near)
    return vmem_call(kernel, "merge_parts", out_shape, *early, *near)


def finish_call(factor, far, merged):
    early = merged[0].shape[1] - far[0].shape[1]

    def kernel(*refs):
        far_refs, merged_refs, out = refs[:len(far)], refs[len(far):-1], refs[-1]
        rowblocks = out.shape[1] // (2 * BLOCK)
        for unit in range(out.shape[1] // CHUNK):
            at = unit * CHUNK
            for j in range(out.shape[0]):
                total = add(merged_refs, j, slice(at, at + CHUNK))
                if at >= early:
                    total = total + add(far_refs, j, slice(at - early, at - early + CHUNK))
                if unit % 2 == 0:
                    row = lax.axis_index("orb") * rowblocks + at // (2 * BLOCK)
                    total = jnp.where(row % 2 == 1, pltpu.roll(total, BLOCK, 1), total)
                out[j, at:at + CHUNK] = (factor * total).astype(out.dtype)

    return vmem_call(kernel, "finish", pltpu.VMEM(merged[0].shape, jnp.bfloat16), *far, *merged)


def stack_call(near, pieces, slots):
    def kernel(*refs):
        ins, outs = refs[:len(pieces) + len(near)], refs[len(pieces) + len(near):]
        for ref, slot in zip(ins[len(near):], slots):
            outs[0][slot] = ref[...]
        for ref, out in zip(ins, outs[1:]):
            out[...] = ref[...]

    one = pltpu.VMEM(pieces[0].shape, jnp.bfloat16)
    out_shape = [pltpu.VMEM((len(pieces), *pieces[0].shape), jnp.bfloat16)] + [one] * len(near)
    return vmem_call(kernel, "stack_pieces", out_shape, *near, *pieces)


def series_kernel(n_orb, *refs):
    found, start = refs[:n_orb], refs[n_orb:2 * n_orb]
    energy_ref, moved_ref, pot, begin, total = refs[2 * n_orb:]
    me = lax.axis_index("orb")
    own, half_rows = start[0].shape[:2]
    per = BLOCK // CHUNK
    for d in range(n_orb):
        at = lax.rem(me + d, n_orb)
        begin[:, pl.ds(pl.multiple_of(at * half_rows, half_rows), half_rows)] = start[d][...]
        for t in range(half_rows // CHUNK):
            row = at * (half_rows // BLOCK) + t // per
            rows = pl.ds(pl.multiple_of(row * BLOCK + t % per * CHUNK, CHUNK), CHUNK)
            for half in range(2):
                side = lax.rem(lax.div(row, 2) + half, 2)
                lanes = pl.ds(pl.multiple_of(side * LANES, LANES), LANES)
                pot[:, rows, lanes] = found[d][:, (2 * t + half) * CHUNK:(2 * t + half + 1) * CHUNK]
    terms = [begin[j] for j in range(own)]
    sums = [term.astype(jnp.float32) for term in terms]
    added = [jnp.zeros(terms[0].shape, jnp.float32)] * own
    for degree in range(1, TAYLOR + 1):
        for j in range(own):
            product = jnp.dot(pot[j], terms[j], preferred_element_type=jnp.float32)
            terms[j] = (product / degree).astype(jnp.bfloat16)
            added[j] = added[j] + terms[j].astype(jnp.float32)
    for j in range(own):
        total[j] = (sums[j] + added[j]).astype(jnp.bfloat16)
    mine = total[:, pl.ds(pl.multiple_of(me * half_rows, half_rows), half_rows)]
    at = lax.broadcasted_iota(jnp.int32, (EXTRA, LANES), 0)
    high, middle, low = (part.astype(jnp.float32) for part in split(energy_ref[:EXTRA]))
    tile = jnp.where(at == 0, high, jnp.where(at == 1, middle, jnp.where(at == 2, low, 0.0)))
    moved_ref[:own * half_rows] = mine.reshape(own * half_rows, mine.shape[2])
    moved_ref[own * half_rows:] = tile.astype(jnp.bfloat16)


def series_call(found, start, energy):
    n_orb = len(found)
    own, half_rows, nocc = start[0].shape
    return pl.pallas_call(
        functools.partial(series_kernel, n_orb),
        out_shape=pltpu.VMEM((own * half_rows + EXTRA, nocc), jnp.bfloat16),
        scratch_shapes=[
            pltpu.VMEM((own, n_orb * half_rows, 2 * LANES), jnp.bfloat16),
            pltpu.VMEM((own, n_orb * half_rows, nocc), jnp.bfloat16),
            pltpu.VMEM((own, n_orb * half_rows, nocc), jnp.bfloat16),
        ],
        cost_estimate=FREE,
        compiler_params=params(16),
        name="series",
    )(*in_vmem(*found, *start, energy))


def place_kernel(layout, *refs):
    nz, plane, own = layout
    near, far = refs[:plane], refs[plane:2 * plane]
    out, energy_ref = refs[2 * plane:]
    me = lax.axis_index("chol")
    rows = out.shape[1]
    energy = jnp.zeros((EXTRA, LANES), jnp.float32)
    for dp in range(plane):
        for dz in range(nz):
            z = hop(lax.div(me, plane), -dz if nz & (nz - 1) else dz, nz)
            p = hop(lax.rem(me, plane), -dp if plane & (plane - 1) else dp, plane)
            piece = far[dp].at[dz - 1] if dz else near[dp]
            for j in range(own):
                out[(z * plane + p) * own + j] = piece[j * rows:(j + 1) * rows]
            energy = energy + piece[own * rows:].astype(jnp.float32)
    energy_ref[...] = (energy[0:1] + energy[1:2] + energy[2:3])[:, :energy_ref.shape[1]]


def place_call(layout, near, far):
    nz, plane, own = layout
    walk = nz * plane * own
    rows = (near[0].shape[0] - EXTRA) // own
    return pl.pallas_call(
        functools.partial(place_kernel, layout),
        out_shape=[
            jax.ShapeDtypeStruct((walk, rows, near[0].shape[1]), jnp.bfloat16),
            jax.ShapeDtypeStruct((1, walk), jnp.float32),
        ],
        cost_estimate=FREE,
        compiler_params=params(16),
        name="place_walkers",
    )(*in_vmem(*near, *far))


def per_device(chol_vals, chol_cols, greens, walkers, fields):
    vectors, rowblocks = chol_vals.shape[:2]
    walk, half_rows = greens.shape[:2]
    chips = lax.axis_size("chol")
    n_orb = lax.axis_size("orb")
    plane = 4 if chips % 4 == 0 else 1
    nz = chips // plane
    own = walk // chips
    layout = (nz, plane, own)
    step_factor = 72.0 / float(vectors * chips * BLOCK) ** 0.5

    def to_plane(a, dp):
        return lax.ppermute(a, "chol", [(c, (c // plane) * plane + hop(c % plane, dp, plane)) for c in range(chips)])

    def to_z(a, dz):
        return lax.ppermute(a, "chol", [(c, hop(c // plane, dz, nz) * plane + c % plane) for c in range(chips)])

    def around_orb(a):
        return [a] + [lax.ppermute(a, "orb", [((c + d) % n_orb, c) for c in range(n_orb)]) for d in range(1, n_orb)]

    cols = jnp.transpose(chol_cols, (1, 2, 0))
    turned, partial_bias, mine, cols = bias_call(chol_vals, greens, walkers, cols, own)
    start = around_orb(mine)
    bias, *others = around_orb(partial_bias)
    start, others = lax.optimization_barrier((start, others))

    units = 2 * rowblocks * BLOCK // CHUNK
    early_units = units // 8
    fields_t = fields.T
    def all_plane(arrays):
        return [to_plane(arrays[dp - 1], dp) for dp in reversed(range(1, plane))]

    z_order = [*range(2, nz), 1]

    def all_z(arrays):
        return [to_z(arrays[dz - 1], dz) for dz in z_order]

    late, energy = potential_call(early_units, units, layout, True, fields_t, bias, others, cols, turned)
    far, near = late[:plane], late[plane:]
    early, _ = potential_call(0, early_units, layout, False, fields_t, bias, others, cols, turned)
    early_came = all_z(early[1:])
    merged = merge_call([early[0], *early_came], near)
    far_came = all_z(sum_call([far[0], *all_plane(far[1:])], merged[:1]))
    found = finish_call(step_factor, far_came, [merged[0], *all_plane(merged[1:])])

    piece = series_call(around_orb(found), start, energy)
    near = [piece, *(to_plane(piece, dp) for dp in range(1, plane))]
    came = all_z([piece] * (nz - 1))
    pieces, *near[2:] = stack_call(near[2:], came[::-1], [dz - 1 for dz in z_order[::-1]])
    far = {dp: to_plane(pieces, dp) for dp in reversed(range(1, plane))}
    moved, energy = place_call(layout, near, [pieces, *(far[dp] for dp in range(1, plane))])
    return moved, energy.reshape(walk)


def solution(mesh):
    in_specs = (
        P("chol", "orb", None, None),
        P("chol", "orb", None),
        P("walker", "orb", None),
        P("walker", "orb", None),
        P("chol", "walker"),
    )
    out_specs = (P("walker", "orb", None), P("walker"))
    return jax.shard_map(
        per_device, mesh=mesh, in_specs=in_specs, out_specs=out_specs, check_vma=False
    )
```

```python
import functools

import jax
import jax.numpy as jnp
from jax import lax
from jax.experimental import pallas as pl
from jax.experimental.pallas import tpu as pltpu
from jax.sharding import PartitionSpec as P

BLOCK = 64
TAYLOR = 4
LANES = 2 * BLOCK
CHUNK = 16
EXTRA = 8
MIB = 1024 * 1024


FREE = pl.CostEstimate(flops=0, bytes_accessed=0, transcendentals=0)


def params(mib):
    return pltpu.CompilerParams(vmem_limit_bytes=mib * MIB)


def split(value):
    parts = []
    for _ in range(3):
        parts.append(value.astype(jnp.bfloat16))
        value = value - parts[-1].astype(jnp.float32)
    return parts


def in_vmem(*arrays):
    return [pltpu.with_memory_space_constraint(a, pltpu.VMEM) for a in arrays]


def in_hbm(*arrays):
    return [pltpu.with_memory_space_constraint(a, pltpu.HBM) for a in arrays]


def hop(at, distance, count):
    return at ^ distance if count & (count - 1) == 0 else (at + distance) % count


def swap_matrix():
    to = lax.broadcasted_iota(jnp.int32, (CHUNK * CHUNK, CHUNK * CHUNK), 0)
    at = lax.broadcasted_iota(jnp.int32, (CHUNK * CHUNK, CHUNK * CHUNK), 1)
    same = (to // CHUNK == at % CHUNK) & (to % CHUNK == at // CHUNK)
    return same.astype(jnp.float32).astype(jnp.bfloat16)


def column_order(row):
    other = 2 - 2 * (row // 2)
    return row, row + 1 - 2 * (row % 2), other, other + 1


def slot_masks(cols, row):
    return [cols == column for column in column_order(row)[1:]]


def bias_kernel(vals_hbm, greens_hbm, walkers_hbm, cols_hbm, turned_ref, bias_ref, mine_ref, cols_ref, vals, greens, swap, gs,
                acc, vsem, gsem, wsem, csem):
    total_steps, vectors = turned_ref.shape[:2]
    walk = bias_ref.shape[0]
    steps = BLOCK // CHUNK

    def copies(t):
        rows = pl.ds(lax.rem(t, steps) * CHUNK, CHUNK)
        return (
            pltpu.make_async_copy(vals_hbm.at[:, lax.div(t, steps), rows, :], vals.at[t], vsem.at[t]),
            pltpu.make_async_copy(greens_hbm.at[:, pl.ds(t * CHUNK, CHUNK), :], greens.at[t], gsem.at[t]),
        )

    def begin(t, carry):
        for copy in copies(t):
            copy.start()
        return carry

    own = mine_ref.shape[0]
    take = pltpu.make_async_copy(walkers_hbm.at[pl.ds(lax.axis_index("chol") * own, own)], mine_ref, wsem)
    take.start()
    take_cols = pltpu.make_async_copy(cols_hbm, cols_ref, csem)
    take_cols.start()
    lax.fori_loop(0, total_steps, begin, 0)
    swap[...] = swap_matrix()
    bias_ref[...] = jnp.zeros_like(bias_ref)
    first = lax.broadcasted_iota(jnp.int32, (CHUNK * CHUNK, LANES), 1) < BLOCK

    def step(t, side):
        for copy in copies(t):
            copy.wait()
        local = lax.div(t, steps)
        row = lax.axis_index("orb") * cols_ref.shape[0] + local
        upper = row // 2 == 1
        odd = row % 2 == 1
        for w in range(0, walk, CHUNK):
            mixed = greens[t, w:w + CHUNK].reshape(CHUNK * CHUNK, 2 * LANES)
            mixed = jnp.dot(swap[...], mixed, preferred_element_type=jnp.float32)
            pair = jnp.where(upper, mixed[:, LANES:], mixed[:, :LANES])
            rest = jnp.where(upper, mixed[:, :LANES], mixed[:, LANES:])
            pair = jnp.where(odd, pltpu.roll(pair, BLOCK, 1), pair)
            pieces = (
                jnp.where(first, pair, 0.0),
                jnp.where(first, 0.0, pair),
                jnp.where(first, 0.0, pltpu.roll(rest, BLOCK, 1)),
                jnp.where(first, 0.0, rest),
            )
            for k, piece in enumerate(pieces):
                piece = piece.astype(jnp.bfloat16)
                for i in range(CHUNK):
                    gs[side, k * walk + w:k * walk + w + CHUNK, i * LANES:(i + 1) * LANES] = (
                        piece[i * CHUNK:(i + 1) * CHUNK]
                    )
        for g in range(0, vectors, 4 * CHUNK):
            both = [vals[t, g + k * CHUNK:g + (k + 1) * CHUNK].reshape(CHUNK * CHUNK, LANES) for k in range(2)]
            both = jnp.dot(swap[...], jnp.concatenate(both, axis=1), preferred_element_type=jnp.float32)
            both = both.astype(jnp.bfloat16)
            for i in range(CHUNK):
                for k in range(2):
                    turned_ref[t, g + k * CHUNK:g + (k + 1) * CHUNK, i * LANES:(i + 1) * LANES] = (
                        both[i * CHUNK:(i + 1) * CHUNK, k * LANES:(k + 1) * LANES]
                    )
            for k in range(2, 4):
                other = vals[t, g + k * CHUNK:g + (k + 1) * CHUNK].astype(jnp.float32)
                other = jnp.swapaxes(other, 0, 1).astype(jnp.bfloat16)
                for i in range(CHUNK):
                    turned_ref[t, g + k * CHUNK:g + (k + 1) * CHUNK, i * LANES:(i + 1) * LANES] = other[i]
        part = lax.dot_general(
            turned_ref[t], gs[side], (((1,), (1,)), ((), ())), preferred_element_type=jnp.float32
        )
        begins = lax.rem(t, steps) == 0
        acc[...] = jnp.where(begins, 0.0, acc[...]) + part

        @pl.when(lax.rem(t, steps) == steps - 1)
        def _():
            flat = acc[...].T
            total = flat[0:walk]
            cols = cols_ref[local, 1:2, :]
            for k, mask in enumerate(slot_masks(cols, row)):
                total = total + jnp.where(mask, flat[(k + 1) * walk:(k + 2) * walk], 0.0)
            bias_ref[...] += total

    def pair(t, carry):
        step(2 * t, 0)
        step(2 * t + 1, 1)
        return carry

    acc[...] = jnp.zeros_like(acc)
    take_cols.wait()
    lax.fori_loop(0, total_steps // 2, pair, 0)
    take.wait()


def bias_call(vals, greens, walkers, cols, own):
    vectors, rowblocks = vals.shape[:2]
    walk, half_rows, norb = greens.shape
    steps = half_rows // CHUNK
    wide = CHUNK * LANES
    return pl.pallas_call(
        bias_kernel,
        in_specs=[
            *[pl.BlockSpec(memory_space=pl.ANY)] * 4,
        ],
        out_specs=[pl.BlockSpec(memory_space=pltpu.VMEM)] * 4,
        out_shape=[
            pltpu.VMEM((steps, vectors, wide), jnp.bfloat16),
            pltpu.VMEM((walk, vectors), jnp.float32),
            pltpu.VMEM((own, *walkers.shape[1:]), jnp.bfloat16),
            pltpu.VMEM(cols.shape, jnp.int32),
        ],
        scratch_shapes=[
            pltpu.VMEM((steps, vectors, CHUNK, LANES), jnp.bfloat16),
            pltpu.VMEM((steps, walk, CHUNK, norb), jnp.bfloat16),
            pltpu.VMEM((CHUNK * CHUNK, CHUNK * CHUNK), jnp.bfloat16),
            pltpu.VMEM((2, 4 * walk, wide), jnp.bfloat16),
            pltpu.VMEM((vectors, 4 * walk), jnp.float32),
            pltpu.SemaphoreType.DMA((steps,)),
            pltpu.SemaphoreType.DMA((steps,)),
            pltpu.SemaphoreType.DMA,
            pltpu.SemaphoreType.DMA,
        ],
        cost_estimate=FREE,
        compiler_params=params(24),
        name="force_bias",
    )(*in_hbm(vals, greens, walkers, cols))


def potential_kernel(begin, end, layout, by_plane, fields_ref, own_ref, *refs):
    nz, plane, own = layout
    others = refs[:lax.axis_size("orb") - 1]
    cols_ref, turned_ref = refs[len(others):len(others) + 2]
    groups = 2 * plane if by_plane else nz
    outs = refs[len(others) + 2:len(others) + 2 + groups]
    energy_ref, s_ref, swap = refs[len(others) + 2 + groups:]
    walk, vectors = fields_ref.shape
    rowblocks = cols_ref.shape[0]

    me = lax.axis_index("chol")
    bias = own_ref[...]
    for other in others:
        bias = bias + other[...]
    energy = 0.5 * jnp.sum(bias * bias, axis=1, keepdims=True)
    energy_ref[...] = jnp.zeros_like(energy_ref)
    energy_ref[:, :walk] = jnp.broadcast_to(energy, (walk, LANES)).T[:CHUNK]
    shifted = (fields_ref[...] - bias).astype(jnp.bfloat16)
    at = lax.broadcasted_iota(jnp.int32, (walk, walk), 0)
    source = lax.broadcasted_iota(jnp.int32, (walk, walk), 1)
    chip = at // own
    z = hop(me // plane, chip // plane, nz)
    p = hop(me % plane, chip % plane, plane)
    wanted = (z * plane + p) * own + at % own
    pick = (wanted == source).astype(jnp.float32).astype(jnp.bfloat16)
    ordered = jnp.dot(pick, shifted, preferred_element_type=jnp.float32)
    for local in range(rowblocks):
        row = lax.axis_index("orb") * rowblocks + local
        s_ref[local, 0:walk] = ordered.astype(jnp.bfloat16)
        for k, mask in enumerate(slot_masks(cols_ref[local, 1:2, :], row)):
            s_ref[local, (k + 1) * walk:(k + 2) * walk] = jnp.where(mask, ordered, 0.0).astype(jnp.bfloat16)
    swap[...] = swap_matrix()
    first = lax.broadcasted_iota(jnp.int32, (walk, LANES), 1) < BLOCK

    def step(t, halves=(0, 1)):
        left = s_ref[lax.div(t, BLOCK // CHUNK)]
        tiles = []
        for i in range(0, CHUNK, 2):
            both = jnp.dot(left, turned_ref[t, :, i * LANES:(i + 2) * LANES], preferred_element_type=jnp.float32)
            for side in range(2):
                out = both[:, side * LANES:(side + 1) * LANES]
                near = jnp.where(first, out[0:walk], out[walk:2 * walk])
                far = jnp.where(first, pltpu.roll(out[2 * walk:3 * walk], BLOCK, 1), out[3 * walk:])
                wanted = [(near, far)[half] for half in halves]
                tiles.append(jnp.concatenate(wanted, axis=1).astype(jnp.bfloat16))
        for w0 in range(0, walk, CHUNK):
            mixed = jnp.concatenate([tile[w0:w0 + CHUNK] for tile in tiles], axis=0)
            mixed = jnp.dot(swap[...], mixed, preferred_element_type=jnp.float32).astype(jnp.bfloat16)
            for w in range(CHUNK):
                chip, j = (w0 + w) // own, (w0 + w) % own
                dz, dp = chip // plane, chip % plane
                if not by_plane:
                    out, inner = outs[dz], (dp,)
                elif dz:
                    out, inner = outs[dp], (dz - 1,)
                else:
                    out, inner = outs[plane + dp], ()
                for k, half in enumerate(halves):
                    at = (2 * t + half - begin) * CHUNK
                    rows = pl.ds(at if isinstance(t, int) else pl.multiple_of(at, CHUNK), CHUNK)
                    out[(*inner, j, rows)] = mixed[w * CHUNK:(w + 1) * CHUNK, k * LANES:(k + 1) * LANES]

    def pair(t, carry):
        step(from_step + 2 * t)
        step(from_step + 2 * t + 1)
        return carry

    from_step, to_step = (begin + 1) // 2, end // 2
    if begin % 2:
        step(begin // 2, (1,))
    lax.fori_loop(0, (to_step - from_step) // 2, pair, 0)
    if (to_step - from_step) % 2:
        step(to_step - 1)
    if end % 2:
        step(end // 2, (0,))


def potential_call(begin, end, layout, by_plane, fields, bias, others, cols, turned):
    nz, plane, own = layout
    walk, vectors = fields.shape
    leading = [(nz - 1,)] * plane + [()] * plane if by_plane else [(plane,)] * nz
    rows = (end - begin) * CHUNK
    *parts, energy = pl.pallas_call(
        functools.partial(potential_kernel, begin, end, layout, by_plane),
        out_shape=[
            *[pltpu.VMEM((*inner, own, rows, LANES), jnp.bfloat16) for inner in leading],
            pltpu.VMEM((CHUNK, LANES), jnp.float32),
        ],
        scratch_shapes=[
            pltpu.VMEM((cols.shape[0], 4 * walk, vectors), jnp.bfloat16),
            pltpu.VMEM((CHUNK * CHUNK, CHUNK * CHUNK), jnp.bfloat16),
        ],
        cost_estimate=FREE,
        compiler_params=params(16),
        name="potential",
    )(fields, *in_vmem(bias, *others, cols, turned))
    return parts, energy


def add(refs, *at):
    total = refs[0][at].astype(jnp.float32)
    for ref in refs[1:]:
        total = total + ref[at].astype(jnp.float32)
    return total


def vmem_call(kernel, name, out_shape, *arrays):
    return pl.pallas_call(
        kernel, out_shape=out_shape, cost_estimate=FREE, compiler_params=params(16), name=name
    )(*in_vmem(*arrays))


def sum_call(arrays, after):
    def kernel(*refs):
        for k, out in enumerate(refs[len(arrays) + len(after):]):
            out[...] = add(refs[:len(arrays)], k).astype(out.dtype)

    out_shape = [pltpu.VMEM(arrays[0].shape[1:], jnp.bfloat16)] * arrays[0].shape[0]
    return vmem_call(kernel, "sum_parts", out_shape, *arrays, *after)


def merge_call(early, near):
    own, rows, lanes = early[0].shape[1:]

    def kernel(*refs):
        early_refs, near_refs, outs = refs[:len(early)], refs[len(early):len(early) + len(near)], refs[-len(near):]
        for k, (ref, out) in enumerate(zip(near_refs, outs)):
            out[:, :rows] = add(early_refs, k).astype(out.dtype)
            out[:, rows:] = ref[...]

    out_shape = [pltpu.VMEM((own, rows + near[0].shape[1], lanes), jnp.bfloat16)] * len(near)
    return vmem_call(kernel, "merge_parts", out_shape, *early, *near)


def finish_call(factor, far, merged):
    early = merged[0].shape[1] - far[0].shape[1]

    def kernel(*refs):
        far_refs, merged_refs, out = refs[:len(far)], refs[len(far):-1], refs[-1]
        rowblocks = out.shape[1] // (2 * BLOCK)
        for unit in range(out.shape[1] // CHUNK):
            at = unit * CHUNK
            for j in range(out.shape[0]):
                total = add(merged_refs, j, slice(at, at + CHUNK))
                if at >= early:
                    total = total + add(far_refs, j, slice(at - early, at - early + CHUNK))
                if unit % 2 == 0:
                    row = lax.axis_index("orb") * rowblocks + at // (2 * BLOCK)
                    total = jnp.where(row % 2 == 1, pltpu.roll(total, BLOCK, 1), total)
                out[j, at:at + CHUNK] = (factor * total).astype(out.dtype)

    return vmem_call(kernel, "finish", pltpu.VMEM(merged[0].shape, jnp.bfloat16), *far, *merged)


def stack_call(near, pieces, slots):
    def kernel(*refs):
        ins, outs = refs[:len(pieces) + len(near)], refs[len(pieces) + len(near):]
        for ref, slot in zip(ins[len(near):], slots):
            outs[0][slot] = ref[...]
        for ref, out in zip(ins, outs[1:]):
            out[...] = ref[...]

    one = pltpu.VMEM(pieces[0].shape, jnp.bfloat16)
    out_shape = [pltpu.VMEM((len(pieces), *pieces[0].shape), jnp.bfloat16)] + [one] * len(near)
    return vmem_call(kernel, "stack_pieces", out_shape, *near, *pieces)


def series_kernel(n_orb, *refs):
    found, start = refs[:n_orb], refs[n_orb:2 * n_orb]
    energy_ref, moved_ref, pot, begin, total = refs[2 * n_orb:]
    me = lax.axis_index("orb")
    own, half_rows = start[0].shape[:2]
    per = BLOCK // CHUNK
    for d in range(n_orb):
        at = lax.rem(me + d, n_orb)
        begin[:, pl.ds(pl.multiple_of(at * half_rows, half_rows), half_rows)] = start[d][...]
        for t in range(half_rows // CHUNK):
            row = at * (half_rows // BLOCK) + t // per
            rows = pl.ds(pl.multiple_of(row * BLOCK + t % per * CHUNK, CHUNK), CHUNK)
            for half in range(2):
                side = lax.rem(lax.div(row, 2) + half, 2)
                lanes = pl.ds(pl.multiple_of(side * LANES, LANES), LANES)
                pot[:, rows, lanes] = found[d][:, (2 * t + half) * CHUNK:(2 * t + half + 1) * CHUNK]
    terms = [begin[j] for j in range(own)]
    sums = [term.astype(jnp.float32) for term in terms]
    added = [jnp.zeros(terms[0].shape, jnp.float32)] * own
    for degree in range(1, TAYLOR + 1):
        for j in range(own):
            product = jnp.dot(pot[j], terms[j], preferred_element_type=jnp.float32)
            terms[j] = (product / degree).astype(jnp.bfloat16)
            added[j] = added[j] + terms[j].astype(jnp.float32)
    for j in range(own):
        total[j] = (sums[j] + added[j]).astype(jnp.bfloat16)
    mine = total[:, pl.ds(pl.multiple_of(me * half_rows, half_rows), half_rows)]
    at = lax.broadcasted_iota(jnp.int32, (EXTRA, LANES), 0)
    high, middle, low = (part.astype(jnp.float32) for part in split(energy_ref[:EXTRA]))
    tile = jnp.where(at == 0, high, jnp.where(at == 1, middle, jnp.where(at == 2, low, 0.0)))
    moved_ref[:own * half_rows] = mine.reshape(own * half_rows, mine.shape[2])
    moved_ref[own * half_rows:] = tile.astype(jnp.bfloat16)


def series_call(found, start, energy):
    n_orb = len(found)
    own, half_rows, nocc = start[0].shape
    return pl.pallas_call(
        functools.partial(series_kernel, n_orb),
        out_shape=pltpu.VMEM((own * half_rows + EXTRA, nocc), jnp.bfloat16),
        scratch_shapes=[
            pltpu.VMEM((own, n_orb * half_rows, 2 * LANES), jnp.bfloat16),
            pltpu.VMEM((own, n_orb * half_rows, nocc), jnp.bfloat16),
            pltpu.VMEM((own, n_orb * half_rows, nocc), jnp.bfloat16),
        ],
        cost_estimate=FREE,
        compiler_params=params(16),
        name="series",
    )(*in_vmem(*found, *start, energy))


def place_kernel(layout, *refs):
    nz, plane, own = layout
    near, far = refs[:plane], refs[plane:2 * plane]
    out, energy_ref = refs[2 * plane:]
    me = lax.axis_index("chol")
    rows = out.shape[1]
    energy = jnp.zeros((EXTRA, LANES), jnp.float32)
    for dp in range(plane):
        for dz in range(nz):
            z = hop(lax.div(me, plane), -dz if nz & (nz - 1) else dz, nz)
            p = hop(lax.rem(me, plane), -dp if plane & (plane - 1) else dp, plane)
            piece = far[dp].at[dz - 1] if dz else near[dp]
            for j in range(own):
                out[(z * plane + p) * own + j] = piece[j * rows:(j + 1) * rows]
            energy = energy + piece[own * rows:].astype(jnp.float32)
    energy_ref[...] = (energy[0:1] + energy[1:2] + energy[2:3])[:, :energy_ref.shape[1]]


def place_call(layout, near, far):
    nz, plane, own = layout
    walk = nz * plane * own
    rows = (near[0].shape[0] - EXTRA) // own
    return pl.pallas_call(
        functools.partial(place_kernel, layout),
        out_shape=[
            jax.ShapeDtypeStruct((walk, rows, near[0].shape[1]), jnp.bfloat16),
            jax.ShapeDtypeStruct((1, walk), jnp.float32),
        ],
        cost_estimate=FREE,
        compiler_params=params(16),
        name="place_walkers",
    )(*in_vmem(*near, *far))


def per_device(chol_vals, chol_cols, greens, walkers, fields):
    vectors, rowblocks = chol_vals.shape[:2]
    walk, half_rows = greens.shape[:2]
    chips = lax.axis_size("chol")
    n_orb = lax.axis_size("orb")
    plane = 4 if chips % 4 == 0 else 1
    nz = chips // plane
    own = walk // chips
    layout = (nz, plane, own)
    step_factor = 72.0 / float(vectors * chips * BLOCK) ** 0.5

    def to_plane(a, dp):
        return lax.ppermute(a, "chol", [(c, (c // plane) * plane + hop(c % plane, dp, plane)) for c in range(chips)])

    def to_z(a, dz):
        return lax.ppermute(a, "chol", [(c, hop(c // plane, dz, nz) * plane + c % plane) for c in range(chips)])

    def around_orb(a):
        return [a] + [lax.ppermute(a, "orb", [((c + d) % n_orb, c) for c in range(n_orb)]) for d in range(1, n_orb)]

    cols = jnp.transpose(chol_cols, (1, 2, 0))
    turned, partial_bias, mine, cols = bias_call(chol_vals, greens, walkers, cols, own)
    start = around_orb(mine)
    bias, *others = around_orb(partial_bias)
    start, others = lax.optimization_barrier((start, others))

    units = 2 * rowblocks * BLOCK // CHUNK
    early_units = units // 8
    fields_t = fields.T
    def all_plane(arrays):
        return [to_plane(arrays[dp - 1], dp) for dp in reversed(range(1, plane))]

    z_order = [*range(2, nz), 1]

    def all_z(arrays):
        return [to_z(arrays[dz - 1], dz) for dz in z_order]

    late, energy = potential_call(early_units, units, layout, True, fields_t, bias, others, cols, turned)
    far, near = late[:plane], late[plane:]
    early, _ = potential_call(0, early_units, layout, False, fields_t, bias, others, cols, turned)
    early_came = all_z(early[1:])
    merged = merge_call([early[0], *early_came], near)
    far_came = all_z(sum_call([far[0], *all_plane(far[1:])], merged[:1]))
    found = finish_call(step_factor, far_came, [merged[0], *all_plane(merged[1:])])

    piece = series_call(around_orb(found), start, energy)
    near = [piece, *(to_plane(piece, dp) for dp in range(1, plane))]
    came = all_z([piece] * (nz - 1))
    pieces, *near[2:] = stack_call(near[2:], came[::-1], [dz - 1 for dz in z_order[::-1]])
    far = {dp: to_plane(pieces, dp) for dp in reversed(range(1, plane))}
    moved, energy = place_call(layout, near, [pieces, *(far[dp] for dp in range(1, plane))])
    return moved, energy.reshape(walk)


def solution(mesh):
    in_specs = (
        P("chol", "orb", None, None),
        P("chol", "orb", None),
        P("walker", "orb", None),
        P("walker", "orb", None),
        P("chol", "walker"),
    )
    out_specs = (P("walker", "orb", None), P("walker"))
    return jax.shard_map(
        per_device, mesh=mesh, in_specs=in_specs, out_specs=out_specs, check_vma=False
    )
```

```python
import functools

import jax
import jax.numpy as jnp
from jax import lax
from jax.experimental import pallas as pl
from jax.experimental.pallas import tpu as pltpu
from jax.sharding import PartitionSpec as P

BLOCK = 64
TAYLOR = 4
LANES = 2 * BLOCK
CHUNK = 16
EXTRA = 8
MIB = 1024 * 1024


FREE = pl.CostEstimate(flops=0, bytes_accessed=0, transcendentals=0)


def params(mib):
    return pltpu.CompilerParams(vmem_limit_bytes=mib * MIB)


def split(value):
    parts = []
    for _ in range(3):
        parts.append(value.astype(jnp.bfloat16))
        value = value - parts[-1].astype(jnp.float32)
    return parts


def in_vmem(*arrays):
    return [pltpu.with_memory_space_constraint(a, pltpu.VMEM) for a in arrays]


def in_hbm(*arrays):
    return [pltpu.with_memory_space_constraint(a, pltpu.HBM) for a in arrays]


def hop(at, distance, count):
    return at ^ distance if count & (count - 1) == 0 else (at + distance) % count


def swap_matrix():
    to = lax.broadcasted_iota(jnp.int32, (CHUNK * CHUNK, CHUNK * CHUNK), 0)
    at = lax.broadcasted_iota(jnp.int32, (CHUNK * CHUNK, CHUNK * CHUNK), 1)
    same = (to // CHUNK == at % CHUNK) & (to % CHUNK == at // CHUNK)
    return same.astype(jnp.float32).astype(jnp.bfloat16)


def column_order(row):
    other = 2 - 2 * (row // 2)
    return row, row + 1 - 2 * (row % 2), other, other + 1


def slot_masks(cols, row):
    return [cols == column for column in column_order(row)[1:]]


def bias_kernel(vals_hbm, greens_hbm, walkers_hbm, cols_hbm, turned_ref, bias_ref, mine_ref, cols_ref, vals, greens, swap, packed,
                gs, acc, vsem, gsem, wsem, csem):
    total_steps, vectors = turned_ref.shape[:2]
    walk = bias_ref.shape[0]
    steps = BLOCK // CHUNK

    def copies(t):
        rows = pl.ds(lax.rem(t, steps) * CHUNK, CHUNK)
        return (
            pltpu.make_async_copy(vals_hbm.at[:, lax.div(t, steps), rows, :], vals.at[t], vsem.at[t]),
            pltpu.make_async_copy(greens_hbm.at[:, pl.ds(t * CHUNK, CHUNK), :], greens.at[t], gsem.at[t]),
        )

    def begin(t, carry):
        for copy in copies(t):
            copy.start()
        return carry

    own = mine_ref.shape[0]
    take = pltpu.make_async_copy(walkers_hbm.at[pl.ds(lax.axis_index("chol") * own, own)], mine_ref, wsem)
    take.start()
    take_cols = pltpu.make_async_copy(cols_hbm, cols_ref, csem)
    take_cols.start()
    lax.fori_loop(0, total_steps, begin, 0)
    swap[...] = swap_matrix()
    bias_ref[...] = jnp.zeros_like(bias_ref)
    first = lax.broadcasted_iota(jnp.int32, (CHUNK, LANES), 1) < BLOCK
    kept_shape = (LANES, 4 * walk)
    kept = (lax.broadcasted_iota(jnp.int32, kept_shape, 0) < BLOCK) == (lax.broadcasted_iota(jnp.int32, kept_shape, 1) < walk)

    def step(t, side):
        for copy in copies(t):
            copy.wait()
        local = lax.div(t, steps)
        row = lax.axis_index("orb") * cols_ref.shape[0] + local
        upper = row // 2 == 1
        odd = row % 2 == 1
        for w in range(0, walk, CHUNK):
            mixed = greens[t, w:w + CHUNK].reshape(CHUNK * CHUNK, 2 * LANES)
            mixed = jnp.dot(swap[...], mixed, preferred_element_type=jnp.float32)
            pair = jnp.where(upper, mixed[:, LANES:], mixed[:, :LANES])
            rest = jnp.where(upper, mixed[:, :LANES], mixed[:, LANES:])
            pair = jnp.where(odd, pltpu.roll(pair, BLOCK, 1), pair)
            pair_turned = pltpu.roll(pair, BLOCK, 1)
            rest_turned = pltpu.roll(rest, BLOCK, 1)
            for i in range(0, CHUNK, 2):
                even, odd_row = slice(i * CHUNK, (i + 1) * CHUNK), slice((i + 1) * CHUNK, (i + 2) * CHUNK)
                pieces = (
                    jnp.where(first, pair[even], pair_turned[odd_row]),
                    jnp.where(first, pair_turned[odd_row], pair[even]),
                    jnp.where(first, rest[odd_row], rest_turned[even]),
                    jnp.where(first, rest_turned[odd_row], rest[even]),
                )
                for k, piece in enumerate(pieces):
                    packed[side, i // 2, k * walk + w:k * walk + w + CHUNK, :] = piece.astype(jnp.bfloat16)
        for i in range(0, CHUNK, 2):
            both = packed[side, i // 2].T.astype(jnp.float32)
            swapped = jnp.concatenate([both[BLOCK:], both[:BLOCK]], axis=0)
            gs[side, i * LANES:(i + 1) * LANES] = jnp.where(kept, both, 0.0).astype(jnp.bfloat16)
            gs[side, (i + 1) * LANES:(i + 2) * LANES] = jnp.where(kept, swapped, 0.0).astype(jnp.bfloat16)
        for g in range(0, vectors, 2 * CHUNK):
            both = [vals[t, g + k * CHUNK:g + (k + 1) * CHUNK].reshape(CHUNK * CHUNK, LANES) for k in range(2)]
            both = jnp.dot(swap[...], jnp.concatenate(both, axis=1), preferred_element_type=jnp.float32)
            both = both.astype(jnp.bfloat16)
            for i in range(CHUNK):
                for k in range(2):
                    turned_ref[t, g + k * CHUNK:g + (k + 1) * CHUNK, i * LANES:(i + 1) * LANES] = (
                        both[i * CHUNK:(i + 1) * CHUNK, k * LANES:(k + 1) * LANES]
                    )
        part = lax.dot_general(
            turned_ref[t], gs[side], (((1,), (0,)), ((), ())), preferred_element_type=jnp.float32
        )
        begins = lax.rem(t, steps) == 0
        acc[...] = jnp.where(begins, 0.0, acc[...]) + part

        @pl.when(lax.rem(t, steps) == steps - 1)
        def _():
            flat = acc[...].T
            total = flat[0:walk]
            cols = cols_ref[local, 1:2, :]
            for k, mask in enumerate(slot_masks(cols, row)):
                total = total + jnp.where(mask, flat[(k + 1) * walk:(k + 2) * walk], 0.0)
            bias_ref[...] += total

    def pair(t, carry):
        step(2 * t, 0)
        step(2 * t + 1, 1)
        return carry

    acc[...] = jnp.zeros_like(acc)
    take_cols.wait()
    lax.fori_loop(0, total_steps // 2, pair, 0)
    take.wait()


def bias_call(vals, greens, walkers, cols, own):
    vectors, rowblocks = vals.shape[:2]
    walk, half_rows, norb = greens.shape
    steps = half_rows // CHUNK
    wide = CHUNK * LANES
    return pl.pallas_call(
        bias_kernel,
        in_specs=[
            *[pl.BlockSpec(memory_space=pl.ANY)] * 4,
        ],
        out_specs=[pl.BlockSpec(memory_space=pltpu.VMEM)] * 4,
        out_shape=[
            pltpu.VMEM((steps, vectors, wide), jnp.bfloat16),
            pltpu.VMEM((walk, vectors), jnp.float32),
            pltpu.VMEM((own, *walkers.shape[1:]), jnp.bfloat16),
            pltpu.VMEM(cols.shape, jnp.int32),
        ],
        scratch_shapes=[
            pltpu.VMEM((steps, vectors, CHUNK, LANES), jnp.bfloat16),
            pltpu.VMEM((steps, walk, CHUNK, norb), jnp.bfloat16),
            pltpu.VMEM((CHUNK * CHUNK, CHUNK * CHUNK), jnp.bfloat16),
            pltpu.VMEM((2, CHUNK // 2, 4 * walk, LANES), jnp.bfloat16),
            pltpu.VMEM((2, wide, 4 * walk), jnp.bfloat16),
            pltpu.VMEM((vectors, 4 * walk), jnp.float32),
            pltpu.SemaphoreType.DMA((steps,)),
            pltpu.SemaphoreType.DMA((steps,)),
            pltpu.SemaphoreType.DMA,
            pltpu.SemaphoreType.DMA,
        ],
        cost_estimate=FREE,
        compiler_params=params(24),
        name="force_bias",
    )(*in_hbm(vals, greens, walkers, cols))


def potential_kernel(begin, end, layout, by_plane, fields_ref, own_ref, *refs):
    nz, plane, own = layout
    others = refs[:lax.axis_size("orb") - 1]
    cols_ref, turned_ref = refs[len(others):len(others) + 2]
    groups = 2 * plane if by_plane else nz
    outs = refs[len(others) + 2:len(others) + 2 + groups]
    energy_ref, s_ref, swap = refs[len(others) + 2 + groups:]
    walk, vectors = fields_ref.shape
    rowblocks = cols_ref.shape[0]

    me = lax.axis_index("chol")
    bias = own_ref[...]
    for other in others:
        bias = bias + other[...]
    energy = 0.5 * jnp.sum(bias * bias, axis=1, keepdims=True)
    energy_ref[...] = jnp.zeros_like(energy_ref)
    energy_ref[:, :walk] = jnp.broadcast_to(energy, (walk, LANES)).T[:CHUNK]
    shifted = (fields_ref[...] - bias).astype(jnp.bfloat16)
    at = lax.broadcasted_iota(jnp.int32, (walk, walk), 0)
    source = lax.broadcasted_iota(jnp.int32, (walk, walk), 1)
    chip = at // own
    z = hop(me // plane, chip // plane, nz)
    p = hop(me % plane, chip % plane, plane)
    wanted = (z * plane + p) * own + at % own
    pick = (wanted == source).astype(jnp.float32).astype(jnp.bfloat16)
    ordered = jnp.dot(pick, shifted, preferred_element_type=jnp.float32)
    for local in range(rowblocks):
        row = lax.axis_index("orb") * rowblocks + local
        s_ref[local, 0:walk] = ordered.astype(jnp.bfloat16)
        for k, mask in enumerate(slot_masks(cols_ref[local, 1:2, :], row)):
            s_ref[local, (k + 1) * walk:(k + 2) * walk] = jnp.where(mask, ordered, 0.0).astype(jnp.bfloat16)
    swap[...] = swap_matrix()
    first = lax.broadcasted_iota(jnp.int32, (walk, LANES), 1) < BLOCK

    def step(t, halves=(0, 1)):
        left = s_ref[lax.div(t, BLOCK // CHUNK)]
        tiles = []
        for i in range(0, CHUNK, 2):
            both = jnp.dot(left, turned_ref[t, :, i * LANES:(i + 2) * LANES], preferred_element_type=jnp.float32)
            for side in range(2):
                out = both[:, side * LANES:(side + 1) * LANES]
                near = jnp.where(first, out[0:walk], out[walk:2 * walk])
                far = jnp.where(first, pltpu.roll(out[2 * walk:3 * walk], BLOCK, 1), out[3 * walk:])
                wanted = [(near, far)[half] for half in halves]
                tiles.append(jnp.concatenate(wanted, axis=1).astype(jnp.bfloat16))
        for w0 in range(0, walk, CHUNK):
            mixed = jnp.concatenate([tile[w0:w0 + CHUNK] for tile in tiles], axis=0)
            mixed = jnp.dot(swap[...], mixed, preferred_element_type=jnp.float32).astype(jnp.bfloat16)
            for w in range(CHUNK):
                chip, j = (w0 + w) // own, (w0 + w) % own
                dz, dp = chip // plane, chip % plane
                if not by_plane:
                    out, inner = outs[dz], (dp,)
                elif dz:
                    out, inner = outs[dp], (dz - 1,)
                else:
                    out, inner = outs[plane + dp], ()
                for k, half in enumerate(halves):
                    at = (2 * t + half - begin) * CHUNK
                    rows = pl.ds(at if isinstance(t, int) else pl.multiple_of(at, CHUNK), CHUNK)
                    out[(*inner, j, rows)] = mixed[w * CHUNK:(w + 1) * CHUNK, k * LANES:(k + 1) * LANES]

    def pair(t, carry):
        step(from_step + 2 * t)
        step(from_step + 2 * t + 1)
        return carry

    from_step, to_step = (begin + 1) // 2, end // 2
    if begin % 2:
        step(begin // 2, (1,))
    lax.fori_loop(0, (to_step - from_step) // 2, pair, 0)
    if (to_step - from_step) % 2:
        step(to_step - 1)
    if end % 2:
        step(end // 2, (0,))


def potential_call(begin, end, layout, by_plane, fields, bias, others, cols, turned):
    nz, plane, own = layout
    walk, vectors = fields.shape
    leading = [(nz - 1,)] * plane + [()] * plane if by_plane else [(plane,)] * nz
    rows = (end - begin) * CHUNK
    *parts, energy = pl.pallas_call(
        functools.partial(potential_kernel, begin, end, layout, by_plane),
        out_shape=[
            *[pltpu.VMEM((*inner, own, rows, LANES), jnp.bfloat16) for inner in leading],
            pltpu.VMEM((CHUNK, LANES), jnp.float32),
        ],
        scratch_shapes=[
            pltpu.VMEM((cols.shape[0], 4 * walk, vectors), jnp.bfloat16),
            pltpu.VMEM((CHUNK * CHUNK, CHUNK * CHUNK), jnp.bfloat16),
        ],
        cost_estimate=FREE,
        compiler_params=params(16),
        name="potential",
    )(fields, *in_vmem(bias, *others, cols, turned))
    return parts, energy


def add(refs, *at):
    total = refs[0][at].astype(jnp.float32)
    for ref in refs[1:]:
        total = total + ref[at].astype(jnp.float32)
    return total


def vmem_call(kernel, name, out_shape, *arrays):
    return pl.pallas_call(
        kernel, out_shape=out_shape, cost_estimate=FREE, compiler_params=params(16), name=name
    )(*in_vmem(*arrays))


def sum_call(arrays, after):
    def kernel(*refs):
        for k, out in enumerate(refs[len(arrays) + len(after):]):
            out[...] = add(refs[:len(arrays)], k).astype(out.dtype)

    out_shape = [pltpu.VMEM(arrays[0].shape[1:], jnp.bfloat16)] * arrays[0].shape[0]
    return vmem_call(kernel, "sum_parts", out_shape, *arrays, *after)


def merge_call(early, near):
    own, rows, lanes = early[0].shape[1:]

    def kernel(*refs):
        early_refs, near_refs, outs = refs[:len(early)], refs[len(early):len(early) + len(near)], refs[-len(near):]
        for k, (ref, out) in enumerate(zip(near_refs, outs)):
            out[:, :rows] = add(early_refs, k).astype(out.dtype)
            out[:, rows:] = ref[...]

    out_shape = [pltpu.VMEM((own, rows + near[0].shape[1], lanes), jnp.bfloat16)] * len(near)
    return vmem_call(kernel, "merge_parts", out_shape, *early, *near)


def finish_call(factor, far, merged):
    early = merged[0].shape[1] - far[0].shape[1]

    def kernel(*refs):
        far_refs, merged_refs, out = refs[:len(far)], refs[len(far):-1], refs[-1]
        rowblocks = out.shape[1] // (2 * BLOCK)
        for unit in range(out.shape[1] // CHUNK):
            at = unit * CHUNK
            for j in range(out.shape[0]):
                total = add(merged_refs, j, slice(at, at + CHUNK))
                if at >= early:
                    total = total + add(far_refs, j, slice(at - early, at - early + CHUNK))
                if unit % 2 == 0:
                    row = lax.axis_index("orb") * rowblocks + at // (2 * BLOCK)
                    total = jnp.where(row % 2 == 1, pltpu.roll(total, BLOCK, 1), total)
                out[j, at:at + CHUNK] = (factor * total).astype(out.dtype)

    return vmem_call(kernel, "finish", pltpu.VMEM(merged[0].shape, jnp.bfloat16), *far, *merged)


def stack_call(near, pieces, slots):
    def kernel(*refs):
        ins, outs = refs[:len(pieces) + len(near)], refs[len(pieces) + len(near):]
        for ref, slot in zip(ins[len(near):], slots):
            outs[0][slot] = ref[...]
        for ref, out in zip(ins, outs[1:]):
            out[...] = ref[...]

    one = pltpu.VMEM(pieces[0].shape, jnp.bfloat16)
    out_shape = [pltpu.VMEM((len(pieces), *pieces[0].shape), jnp.bfloat16)] + [one] * len(near)
    return vmem_call(kernel, "stack_pieces", out_shape, *near, *pieces)


def series_kernel(n_orb, *refs):
    found, start = refs[:n_orb], refs[n_orb:2 * n_orb]
    energy_ref, moved_ref, pot, begin, total = refs[2 * n_orb:]
    me = lax.axis_index("orb")
    own, half_rows = start[0].shape[:2]
    per = BLOCK // CHUNK
    for d in range(n_orb):
        at = lax.rem(me + d, n_orb)
        begin[:, pl.ds(pl.multiple_of(at * half_rows, half_rows), half_rows)] = start[d][...]
        for t in range(half_rows // CHUNK):
            row = at * (half_rows // BLOCK) + t // per
            rows = pl.ds(pl.multiple_of(row * BLOCK + t % per * CHUNK, CHUNK), CHUNK)
            for half in range(2):
                side = lax.rem(lax.div(row, 2) + half, 2)
                lanes = pl.ds(pl.multiple_of(side * LANES, LANES), LANES)
                pot[:, rows, lanes] = found[d][:, (2 * t + half) * CHUNK:(2 * t + half + 1) * CHUNK]
    terms = [begin[j] for j in range(own)]
    sums = [term.astype(jnp.float32) for term in terms]
    added = [jnp.zeros(terms[0].shape, jnp.float32)] * own
    for degree in range(1, TAYLOR + 1):
        for j in range(own):
            product = jnp.dot(pot[j], terms[j], preferred_element_type=jnp.float32)
            terms[j] = (product / degree).astype(jnp.bfloat16)
            added[j] = added[j] + terms[j].astype(jnp.float32)
    for j in range(own):
        total[j] = (sums[j] + added[j]).astype(jnp.bfloat16)
    mine = total[:, pl.ds(pl.multiple_of(me * half_rows, half_rows), half_rows)]
    at = lax.broadcasted_iota(jnp.int32, (EXTRA, LANES), 0)
    high, middle, low = (part.astype(jnp.float32) for part in split(energy_ref[:EXTRA]))
    tile = jnp.where(at == 0, high, jnp.where(at == 1, middle, jnp.where(at == 2, low, 0.0)))
    moved_ref[:own * half_rows] = mine.reshape(own * half_rows, mine.shape[2])
    moved_ref[own * half_rows:] = tile.astype(jnp.bfloat16)


def series_call(found, start, energy):
    n_orb = len(found)
    own, half_rows, nocc = start[0].shape
    return pl.pallas_call(
        functools.partial(series_kernel, n_orb),
        out_shape=pltpu.VMEM((own * half_rows + EXTRA, nocc), jnp.bfloat16),
        scratch_shapes=[
            pltpu.VMEM((own, n_orb * half_rows, 2 * LANES), jnp.bfloat16),
            pltpu.VMEM((own, n_orb * half_rows, nocc), jnp.bfloat16),
            pltpu.VMEM((own, n_orb * half_rows, nocc), jnp.bfloat16),
        ],
        cost_estimate=FREE,
        compiler_params=params(16),
        name="series",
    )(*in_vmem(*found, *start, energy))


def place_kernel(layout, *refs):
    nz, plane, own = layout
    near, far = refs[:plane], refs[plane:2 * plane]
    out, energy_ref = refs[2 * plane:]
    me = lax.axis_index("chol")
    rows = out.shape[1]
    energy = jnp.zeros((EXTRA, LANES), jnp.float32)
    for dp in range(plane):
        for dz in range(nz):
            z = hop(lax.div(me, plane), -dz if nz & (nz - 1) else dz, nz)
            p = hop(lax.rem(me, plane), -dp if plane & (plane - 1) else dp, plane)
            piece = far[dp].at[dz - 1] if dz else near[dp]
            for j in range(own):
                out[(z * plane + p) * own + j] = piece[j * rows:(j + 1) * rows]
            energy = energy + piece[own * rows:].astype(jnp.float32)
    energy_ref[...] = (energy[0:1] + energy[1:2] + energy[2:3])[:, :energy_ref.shape[1]]


def place_call(layout, near, far):
    nz, plane, own = layout
    walk = nz * plane * own
    rows = (near[0].shape[0] - EXTRA) // own
    return pl.pallas_call(
        functools.partial(place_kernel, layout),
        out_shape=[
            jax.ShapeDtypeStruct((walk, rows, near[0].shape[1]), jnp.bfloat16),
            jax.ShapeDtypeStruct((1, walk), jnp.float32),
        ],
        cost_estimate=FREE,
        compiler_params=params(16),
        name="place_walkers",
    )(*in_vmem(*near, *far))


def per_device(chol_vals, chol_cols, greens, walkers, fields):
    vectors, rowblocks = chol_vals.shape[:2]
    walk, half_rows = greens.shape[:2]
    chips = lax.axis_size("chol")
    n_orb = lax.axis_size("orb")
    plane = 4 if chips % 4 == 0 else 1
    nz = chips // plane
    own = walk // chips
    layout = (nz, plane, own)
    step_factor = 72.0 / float(vectors * chips * BLOCK) ** 0.5

    def to_plane(a, dp):
        return lax.ppermute(a, "chol", [(c, (c // plane) * plane + hop(c % plane, dp, plane)) for c in range(chips)])

    def to_z(a, dz):
        return lax.ppermute(a, "chol", [(c, hop(c // plane, dz, nz) * plane + c % plane) for c in range(chips)])

    def around_orb(a):
        return [a] + [lax.ppermute(a, "orb", [((c + d) % n_orb, c) for c in range(n_orb)]) for d in range(1, n_orb)]

    cols = jnp.transpose(chol_cols, (1, 2, 0))
    turned, partial_bias, mine, cols = bias_call(chol_vals, greens, walkers, cols, own)
    start = around_orb(mine)
    bias, *others = around_orb(partial_bias)
    start, others = lax.optimization_barrier((start, others))

    units = 2 * rowblocks * BLOCK // CHUNK
    early_units = units // 8
    fields_t = fields.T
    def all_plane(arrays):
        return [to_plane(arrays[dp - 1], dp) for dp in reversed(range(1, plane))]

    z_order = [*range(2, nz), 1]

    def all_z(arrays):
        return [to_z(arrays[dz - 1], dz) for dz in z_order]

    late, energy = potential_call(early_units, units, layout, True, fields_t, bias, others, cols, turned)
    far, near = late[:plane], late[plane:]
    early, _ = potential_call(0, early_units, layout, False, fields_t, bias, others, cols, turned)
    early_came = all_z(early[1:])
    merged = merge_call([early[0], *early_came], near)
    far_came = all_z(sum_call([far[0], *all_plane(far[1:])], merged[:1]))
    found = finish_call(step_factor, far_came, [merged[0], *all_plane(merged[1:])])

    piece = series_call(around_orb(found), start, energy)
    near = [piece, *(to_plane(piece, dp) for dp in range(1, plane))]
    came = all_z([piece] * (nz - 1))
    pieces, *near[2:] = stack_call(near[2:], came[::-1], [dz - 1 for dz in z_order[::-1]])
    far = {dp: to_plane(pieces, dp) for dp in reversed(range(1, plane))}
    moved, energy = place_call(layout, near, [pieces, *(far[dp] for dp in range(1, plane))])
    return moved, energy.reshape(walk)


def solution(mesh):
    in_specs = (
        P("chol", "orb", None, None),
        P("chol", "orb", None),
        P("walker", "orb", None),
        P("walker", "orb", None),
        P("chol", "walker"),
    )
    out_specs = (P("walker", "orb", None), P("walker"))
    return jax.shard_map(
        per_device, mesh=mesh, in_specs=in_specs, out_specs=out_specs, check_vma=False
    )
```

```python
import functools

import jax
import jax.numpy as jnp
from jax import lax
from jax.experimental import pallas as pl
from jax.experimental.pallas import tpu as pltpu
from jax.sharding import PartitionSpec as P

BLOCK = 64
TAYLOR = 4
LANES = 2 * BLOCK
CHUNK = 16
EXTRA = 8
MIB = 1024 * 1024


FREE = pl.CostEstimate(flops=0, bytes_accessed=0, transcendentals=0)


def params(mib):
    return pltpu.CompilerParams(vmem_limit_bytes=mib * MIB)


def split(value):
    parts = []
    for _ in range(3):
        parts.append(value.astype(jnp.bfloat16))
        value = value - parts[-1].astype(jnp.float32)
    return parts


def in_vmem(*arrays):
    return [pltpu.with_memory_space_constraint(a, pltpu.VMEM) for a in arrays]


def in_hbm(*arrays):
    return [pltpu.with_memory_space_constraint(a, pltpu.HBM) for a in arrays]


def hop(at, distance, count):
    return at ^ distance if count & (count - 1) == 0 else (at + distance) % count


def swap_matrix():
    to = lax.broadcasted_iota(jnp.int32, (CHUNK * CHUNK, CHUNK * CHUNK), 0)
    at = lax.broadcasted_iota(jnp.int32, (CHUNK * CHUNK, CHUNK * CHUNK), 1)
    same = (to // CHUNK == at % CHUNK) & (to % CHUNK == at // CHUNK)
    return same.astype(jnp.float32).astype(jnp.bfloat16)


def column_order(row):
    other = 2 - 2 * (row // 2)
    return row, row + 1 - 2 * (row % 2), other, other + 1


def slot_masks(cols, row):
    return [cols == column for column in column_order(row)[1:]]


def bias_kernel(vals_hbm, greens_hbm, walkers_hbm, cols_hbm, turned_ref, bias_ref, mine_ref, cols_ref, vals, greens, swap, gs,
                acc, vsem, gsem, wsem, csem):
    total_steps, vectors = turned_ref.shape[:2]
    walk = bias_ref.shape[0]
    steps = BLOCK // CHUNK

    def copies(t):
        rows = pl.ds(lax.rem(t, steps) * CHUNK, CHUNK)
        return (
            pltpu.make_async_copy(vals_hbm.at[:, lax.div(t, steps), rows, :], vals.at[t], vsem.at[t]),
            pltpu.make_async_copy(greens_hbm.at[:, pl.ds(t * CHUNK, CHUNK), :], greens.at[t], gsem.at[t]),
        )

    def begin(t, carry):
        for copy in copies(t):
            copy.start()
        return carry

    own = mine_ref.shape[0]
    take = pltpu.make_async_copy(walkers_hbm.at[pl.ds(lax.axis_index("chol") * own, own)], mine_ref, wsem)
    take.start()
    take_cols = pltpu.make_async_copy(cols_hbm, cols_ref, csem)
    take_cols.start()
    lax.fori_loop(0, total_steps, begin, 0)
    swap[...] = swap_matrix()
    bias_ref[...] = jnp.zeros_like(bias_ref)
    first = lax.broadcasted_iota(jnp.int32, (CHUNK * CHUNK, LANES), 1) < BLOCK

    def step(t, side):
        for copy in copies(t):
            copy.wait()
        local = lax.div(t, steps)
        row = lax.axis_index("orb") * cols_ref.shape[0] + local
        upper = row // 2 == 1
        odd = row % 2 == 1
        for w in range(0, walk, CHUNK):
            mixed = greens[t, w:w + CHUNK].reshape(CHUNK * CHUNK, 2 * LANES)
            mixed = jnp.dot(swap[...], mixed, preferred_element_type=jnp.float32)
            pair = jnp.where(upper, mixed[:, LANES:], mixed[:, :LANES])
            rest = jnp.where(upper, mixed[:, :LANES], mixed[:, LANES:])
            pair = jnp.where(odd, pltpu.roll(pair, BLOCK, 1), pair)
            pieces = (
                jnp.where(first, pair, 0.0),
                jnp.where(first, 0.0, pair),
                jnp.where(first, 0.0, pltpu.roll(rest, BLOCK, 1)),
                jnp.where(first, 0.0, rest),
            )
            for k, piece in enumerate(pieces):
                piece = piece.astype(jnp.bfloat16)
                for i in range(CHUNK):
                    gs[side, k * walk + w:k * walk + w + CHUNK, i * LANES:(i + 1) * LANES] = (
                        piece[i * CHUNK:(i + 1) * CHUNK]
                    )
        for g in range(0, vectors, 2 * CHUNK):
            both = [vals[t, g + k * CHUNK:g + (k + 1) * CHUNK].reshape(CHUNK * CHUNK, LANES) for k in range(2)]
            both = jnp.dot(swap[...], jnp.concatenate(both, axis=1), preferred_element_type=jnp.float32)
            both = both.astype(jnp.bfloat16)
            for i in range(CHUNK):
                for k in range(2):
                    turned_ref[t, g + k * CHUNK:g + (k + 1) * CHUNK, i * LANES:(i + 1) * LANES] = (
                        both[i * CHUNK:(i + 1) * CHUNK, k * LANES:(k + 1) * LANES]
                    )
        part = lax.dot_general(
            turned_ref[t], gs[side], (((1,), (1,)), ((), ())), preferred_element_type=jnp.float32
        )
        begins = lax.rem(t, steps) == 0
        acc[...] = jnp.where(begins, 0.0, acc[...]) + part

        @pl.when(lax.rem(t, steps) == steps - 1)
        def _():
            flat = acc[...].T
            total = flat[0:walk]
            cols = cols_ref[local, 1:2, :]
            for k, mask in enumerate(slot_masks(cols, row)):
                total = total + jnp.where(mask, flat[(k + 1) * walk:(k + 2) * walk], 0.0)
            bias_ref[...] += total

    def pair(t, carry):
        step(2 * t, 0)
        step(2 * t + 1, 1)
        return carry

    acc[...] = jnp.zeros_like(acc)
    take_cols.wait()
    lax.fori_loop(0, total_steps // 2, pair, 0)
    take.wait()


def bias_call(vals, greens, walkers, cols, own):
    vectors, rowblocks = vals.shape[:2]
    walk, half_rows, norb = greens.shape
    steps = half_rows // CHUNK
    wide = CHUNK * LANES
    return pl.pallas_call(
        bias_kernel,
        in_specs=[
            *[pl.BlockSpec(memory_space=pl.ANY)] * 4,
        ],
        out_specs=[pl.BlockSpec(memory_space=pltpu.VMEM)] * 4,
        out_shape=[
            pltpu.VMEM((steps, vectors, wide), jnp.bfloat16),
            pltpu.VMEM((walk, vectors), jnp.float32),
            pltpu.VMEM((own, *walkers.shape[1:]), jnp.bfloat16),
            pltpu.VMEM(cols.shape, jnp.int32),
        ],
        scratch_shapes=[
            pltpu.VMEM((steps, vectors, CHUNK, LANES), jnp.bfloat16),
            pltpu.VMEM((steps, walk, CHUNK, norb), jnp.bfloat16),
            pltpu.VMEM((CHUNK * CHUNK, CHUNK * CHUNK), jnp.bfloat16),
            pltpu.VMEM((2, 4 * walk, wide), jnp.bfloat16),
            pltpu.VMEM((vectors, 4 * walk), jnp.float32),
            pltpu.SemaphoreType.DMA((steps,)),
            pltpu.SemaphoreType.DMA((steps,)),
            pltpu.SemaphoreType.DMA,
            pltpu.SemaphoreType.DMA,
        ],
        cost_estimate=FREE,
        compiler_params=params(24),
        name="force_bias",
    )(*in_hbm(vals, greens, walkers, cols))


def potential_kernel(begin, end, layout, by_plane, fields_ref, own_ref, *refs):
    nz, plane, own = layout
    others = refs[:lax.axis_size("orb") - 1]
    cols_ref, turned_ref = refs[len(others):len(others) + 2]
    groups = 2 * plane if by_plane else nz
    outs = refs[len(others) + 2:len(others) + 2 + groups]
    energy_ref, s_ref, swap = refs[len(others) + 2 + groups:]
    walk, vectors = fields_ref.shape
    rowblocks = cols_ref.shape[0]

    me = lax.axis_index("chol")
    bias = own_ref[...]
    for other in others:
        bias = bias + other[...]
    energy_ref[...] = jnp.zeros_like(energy_ref)
    if not by_plane:
        energy = 0.5 * jnp.sum(bias * bias, axis=1, keepdims=True)
        energy_ref[:, :walk] = jnp.broadcast_to(energy, (walk, LANES)).T[:CHUNK]
    shifted = (fields_ref[...] - bias).astype(jnp.bfloat16)
    at = lax.broadcasted_iota(jnp.int32, (walk, walk), 0)
    source = lax.broadcasted_iota(jnp.int32, (walk, walk), 1)
    chip = at // own
    z = hop(me // plane, chip // plane, nz)
    p = hop(me % plane, chip % plane, plane)
    wanted = (z * plane + p) * own + at % own
    pick = (wanted == source).astype(jnp.float32).astype(jnp.bfloat16)
    ordered = jnp.dot(pick, shifted, preferred_element_type=jnp.float32)
    for local in range(rowblocks):
        row = lax.axis_index("orb") * rowblocks + local
        s_ref[local, 0:walk] = ordered.astype(jnp.bfloat16)
        for k, mask in enumerate(slot_masks(cols_ref[local, 1:2, :], row)):
            s_ref[local, (k + 1) * walk:(k + 2) * walk] = jnp.where(mask, ordered, 0.0).astype(jnp.bfloat16)
    swap[...] = swap_matrix()
    first = lax.broadcasted_iota(jnp.int32, (walk, LANES), 1) < BLOCK

    def step(t, halves=(0, 1)):
        left = s_ref[lax.div(t, BLOCK // CHUNK)]
        tiles = []
        for i in range(0, CHUNK, 2):
            both = jnp.dot(left, turned_ref[t, :, i * LANES:(i + 2) * LANES], preferred_element_type=jnp.float32)
            for side in range(2):
                out = both[:, side * LANES:(side + 1) * LANES]
                near = jnp.where(first, out[0:walk], out[walk:2 * walk])
                far = jnp.where(first, pltpu.roll(out[2 * walk:3 * walk], BLOCK, 1), out[3 * walk:])
                wanted = [(near, far)[half] for half in halves]
                tiles.append(jnp.concatenate(wanted, axis=1).astype(jnp.bfloat16))
        for w0 in range(0, walk, CHUNK):
            mixed = jnp.concatenate([tile[w0:w0 + CHUNK] for tile in tiles], axis=0)
            mixed = jnp.dot(swap[...], mixed, preferred_element_type=jnp.float32).astype(jnp.bfloat16)
            for w in range(CHUNK):
                chip, j = (w0 + w) // own, (w0 + w) % own
                dz, dp = chip // plane, chip % plane
                if not by_plane:
                    out, inner = outs[dz], (dp,)
                elif dz:
                    out, inner = outs[dp], (dz - 1,)
                else:
                    out, inner = outs[plane + dp], ()
                for k, half in enumerate(halves):
                    at = (2 * t + half - begin) * CHUNK
                    rows = pl.ds(at if isinstance(t, int) else pl.multiple_of(at, CHUNK), CHUNK)
                    out[(*inner, j, rows)] = mixed[w * CHUNK:(w + 1) * CHUNK, k * LANES:(k + 1) * LANES]

    def pair(t, carry):
        step(from_step + 2 * t)
        step(from_step + 2 * t + 1)
        return carry

    from_step, to_step = (begin + 1) // 2, end // 2
    if begin % 2:
        step(begin // 2, (1,))
    lax.fori_loop(0, (to_step - from_step) // 2, pair, 0)
    if (to_step - from_step) % 2:
        step(to_step - 1)
    if end % 2:
        step(end // 2, (0,))


def potential_call(begin, end, layout, by_plane, fields, bias, others, cols, turned):
    nz, plane, own = layout
    walk, vectors = fields.shape
    leading = [(nz - 1,)] * plane + [()] * plane if by_plane else [(plane,)] * nz
    rows = (end - begin) * CHUNK
    *parts, energy = pl.pallas_call(
        functools.partial(potential_kernel, begin, end, layout, by_plane),
        out_shape=[
            *[pltpu.VMEM((*inner, own, rows, LANES), jnp.bfloat16) for inner in leading],
            pltpu.VMEM((CHUNK, LANES), jnp.float32),
        ],
        scratch_shapes=[
            pltpu.VMEM((cols.shape[0], 4 * walk, vectors), jnp.bfloat16),
            pltpu.VMEM((CHUNK * CHUNK, CHUNK * CHUNK), jnp.bfloat16),
        ],
        cost_estimate=FREE,
        compiler_params=params(16),
        name="potential",
    )(fields, *in_vmem(bias, *others, cols, turned))
    return parts, energy


def add(refs, *at):
    total = refs[0][at].astype(jnp.float32)
    for ref in refs[1:]:
        total = total + ref[at].astype(jnp.float32)
    return total


def vmem_call(kernel, name, out_shape, *arrays):
    return pl.pallas_call(
        kernel, out_shape=out_shape, cost_estimate=FREE, compiler_params=params(16), name=name
    )(*in_vmem(*arrays))


def sum_call(arrays, after):
    def kernel(*refs):
        for k, out in enumerate(refs[len(arrays) + len(after):]):
            out[...] = add(refs[:len(arrays)], k).astype(out.dtype)

    out_shape = [pltpu.VMEM(arrays[0].shape[1:], jnp.bfloat16)] * arrays[0].shape[0]
    return vmem_call(kernel, "sum_parts", out_shape, *arrays, *after)


def merge_call(early, near):
    own, rows, lanes = early[0].shape[1:]

    def kernel(*refs):
        early_refs, near_refs, outs = refs[:len(early)], refs[len(early):len(early) + len(near)], refs[-len(near):]
        for k, (ref, out) in enumerate(zip(near_refs, outs)):
            out[:, :rows] = add(early_refs, k).astype(out.dtype)
            out[:, rows:] = ref[...]

    out_shape = [pltpu.VMEM((own, rows + near[0].shape[1], lanes), jnp.bfloat16)] * len(near)
    return vmem_call(kernel, "merge_parts", out_shape, *early, *near)


def finish_call(factor, far, merged):
    early = merged[0].shape[1] - far[0].shape[1]

    def kernel(*refs):
        far_refs, merged_refs, out = refs[:len(far)], refs[len(far):-1], refs[-1]
        rowblocks = out.shape[1] // (2 * BLOCK)
        for unit in range(out.shape[1] // CHUNK):
            at = unit * CHUNK
            for j in range(out.shape[0]):
                total = add(merged_refs, j, slice(at, at + CHUNK))
                if at >= early:
                    total = total + add(far_refs, j, slice(at - early, at - early + CHUNK))
                if unit % 2 == 0:
                    row = lax.axis_index("orb") * rowblocks + at // (2 * BLOCK)
                    total = jnp.where(row % 2 == 1, pltpu.roll(total, BLOCK, 1), total)
                out[j, at:at + CHUNK] = (factor * total).astype(out.dtype)

    return vmem_call(kernel, "finish", pltpu.VMEM(merged[0].shape, jnp.bfloat16), *far, *merged)


def stack_call(near, pieces, slots):
    def kernel(*refs):
        ins, outs = refs[:len(pieces) + len(near)], refs[len(pieces) + len(near):]
        for ref, slot in zip(ins[len(near):], slots):
            outs[0][slot] = ref[...]
        for ref, out in zip(ins, outs[1:]):
            out[...] = ref[...]

    one = pltpu.VMEM(pieces[0].shape, jnp.bfloat16)
    out_shape = [pltpu.VMEM((len(pieces), *pieces[0].shape), jnp.bfloat16)] + [one] * len(near)
    return vmem_call(kernel, "stack_pieces", out_shape, *near, *pieces)


def series_kernel(n_orb, *refs):
    found, start = refs[:n_orb], refs[n_orb:2 * n_orb]
    energy_ref, moved_ref, pot, begin, total = refs[2 * n_orb:]
    me = lax.axis_index("orb")
    own, half_rows = start[0].shape[:2]
    per = BLOCK // CHUNK
    for d in range(n_orb):
        at = lax.rem(me + d, n_orb)
        begin[:, pl.ds(pl.multiple_of(at * half_rows, half_rows), half_rows)] = start[d][...]
        for t in range(half_rows // CHUNK):
            row = at * (half_rows // BLOCK) + t // per
            rows = pl.ds(pl.multiple_of(row * BLOCK + t % per * CHUNK, CHUNK), CHUNK)
            for half in range(2):
                side = lax.rem(lax.div(row, 2) + half, 2)
                lanes = pl.ds(pl.multiple_of(side * LANES, LANES), LANES)
                pot[:, rows, lanes] = found[d][:, (2 * t + half) * CHUNK:(2 * t + half + 1) * CHUNK]
    terms = [begin[j] for j in range(own)]
    sums = [term.astype(jnp.float32) for term in terms]
    added = [jnp.zeros(terms[0].shape, jnp.float32)] * own
    for degree in range(1, TAYLOR + 1):
        for j in range(own):
            product = jnp.dot(pot[j], terms[j], preferred_element_type=jnp.float32)
            terms[j] = (product / degree).astype(jnp.bfloat16)
            added[j] = added[j] + terms[j].astype(jnp.float32)
    for j in range(own):
        total[j] = (sums[j] + added[j]).astype(jnp.bfloat16)
    mine = total[:, pl.ds(pl.multiple_of(me * half_rows, half_rows), half_rows)]
    at = lax.broadcasted_iota(jnp.int32, (EXTRA, LANES), 0)
    high, middle, low = (part.astype(jnp.float32) for part in split(energy_ref[:EXTRA]))
    tile = jnp.where(at == 0, high, jnp.where(at == 1, middle, jnp.where(at == 2, low, 0.0)))
    moved_ref[:own * half_rows] = mine.reshape(own * half_rows, mine.shape[2])
    moved_ref[own * half_rows:] = tile.astype(jnp.bfloat16)


def series_call(found, start, energy):
    n_orb = len(found)
    own, half_rows, nocc = start[0].shape
    return pl.pallas_call(
        functools.partial(series_kernel, n_orb),
        out_shape=pltpu.VMEM((own * half_rows + EXTRA, nocc), jnp.bfloat16),
        scratch_shapes=[
            pltpu.VMEM((own, n_orb * half_rows, 2 * LANES), jnp.bfloat16),
            pltpu.VMEM((own, n_orb * half_rows, nocc), jnp.bfloat16),
            pltpu.VMEM((own, n_orb * half_rows, nocc), jnp.bfloat16),
        ],
        cost_estimate=FREE,
        compiler_params=params(16),
        name="series",
    )(*in_vmem(*found, *start, energy))


def place_kernel(layout, *refs):
    nz, plane, own = layout
    near, far = refs[:plane], refs[plane:2 * plane]
    out, energy_ref = refs[2 * plane:]
    me = lax.axis_index("chol")
    rows = out.shape[1]
    energy = jnp.zeros((EXTRA, LANES), jnp.float32)
    for dp in range(plane):
        for dz in range(nz):
            z = hop(lax.div(me, plane), -dz if nz & (nz - 1) else dz, nz)
            p = hop(lax.rem(me, plane), -dp if plane & (plane - 1) else dp, plane)
            piece = far[dp].at[dz - 1] if dz else near[dp]
            for j in range(own):
                out[(z * plane + p) * own + j] = piece[j * rows:(j + 1) * rows]
            energy = energy + piece[own * rows:].astype(jnp.float32)
    energy_ref[...] = (energy[0:1] + energy[1:2] + energy[2:3])[:, :energy_ref.shape[1]]


def place_call(layout, near, far):
    nz, plane, own = layout
    walk = nz * plane * own
    rows = (near[0].shape[0] - EXTRA) // own
    return pl.pallas_call(
        functools.partial(place_kernel, layout),
        out_shape=[
            jax.ShapeDtypeStruct((walk, rows, near[0].shape[1]), jnp.bfloat16),
            jax.ShapeDtypeStruct((1, walk), jnp.float32),
        ],
        cost_estimate=FREE,
        compiler_params=params(16),
        name="place_walkers",
    )(*in_vmem(*near, *far))


def per_device(chol_vals, chol_cols, greens, walkers, fields):
    vectors, rowblocks = chol_vals.shape[:2]
    walk, half_rows = greens.shape[:2]
    chips = lax.axis_size("chol")
    n_orb = lax.axis_size("orb")
    plane = 4 if chips % 4 == 0 else 1
    nz = chips // plane
    own = walk // chips
    layout = (nz, plane, own)
    step_factor = 72.0 / float(vectors * chips * BLOCK) ** 0.5

    def to_plane(a, dp):
        return lax.ppermute(a, "chol", [(c, (c // plane) * plane + hop(c % plane, dp, plane)) for c in range(chips)])

    def to_z(a, dz):
        return lax.ppermute(a, "chol", [(c, hop(c // plane, dz, nz) * plane + c % plane) for c in range(chips)])

    def around_orb(a):
        return [a] + [lax.ppermute(a, "orb", [((c + d) % n_orb, c) for c in range(n_orb)]) for d in range(1, n_orb)]

    cols = jnp.transpose(chol_cols, (1, 2, 0))
    turned, partial_bias, mine, cols = bias_call(chol_vals, greens, walkers, cols, own)
    start = around_orb(mine)
    bias, *others = around_orb(partial_bias)

    units = 2 * rowblocks * BLOCK // CHUNK
    early_units = units // 8
    fields_t = fields.T
    def all_plane(arrays):
        return [to_plane(arrays[dp - 1], dp) for dp in reversed(range(1, plane))]

    z_order = [*range(2, nz), 1]

    def all_z(arrays):
        return [to_z(arrays[dz - 1], dz) for dz in z_order]

    late, _ = potential_call(early_units, units, layout, True, fields_t, bias, others, cols, turned)
    far, near = late[:plane], late[plane:]
    early, energy = potential_call(0, early_units, layout, False, fields_t, bias, others, cols, turned)
    early_came = all_z(early[1:])
    merged = merge_call([early[0], *early_came], near)
    far_came = all_z(sum_call([far[0], *all_plane(far[1:])], merged[:1]))
    found = finish_call(step_factor, far_came, [merged[0], *all_plane(merged[1:])])

    piece = series_call(around_orb(found), start, energy)
    near = [piece, *(to_plane(piece, dp) for dp in range(1, plane))]
    came = all_z([piece] * (nz - 1))
    pieces, *near[2:] = stack_call(near[2:], came[::-1], [dz - 1 for dz in z_order[::-1]])
    far = {dp: to_plane(pieces, dp) for dp in reversed(range(1, plane))}
    moved, energy = place_call(layout, near, [pieces, *(far[dp] for dp in range(1, plane))])
    return moved, energy.reshape(walk)


def solution(mesh):
    in_specs = (
        P("chol", "orb", None, None),
        P("chol", "orb", None),
        P("walker", "orb", None),
        P("walker", "orb", None),
        P("chol", "walker"),
    )
    out_specs = (P("walker", "orb", None), P("walker"))
    return jax.shard_map(
        per_device, mesh=mesh, in_specs=in_specs, out_specs=out_specs, check_vma=False
    )
```
